32 devices in a mesh: row: 8 (over z, y), col: 4 (over x, core).
Axes of the slice: x: 2, y: 2, z: 4, core: 2. Of those that a mesh axis runs over, the one named last changes fastest.
Arguments:
- amplitudes: bfloat16 [24576, 3072], P('row', 'col'), may hold values from -6 to 6
- pair_mask: int32 [96, 12], P('row', 'col'), may hold values 0 or 1
- integrals: bfloat16 [8, 4, 2, 256, 256], P('row', 'col'), may hold values from -0.25 to 0.25
- tile_list: int32 [8, 4, 2], P('row', 'col'), may hold values from 0 to 2, as said below
- tile_count: int32 [8, 4], P('row', 'col'), may hold values from 1 to 2, as said below
- owner: int32 [4, 4], P(None, 'col'), may hold values from 0 to 7, as said below
Outputs:
- ladder: bfloat16 [24576, 1024], P('row', 'col')
The draws below stay inside these ranges and needn't reach their ends.
Inputs may be any that keep to these rules, and one draw needn't show every extreme that they name: `owner`: within a column the 4 owners differ. `tile_count`: some panel that serves a step has all 2 slots live. `tile_list`: the live slots of a panel name distinct cd tile pairs; entries past the count are in range and unused.
All inputs are finite; a program needn't handle non-finite values. No bound on the sum of `pair_mask` on one device may be relied on, other than what follows from the above.
Results may differ from the reference program's by a relative error of at most 0.001.
Values may be sent and summed in bfloat16 or wider, within the bound.
No kernel may reach another device: no remote copies, remote signals or barrier semaphores. Data moves between devices by JAX's collectives and lax.ppermute only.
A program may use at most 128 MiB of HBM per device.

```python
import jax
import jax.numpy as jnp
from jax import lax

BLK = 256
NCD = 3
CAP = 2
STEPS = 4
TP = 256
PAIRS = 24576
NBLK = 96
CDT = 12
N_ROW = 8
N_COL = 4


def owner_table(key):
    base_key = jax.random.fold_in(key, 11)
    column_keys = jax.random.split(base_key, N_COL)
    orders = jax.vmap(lambda single: jax.random.permutation(single, N_ROW))(column_keys)
    leading = orders[0]
    top_place = jnp.argmax(leading == N_ROW - 1)
    swapped = leading.at[top_place].set(leading[0]).at[0].set(N_ROW - 1)
    orders = orders.at[0].set(swapped)
    return jnp.transpose(orders[:, :STEPS]).astype(jnp.int32)


def draw_owner(key, part):
    return owner_table(key)


def draw_tile_count(key, part):
    plan = owner_table(key)
    flips = jax.random.randint(jax.random.fold_in(key, 23), (N_ROW, N_COL), 0, 3)
    counts = jnp.where(flips == 0, CAP, 1).astype(jnp.int32)
    counts = counts.at[plan[0, 0], 0].set(CAP)
    counts = counts.at[plan[1, 0], 0].set(1)
    return counts


def draw_tile_list(key, part):
    panel_keys = jax.random.split(jax.random.fold_in(key, 37), N_ROW * N_COL)
    orders = jax.vmap(lambda single: jax.random.permutation(single, NCD))(panel_keys)
    return orders[:, :CAP].reshape(N_ROW, N_COL, CAP).astype(jnp.int32)


def touch_ends(array, own_key, smallest, top_value):
    extent = array.shape
    spot = [jax.random.randint(jax.random.fold_in(own_key, axis), (), 0, extent[axis]) for axis in range(len(extent))]
    array = array.at[tuple(spot)].set(smallest)
    longest = extent.index(max(extent))
    spot[longest] = (spot[longest] + 1) % extent[longest]
    return array.at[tuple(spot)].set(top_value)


def levels(stream_key, extent, cuts, low, high):
    loudness, own = 1.0, jax.random.fold_in(stream_key, 6)
    for position, shards_of in cuts:
        heights = jnp.exp(jax.random.uniform(jax.random.fold_in(own, position), (shards_of,), jnp.float32, low / len(cuts), high / len(cuts)))
        loudness = loudness * jnp.repeat(heights, extent[position] // shards_of).reshape([-1 if axis == position else 1 for axis in range(len(extent))])
    return loudness


def scatter_about(stream_key, dims, deviation, reach, shards=(), kind=jnp.bfloat16):
    level = levels(stream_key, dims, shards, -0.22, 0.18) if shards else 1.0
    values = jax.random.normal(stream_key, dims, jnp.float32) * deviation * level
    return jnp.minimum(jnp.maximum(values, -reach), reach).astype(kind)


def setup_inputs(seed: int = 0) -> dict:
    key_list = jax.random.split(jax.random.key(seed), 7)
    amplitudes = scatter_about(key_list[0], (PAIRS, CDT * TP), 1.0, 6.0, ((0, 8), (1, 4)))
    pair_mask = touch_ends((jax.random.randint(key_list[1], (NBLK, CDT), 0, 4) < 3).astype(jnp.int32), jax.random.fold_in(key_list[1], 1), 0, 1)
    integrals = scatter_about(key_list[2], (N_ROW, N_COL, CAP, TP, TP), (2 * TP) ** -0.5, 0.25, ((0, 8), (1, 4)))
    tile_list = draw_tile_list(jax.random.fold_in(key_list[6], 71), 0)
    tile_count = draw_tile_count(jax.random.fold_in(key_list[6], 71), 0)
    owner = draw_owner(jax.random.fold_in(key_list[6], 71), 0)
    return dict(amplitudes=amplitudes, pair_mask=pair_mask, integrals=integrals, tile_list=tile_list, tile_count=tile_count, owner=owner)


def reference(amplitudes, pair_mask, integrals, tile_list, tile_count, owner):
    pair_rows = amplitudes.shape[0]
    block_mask = jnp.repeat(pair_mask, BLK, axis=0).astype(amplitudes.dtype)

    def column(column_id):
        running = jnp.zeros((pair_rows, TP), jnp.float32)
        for grid_step in range(STEPS):
            source_group = ((column_id - grid_step) % N_COL).astype(jnp.int32)
            holder = owner[grid_step, column_id].astype(jnp.int32)
            for slot_index in range(CAP):
                tile_index = (source_group * NCD + tile_list[holder, column_id, slot_index]).astype(jnp.int32)
                tile_block = lax.dynamic_slice_in_dim(amplitudes, tile_index * TP, TP, 1)
                block_scale = lax.dynamic_slice_in_dim(block_mask, tile_index, 1, 1)
                product = jnp.dot(tile_block * block_scale, integrals[holder, column_id, slot_index], preferred_element_type=jnp.float32)
                running = running + jnp.where(slot_index < tile_count[holder, column_id], product, jnp.zeros_like(product))
        return running.astype(jnp.bfloat16)

    stacked = lax.map(column, jnp.arange(N_COL, dtype=jnp.int32))
    return jnp.transpose(stacked, (1, 0, 2)).reshape(pair_rows, N_COL * TP)
```

```python
from functools import partial

import jax
import jax.numpy as jnp
from jax import lax
from jax.experimental import pallas as pl
from jax.experimental.pallas import tpu as pltpu
from jax.sharding import PartitionSpec as P

STEPS = 4
CORES = 2
CHUNKS = 4
CODE_TOP = 32767.0
META_ROWS = 16


def pair_offsets(col_count):
    pairs = col_count // CORES
    offsets = set()
    for core in range(CORES):
        for step in range(STEPS):
            offsets.add(((core - step) // CORES * -1) % pairs)
    return sorted(offsets)


def fill_weights(info_ref, panels_ref, dense_ref, tile_width):
    pieces, groups, stored, _ = panels_ref.shape
    depth = tile_width // pieces
    slots = stored // depth
    width = dense_ref.shape[0] // groups
    dense_ref[...] = jnp.zeros_like(dense_ref)
    for group in range(groups):
        for slot in range(slots):

            @pl.when(slot < info_ref[group, slots])
            def _():
                start = pl.multiple_of(group * width + info_ref[group, slot] * tile_width, tile_width)
                for piece in range(pieces):
                    dense_ref[pl.ds(start + piece * depth, depth), :] = panels_ref[
                        piece, group, pl.ds(slot * depth, depth), :
                    ]


def block_product(mask_ref, row_block, own_ref, other_ref, dense_ref, tile_width):
    tiles = own_ref.shape[1] // tile_width
    total = None
    for group, source in enumerate((own_ref, other_ref)):
        for tile in range(tiles):
            live = mask_ref[row_block, group * tiles + tile].astype(jnp.float32).astype(jnp.bfloat16)
            screened = source[:, pl.ds(tile * tile_width, tile_width)] * live
            weights = dense_ref[pl.ds((group * tiles + tile) * tile_width, tile_width), :]
            term = jnp.dot(screened, weights, preferred_element_type=jnp.float32)
            total = term if total is None else total + term
    return total


def send_kernel(first, tile_width, info_ref, mask_ref, own_ref, other_ref, panels_ref, code_ref, scale_ref, dense_ref):
    step = pl.program_id(0)

    @pl.when(step == 0)
    def _():
        fill_weights(info_ref, panels_ref, dense_ref, tile_width)

    total = block_product(mask_ref, first + step, own_ref, other_ref, dense_ref, tile_width)
    top = jnp.max(jnp.abs(total), axis=0, keepdims=True)
    safe = jnp.where(top > 0, top, 1.0)
    code_ref[...] = jnp.round(total * (CODE_TOP / safe)).astype(jnp.int32).astype(jnp.int16)
    scale_ref[pl.ds(step, 1), :] = safe * (1.0 / CODE_TOP)


def join_kernel(first, tile_width, arrivals, *refs):
    info_ref, mask_ref, own_ref, other_ref, panels_ref = refs[:5]
    codes, scales = refs[5 : 5 + arrivals], refs[5 + arrivals : 5 + 2 * arrivals]
    out_ref, dense_ref = refs[-2:]
    step = pl.program_id(0)

    @pl.when(step == 0)
    def _():
        fill_weights(info_ref, panels_ref, dense_ref, tile_width)

    total = block_product(mask_ref, first + step, own_ref, other_ref, dense_ref, tile_width)
    for code_ref, scale_ref in zip(codes, scales):
        total = total + code_ref[...].astype(jnp.int32).astype(jnp.float32) * scale_ref[pl.ds(step, 1), :]
    out_ref[...] = total.astype(out_ref.dtype)


def shards(amplitudes, pair_mask, integrals, tile_list, tile_count, owner):
    row_count, full_width = amplitudes.shape
    slots, tile_width = integrals.shape[2], integrals.shape[-1]
    block_count, tiles = pair_mask.shape
    block_rows = row_count // block_count
    row_peers, col_peers = lax.axis_size("row"), lax.axis_size("col")
    depth = tile_width // row_peers
    core = lax.axis_index("col") % CORES
    offsets = pair_offsets(col_peers)

    swap = [(c, c ^ 1) for c in range(col_peers)]
    other = lax.ppermute(amplitudes, "col", swap)
    other_mask = lax.ppermute(pair_mask, "col", swap)
    masks = jnp.concatenate([pair_mask, other_mask], axis=1)

    pieces = integrals[0, 0].reshape(slots, row_peers, depth, tile_width)
    pieces = jnp.transpose(pieces, (1, 0, 2, 3)).reshape(row_peers, slots * depth, tile_width)
    info = jnp.concatenate([tile_list[0, 0], tile_count[0, 0][None]]).astype(integrals.dtype)
    info = jnp.pad(info[None, :], ((0, META_ROWS - 1), (0, tile_width - slots - 1)))
    pieces = jnp.concatenate([pieces, jnp.broadcast_to(info, (row_peers, META_ROWS, tile_width))], axis=1)
    pieces = lax.all_to_all(pieces, "row", 0, 0)

    def wanted(offset):
        chosen = []
        for group_shift in (0, 1 - 2 * core):
            step = (CORES * offset - group_shift) % col_peers
            holder = owner[jnp.minimum(step, STEPS - 1), 0]
            piece = lax.dynamic_index_in_dim(pieces, holder, 0, keepdims=False)
            chosen.append(jnp.where(step < STEPS, piece, jnp.zeros_like(piece)))
        chosen = jnp.stack(chosen)
        if offset % (col_peers // CORES):
            chosen = lax.ppermute(chosen, "col", [(c, (c - CORES * offset) % col_peers) for c in range(col_peers)])
        info = chosen[:, slots * depth, : slots + 1].astype(jnp.int32)
        return info, lax.all_gather(chosen[:, : slots * depth], "row")

    plans = {offset: wanted(offset) for offset in sorted(offsets, reverse=True)}

    chunks = CHUNKS if block_count % CHUNKS == 0 else 1
    span = block_count // chunks
    smem = pl.BlockSpec(memory_space=pltpu.SMEM)

    def inputs(first):
        rows = pl.BlockSpec((block_rows, full_width), lambda i: (first + i, 0))
        panels = pl.BlockSpec((row_peers, CORES, slots * depth, tile_width), lambda i: (0, 0, 0, 0))
        return [smem, smem, rows, rows, panels]

    codes = pl.BlockSpec((block_rows, tile_width), lambda i: (i, 0))
    scale_rows = -(-span // 8) * 8
    scales = pl.BlockSpec((scale_rows, tile_width), lambda i: (0, 0))
    dense = pltpu.VMEM((CORES * full_width, tile_width), jnp.bfloat16)
    cost = pl.CostEstimate(
        flops=2 * span * block_rows * CORES * full_width * tile_width,
        bytes_accessed=span * block_rows * (CORES * full_width + tile_width) * 2,
        transcendentals=0,
    )
    limit = pltpu.CompilerParams(vmem_limit_bytes=32 * 1024 * 1024)

    arrived = []
    for chunk in range(chunks):
        first = chunk * span
        received = []
        for offset in offsets:
            if offset == 0:
                continue
            code, scale = pl.pallas_call(
                partial(send_kernel, first, tile_width),
                grid=(span,),
                in_specs=inputs(first),
                out_specs=[codes, scales],
                out_shape=[
                    jax.ShapeDtypeStruct((span * block_rows, tile_width), jnp.int16),
                    jax.ShapeDtypeStruct((scale_rows, tile_width), jnp.float32),
                ],
                scratch_shapes=[dense],
                compiler_params=limit,
                cost_estimate=cost,
                name="send_part",
            )(plans[offset][0], masks, amplitudes, other, plans[offset][1])
            up = [(c, (c + CORES * offset) % col_peers) for c in range(col_peers)]
            received.append((lax.ppermute(code, "col", up), lax.ppermute(scale, "col", up)))
        arrived.append(received)

    out = None
    for chunk in range(chunks):
        first = chunk * span
        arrivals = len(arrived[chunk])
        operands = [plans[0][0], masks, amplitudes, other, plans[0][1]]
        operands += [code for code, _ in arrived[chunk]] + [scale for _, scale in arrived[chunk]]
        specs = inputs(first) + [codes] * arrivals + [scales] * arrivals
        body = partial(join_kernel, first, tile_width, arrivals)
        aliases = {}
        if out is not None:
            body = partial(skip_operand, len(operands), body)
            aliases = {len(operands): 0}
            operands.append(out)
            specs.append(pl.BlockSpec(memory_space=pl.ANY))
        out = pl.pallas_call(
            body,
            grid=(span,),
            in_specs=specs,
            out_specs=pl.BlockSpec((block_rows, tile_width), lambda i, first=first: (first + i, 0)),
            out_shape=jax.ShapeDtypeStruct((row_count, tile_width), jnp.bfloat16),
            scratch_shapes=[dense],
            input_output_aliases=aliases,
            compiler_params=limit,
            cost_estimate=cost,
            name="join_part",
        )(*operands)
    return out


def skip_operand(position, body, *refs):
    body(*refs[:position], *refs[position + 1 :])


def solution(mesh):
    return jax.shard_map(
        shards,
        mesh=mesh,
        in_specs=(
            P("row", "col"),
            P("row", "col"),
            P("row", "col", None, None, None),
            P("row", "col", None),
            P("row", "col"),
            P(None, "col"),
        ),
        out_specs=P("row", "col"),
        check_vma=False,
    )
```

```python
from functools import partial

import jax
import jax.numpy as jnp
from jax import lax
from jax.experimental import pallas as pl
from jax.experimental.pallas import tpu as pltpu
from jax.sharding import PartitionSpec as P

STEPS = 4
CORES = 2
CHUNKS = 4
CODE_TOP = 32767.0
META_ROWS = 16
META_TILE = (8, 128)
PARAMS = pltpu.CompilerParams(vmem_limit_bytes=56 * 1024 * 1024)
SMEM = pl.BlockSpec(memory_space=pltpu.SMEM)
VMEM = pl.BlockSpec(memory_space=pltpu.VMEM)


def pair_offsets(col_count):
    pairs = col_count // CORES
    offsets = set()
    for core in range(CORES):
        for step in range(STEPS):
            offsets.add(-((core - step) // CORES) % pairs)
    return sorted(offsets)


def pack_kernel(list_ref, count_ref, panel_ref, pieces_ref):
    peers, height, _ = pieces_ref.shape
    slots, tile_width = panel_ref.shape[2:4]
    share = height - META_ROWS
    lane = lax.broadcasted_iota(jnp.int32, (META_ROWS, pieces_ref.shape[2]), 1)
    info = jnp.where(lane == slots, count_ref[0, 0], 0)
    for slot in range(slots):
        info = jnp.where(lane == slot, list_ref[0, 0, slot], info)
    info = info.astype(jnp.float32).astype(pieces_ref.dtype)
    for peer in range(peers):
        slot, start = divmod(peer * share, tile_width)
        pieces_ref[peer, pl.ds(0, share), :] = panel_ref[0, 0, slot, pl.ds(start, share), :]
        pieces_ref[peer, pl.ds(share, META_ROWS), :] = info


def choose_kernel(col_peers, offsets, owner_ref, place_ref, pieces_ref, *out_refs):
    share = pieces_ref.shape[1] - META_ROWS
    core = lax.rem(place_ref[0], CORES)
    sign = 1 - 2 * core
    for number, offset in enumerate(offsets):
        data_ref, info_ref = out_refs[2 * number : 2 * number + 2]
        rows = []
        for group, shift in enumerate((0, sign)):
            step = lax.rem(CORES * offset - shift + col_peers, col_peers)
            used = step < STEPS
            holder = owner_ref[jnp.minimum(step, STEPS - 1), 0]
            data_ref[pl.ds(group * share, share), :] = pieces_ref[holder, pl.ds(0, share), :]
            info = pieces_ref[holder, pl.ds(share, META_ROWS), :].astype(jnp.float32).astype(jnp.int32)
            rows.append(jnp.where(used, info[: META_TILE[0], : META_TILE[1]], 0))
        line = lax.broadcasted_iota(jnp.int32, META_TILE, 0)
        info_ref[...] = jnp.where(line == 0, rows[0], rows[1])


def fill_weights(row_place, info_ref, piece_refs, dense_ref, tile_width, slots):
    peers = len(piece_refs)
    share = piece_refs[0].shape[0] // CORES
    width = dense_ref.shape[0] // CORES
    dense_ref[...] = jnp.zeros_like(dense_ref)
    for shift, piece_ref in enumerate(piece_refs):
        first = lax.rem(row_place - shift + peers, peers) * share
        slot = first // tile_width
        for group in range(CORES):

            @pl.when(slot < info_ref[group, slots])
            def _():
                start = group * width + info_ref[group, slot] * tile_width + lax.rem(first, tile_width)
                dense_ref[pl.ds(pl.multiple_of(start, 16), share), :] = piece_ref[pl.ds(group * share, share), :]


def block_product(mask_refs, row_block, own_ref, other_ref, dense_ref, tile_width):
    tiles = own_ref.shape[1] // tile_width
    width = tiles * tile_width
    total = None
    for group, source in enumerate((own_ref, other_ref)):
        screened = []
        for tile in range(tiles):
            live = mask_refs[group][row_block, tile].astype(jnp.float32).astype(jnp.bfloat16)
            screened.append(source[:, pl.ds(tile * tile_width, tile_width)] * live)
        term = jnp.dot(
            jnp.concatenate(screened, axis=1),
            dense_ref[pl.ds(group * width, width), :],
            preferred_element_type=jnp.float32,
        )
        total = term if total is None else total + term
    return total


def send_kernel(first, tile_width, slots, peers, *refs):
    place_ref, info_ref, mask_ref, other_mask_ref, own_ref, other_ref = refs[:6]
    piece_refs = refs[6 : 6 + peers]
    code_ref, scale_ref, dense_ref = refs[6 + peers :]
    step = pl.program_id(0)

    @pl.when(step == 0)
    def _():
        fill_weights(place_ref[0], info_ref, piece_refs, dense_ref, tile_width, slots)

    total = block_product((mask_ref, other_mask_ref), first + step, own_ref, other_ref, dense_ref, tile_width)
    top = jnp.max(jnp.abs(total), axis=0, keepdims=True)
    safe = jnp.where(top > 0, top, 1.0)
    code_ref[...] = jnp.round(total * (CODE_TOP / safe)).astype(jnp.int32).astype(jnp.int16)
    scale_ref[pl.ds(step, 1), :] = safe * (1.0 / CODE_TOP)


def join_kernel(first, tile_width, slots, peers, arrivals, *refs):
    place_ref, info_ref, mask_ref, other_mask_ref, own_ref, other_ref = refs[:6]
    piece_refs = refs[6 : 6 + peers]
    code_refs = refs[6 + peers : 6 + peers + arrivals]
    scale_refs = refs[6 + peers + arrivals : 6 + peers + 2 * arrivals]
    out_ref, dense_ref = refs[-2:]
    step = pl.program_id(0)

    @pl.when(step == 0)
    def _():
        fill_weights(place_ref[0], info_ref, piece_refs, dense_ref, tile_width, slots)

    total = block_product((mask_ref, other_mask_ref), first + step, own_ref, other_ref, dense_ref, tile_width)
    for code_ref, scale_ref in zip(code_refs, scale_refs):
        total = total + code_ref[...].astype(jnp.int32).astype(jnp.float32) * scale_ref[pl.ds(step, 1), :]
    out_ref[...] = total.astype(out_ref.dtype)


def shards(amplitudes, pair_mask, integrals, tile_list, tile_count, owner):
    row_count, full_width = amplitudes.shape
    slots, tile_width = integrals.shape[2], integrals.shape[-1]
    block_count = pair_mask.shape[0]
    block_rows = row_count // block_count
    row_peers, col_peers = lax.axis_size("row"), lax.axis_size("col")
    share = slots * tile_width // row_peers
    offsets = pair_offsets(col_peers)
    row_place = lax.axis_index("row").reshape(1)
    col_place = lax.axis_index("col").reshape(1)

    swap = [(c, c ^ 1) for c in range(col_peers)]
    other = lax.ppermute(amplitudes, "col", swap)
    other_mask = lax.ppermute(pair_mask, "col", swap)

    pieces = pl.pallas_call(
        pack_kernel,
        in_specs=[SMEM, SMEM, VMEM],
        out_specs=VMEM,
        out_shape=jax.ShapeDtypeStruct((row_peers, share + META_ROWS, tile_width), integrals.dtype),
        compiler_params=PARAMS,
        name="pack",
    )(tile_list, tile_count, integrals)
    pieces = lax.all_to_all(pieces, "row", 0, 0)
    chosen = pl.pallas_call(
        partial(choose_kernel, col_peers, offsets),
        in_specs=[SMEM, SMEM, VMEM],
        out_specs=[VMEM] * (2 * len(offsets)),
        out_shape=[
            jax.ShapeDtypeStruct((CORES * share, tile_width), integrals.dtype),
            jax.ShapeDtypeStruct(META_TILE, jnp.int32),
        ]
        * len(offsets),
        compiler_params=PARAMS,
        name="choose",
    )(owner, col_place, pieces)

    plans = {}
    for number, offset in reversed(list(enumerate(offsets))):
        data, info = chosen[2 * number : 2 * number + 2]
        if offset:
            down = [(c, (c - CORES * offset) % col_peers) for c in range(col_peers)]
            data, info = lax.ppermute(data, "col", down), lax.ppermute(info, "col", down)
        spread = [data]
        for shift in range(1, row_peers):
            spread.append(lax.ppermute(data, "row", [(r, (r + shift) % row_peers) for r in range(row_peers)]))
        plans[offset] = (info, spread)

    chunks = CHUNKS if block_count % CHUNKS == 0 else 1
    span = block_count // chunks

    def inputs(first):
        rows = pl.BlockSpec((block_rows, full_width), lambda i: (first + i, 0))
        piece = pl.BlockSpec((CORES * share, tile_width), lambda i: (0, 0))
        return [SMEM, SMEM, SMEM, SMEM, rows, rows] + [piece] * row_peers

    codes = pl.BlockSpec((block_rows, tile_width), lambda i: (i, 0))
    scale_rows = -(-span // 8) * 8
    scales = pl.BlockSpec((scale_rows, tile_width), lambda i: (0, 0))
    dense = pltpu.VMEM((CORES * full_width, tile_width), jnp.bfloat16)
    cost = pl.CostEstimate(
        flops=2 * span * block_rows * CORES * full_width * tile_width,
        bytes_accessed=span * block_rows * (CORES * full_width + tile_width) * 2,
        transcendentals=0,
    )

    arrived = []
    for chunk in range(chunks):
        first = chunk * span
        received = []
        for offset in offsets:
            if offset == 0:
                continue
            info, spread = plans[offset]
            code, scale = pl.pallas_call(
                partial(send_kernel, first, tile_width, slots, row_peers),
                grid=(span,),
                in_specs=inputs(first),
                out_specs=[codes, scales],
                out_shape=[
                    jax.ShapeDtypeStruct((span * block_rows, tile_width), jnp.int16),
                    jax.ShapeDtypeStruct((scale_rows, tile_width), jnp.float32),
                ],
                scratch_shapes=[dense],
                compiler_params=PARAMS,
                cost_estimate=cost,
                name="send_part",
            )(row_place, info, pair_mask, other_mask, amplitudes, other, *spread)
            up = [(c, (c + CORES * offset) % col_peers) for c in range(col_peers)]
            received.append((lax.ppermute(code, "col", up), lax.ppermute(scale, "col", up)))
        arrived.append(received)

    out = None
    info, spread = plans[0]
    for chunk in range(chunks):
        first = chunk * span
        arrivals = len(arrived[chunk])
        operands = [row_place, info, pair_mask, other_mask, amplitudes, other, *spread]
        operands += [code for code, _ in arrived[chunk]] + [scale for _, scale in arrived[chunk]]
        specs = inputs(first) + [codes] * arrivals + [scales] * arrivals
        body = partial(join_kernel, first, tile_width, slots, row_peers, arrivals)
        aliases = {}
        if out is not None:
            body = partial(skip_operand, len(operands), body)
            aliases = {len(operands): 0}
            operands.append(out)
            specs.append(pl.BlockSpec(memory_space=pl.ANY))
        out = pl.pallas_call(
            body,
            grid=(span,),
            in_specs=specs,
            out_specs=pl.BlockSpec((block_rows, tile_width), lambda i, first=first: (first + i, 0)),
            out_shape=jax.ShapeDtypeStruct((row_count, tile_width), jnp.bfloat16),
            scratch_shapes=[dense],
            input_output_aliases=aliases,
            compiler_params=PARAMS,
            cost_estimate=cost,
            name="join_part",
        )(*operands)
    return out


def skip_operand(position, body, *refs):
    body(*refs[:position], *refs[position + 1 :])


def solution(mesh):
    return jax.shard_map(
        shards,
        mesh=mesh,
        in_specs=(
            P("row", "col"),
            P("row", "col"),
            P("row", "col", None, None, None),
            P("row", "col", None),
            P("row", "col"),
            P(None, "col"),
        ),
        out_specs=P("row", "col"),
        check_vma=False,
    )
```

```python
from functools import partial

import jax
import jax.numpy as jnp
from jax import lax
from jax.experimental import pallas as pl
from jax.experimental.pallas import tpu as pltpu
from jax.sharding import PartitionSpec as P

STEPS = 4
CORES = 2
CUTS = (0.0, 0.25, 0.58, 0.92, 1.0)
CODE_TOP = 32767.0
FRACTION = 8192.0
META_ROWS = 16
PARAMS = pltpu.CompilerParams(vmem_limit_bytes=16 * 1024 * 1024)
SMEM = pl.BlockSpec(memory_space=pltpu.SMEM)
VMEM = pl.BlockSpec(memory_space=pltpu.VMEM)


def pair_offsets(col_count):
    pairs = col_count // CORES
    offsets = set()
    for core in range(CORES):
        for step in range(STEPS):
            offsets.add(-((core - step) // CORES) % pairs)
    return sorted(offsets)


def row_chunks(block_count):
    marks = sorted({round(block_count * cut) for cut in CUTS})
    return [(first, last - first) for first, last in zip(marks, marks[1:])]


def pack_kernel(list_ref, count_ref, panel_ref, pieces_ref):
    peers, height, _ = pieces_ref.shape
    slots, tile_width = panel_ref.shape[2:4]
    share = height - META_ROWS
    lane = lax.broadcasted_iota(jnp.int32, (META_ROWS, pieces_ref.shape[2]), 1)
    info = jnp.where(lane == slots, count_ref[0, 0], 0)
    for slot in range(slots):
        info = jnp.where(lane == slot, list_ref[0, 0, slot], info)
    info = info.astype(jnp.float32).astype(pieces_ref.dtype)
    for peer in range(peers):
        slot, start = divmod(peer * share, tile_width)
        pieces_ref[peer, pl.ds(0, share), :] = panel_ref[0, 0, slot, pl.ds(start, share), :]
        pieces_ref[peer, pl.ds(share, META_ROWS), :] = info


def mask_kernel(chunks, tile_width, mask_ref, rows_ref, *out_refs):
    block = pl.program_id(0)
    for (first, span), out_ref in zip(chunks, out_refs):

        @pl.when((block >= first) & (block < first + span))
        def _():
            for tile in range(rows_ref.shape[1] // tile_width):
                live = mask_ref[block, tile].astype(jnp.float32).astype(rows_ref.dtype)
                columns = pl.ds(tile * tile_width, tile_width)
                out_ref[:, columns] = rows_ref[:, columns] * live


def choose_kernel(col_peers, offsets, owner_ref, place_ref, pieces_ref, *out_refs):
    share = pieces_ref.shape[1] - META_ROWS
    core = lax.rem(place_ref[0], CORES)
    sign = 1 - 2 * core
    line = lax.broadcasted_iota(jnp.int32, (META_ROWS, pieces_ref.shape[2]), 0)
    for offset, out_ref in zip(offsets, out_refs):
        infos = []
        for group, shift in enumerate((0, sign)):
            step = lax.rem(CORES * offset - shift + col_peers, col_peers)
            holder = owner_ref[jnp.minimum(step, STEPS - 1), 0]
            out_ref[pl.ds(group * share, share), :] = pieces_ref[holder, pl.ds(0, share), :]
            info = pieces_ref[holder, pl.ds(share, META_ROWS), :].astype(jnp.float32)
            infos.append(jnp.where(step < STEPS, info, 0.0))
        out_ref[pl.ds(CORES * share, META_ROWS), :] = jnp.where(line == 0, infos[0], infos[1]).astype(out_ref.dtype)


def fill_kernel(slots, place_ref, *refs):
    piece_refs, dense_ref = refs[:-1], refs[-1]
    peers = len(piece_refs)
    share = (piece_refs[0].shape[0] - META_ROWS) // CORES
    width, tile_width = dense_ref.shape[0] // CORES, dense_ref.shape[1]
    table = piece_refs[0][pl.ds(CORES * share, META_ROWS), :].astype(jnp.float32)
    line = lax.broadcasted_iota(jnp.int32, table.shape, 0)
    lane = lax.broadcasted_iota(jnp.int32, table.shape, 1)

    def entry(group, place):
        return jnp.max(jnp.where((line == group) & (lane == place), table, 0.0)).astype(jnp.int32)

    dense_ref[...] = jnp.zeros_like(dense_ref)
    for group in range(CORES):
        count = entry(group, slots)
        starts = [group * width + entry(group, slot) * tile_width for slot in range(slots)]
        for shift, piece_ref in enumerate(piece_refs):
            first = lax.rem(place_ref[0] - shift + peers, peers) * share
            slot = first // tile_width
            start = starts[0]
            for other in range(1, slots):
                start = jnp.where(slot == other, starts[other], start)

            @pl.when(slot < count)
            def _():
                place = pl.multiple_of(start + lax.rem(first, tile_width), META_ROWS)
                dense_ref[pl.ds(place, share), :] = piece_ref[pl.ds(group * share, share), :]


def block_product(own_ref, other_ref, dense_ref):
    width = own_ref.shape[1]
    return jnp.dot(own_ref[...], dense_ref[pl.ds(0, width), :], preferred_element_type=jnp.float32) + jnp.dot(
        other_ref[...], dense_ref[pl.ds(width, width), :], preferred_element_type=jnp.float32
    )


def send_kernel(own_ref, other_ref, dense_ref, code_ref, scale_ref):
    step, span = pl.program_id(0), pl.num_programs(0)
    height = own_ref.shape[0]
    total = block_product(own_ref, other_ref, dense_ref)
    top = jnp.max(jnp.abs(total), axis=0, keepdims=True)
    unit = jnp.where(top > 0, top, 1.0) * (1.0 / CODE_TOP)
    power = jnp.floor(jnp.log2(unit))
    fraction = jnp.ceil(unit * jnp.exp2(-power) * FRACTION)
    unit = fraction * jnp.exp2(power) * (1.0 / FRACTION)
    code = jnp.clip(jnp.round(total * (1.0 / unit)), -CODE_TOP, CODE_TOP)
    code_ref[pl.ds(pl.multiple_of(step * height, height), height), :] = code.astype(jnp.int32).astype(jnp.int16)
    scale_ref[pl.ds(2 * step, 1), :] = power
    scale_ref[pl.ds(2 * step + 1, 1), :] = fraction

    @pl.when(step == span - 1)
    def _():
        rows = scale_ref.shape[0]
        line = lax.broadcasted_iota(jnp.int32, scale_ref.shape, 0)
        kept = jnp.where(line < 2 * span, scale_ref[...], 0.0)
        code_ref[pl.ds(code_ref.shape[0] - rows, rows), :] = kept.astype(jnp.int32).astype(jnp.int16)


def join_kernel(own_ref, other_ref, dense_ref, *refs):
    code_refs, out_ref, scale_ref = refs[:-2], refs[-2], refs[-1]
    step = pl.program_id(0)
    height = own_ref.shape[0]
    rows = scale_ref.shape[0] // max(len(code_refs), 1)

    @pl.when(step == 0)
    def _():
        for number, code_ref in enumerate(code_refs):
            scales = code_ref[pl.ds(code_ref.shape[0] - rows, rows), :].astype(jnp.int32).astype(jnp.float32)
            scale_ref[pl.ds(number * rows, rows), :] = scales

    total = block_product(own_ref, other_ref, dense_ref)
    for number, code_ref in enumerate(code_refs):
        power = scale_ref[pl.ds(number * rows + 2 * step, 1), :]
        fraction = scale_ref[pl.ds(number * rows + 2 * step + 1, 1), :]
        code = code_ref[pl.ds(pl.multiple_of(step * height, height), height), :].astype(jnp.int32).astype(jnp.float32)
        total = total + code * (fraction * jnp.exp2(power) * (1.0 / FRACTION))
    out_ref[...] = total.astype(out_ref.dtype)


def after(value, *earlier):
    return lax.optimization_barrier((value, *earlier))[0]


def shards(amplitudes, pair_mask, integrals, tile_list, tile_count, owner):
    row_count, full_width = amplitudes.shape
    slots, tile_width = integrals.shape[2], integrals.shape[-1]
    block_count = pair_mask.shape[0]
    block_rows = row_count // block_count
    row_peers, col_peers = lax.axis_size("row"), lax.axis_size("col")
    share = slots * tile_width // row_peers
    offsets = pair_offsets(col_peers)
    row_place = lax.axis_index("row").reshape(1)
    col_place = lax.axis_index("col").reshape(1)
    chunks = row_chunks(block_count)

    pieces = pl.pallas_call(
        pack_kernel,
        in_specs=[SMEM, SMEM, VMEM],
        out_specs=VMEM,
        out_shape=jax.ShapeDtypeStruct((row_peers, share + META_ROWS, tile_width), integrals.dtype),
        compiler_params=PARAMS,
        name="pack",
    )(tile_list, tile_count, integrals)
    pieces = lax.all_to_all(pieces, "row", 0, 0)

    masked = pl.pallas_call(
        partial(mask_kernel, chunks, tile_width),
        grid=(block_count,),
        in_specs=[SMEM, pl.BlockSpec((block_rows, full_width), lambda i: (i, 0))],
        out_specs=[
            pl.BlockSpec(
                (block_rows, full_width), lambda i, first=first, span=span: (jnp.clip(i - first, 0, span - 1), 0)
            )
            for first, span in chunks
        ],
        out_shape=[
            jax.ShapeDtypeStruct((span * block_rows, full_width), amplitudes.dtype) for _, span in chunks
        ],
        compiler_params=PARAMS,
        cost_estimate=pl.CostEstimate(
            flops=row_count * full_width, bytes_accessed=4 * row_count * full_width, transcendentals=0
        ),
        name="screen",
    )(pair_mask, amplitudes)
    pieces = after(pieces, *masked)

    chosen = pl.pallas_call(
        partial(choose_kernel, col_peers, offsets),
        in_specs=[SMEM, SMEM, VMEM],
        out_specs=[VMEM] * len(offsets),
        out_shape=[jax.ShapeDtypeStruct((CORES * share + META_ROWS, tile_width), integrals.dtype)] * len(offsets),
        compiler_params=PARAMS,
        name="choose",
    )(owner, col_place, pieces)

    def spread(data):
        held = [data]
        for shift in range(1, row_peers):
            held.append(lax.ppermute(data, "row", [(r, (r + shift) % row_peers) for r in range(row_peers)]))
        return held

    def fill(held):
        return pl.pallas_call(
            partial(fill_kernel, slots),
            in_specs=[SMEM] + [VMEM] * row_peers,
            out_specs=VMEM,
            out_shape=jax.ShapeDtypeStruct((CORES * full_width, tile_width), integrals.dtype),
            compiler_params=PARAMS,
            name="fill",
        )(row_place, *held)

    swap = [(c, c ^ 1) for c in range(col_peers)]
    others = [lax.ppermute(after(masked[0], pieces), "col", swap)]
    plans = {}
    for offset, data in zip(offsets, chosen):
        if offset:
            data = lax.ppermute(data, "col", [(c, (c - CORES * offset) % col_peers) for c in range(col_peers)])
            held = spread(data)
            plans[offset] = fill([after(held[0], others[0])] + held[1:])

    rows = pl.BlockSpec((block_rows, full_width), lambda i: (i, 0))
    weights = pl.BlockSpec((CORES * full_width, tile_width), lambda i: (0, 0))

    def cost(span):
        return pl.CostEstimate(
            flops=2 * span * block_rows * CORES * full_width * tile_width,
            bytes_accessed=span * block_rows * (CORES * full_width + tile_width) * 2,
            transcendentals=0,
        )

    def code_shape(span):
        return (span * block_rows + -(-2 * span // META_ROWS) * META_ROWS, tile_width)

    arrived, sent = [], []
    for number, ((first, span), own) in enumerate(zip(chunks, masked)):
        if number + 1 < len(chunks):
            earlier = [others[number]] + sent[-1:]
            others.append(lax.ppermute(after(masked[number + 1], *earlier), "col", swap))
        received = []
        for offset in offsets:
            if offset == 0:
                continue
            height = code_shape(span)[0] - span * block_rows
            code = pl.pallas_call(
                send_kernel,
                grid=(span,),
                in_specs=[rows, rows, weights],
                out_specs=pl.BlockSpec(code_shape(span), lambda i: (0, 0)),
                out_shape=jax.ShapeDtypeStruct(code_shape(span), jnp.int16),
                scratch_shapes=[pltpu.VMEM((height, tile_width), jnp.float32)],
                compiler_params=PARAMS,
                cost_estimate=cost(span),
                name="send_part",
            )(own, others[number], plans[offset])
            up = [(c, (c + CORES * offset) % col_peers) for c in range(col_peers)]
            received.append(lax.ppermute(code, "col", up))
            sent.append(code)
        arrived.append(received)
    plans[0] = fill(spread(after(chosen[offsets.index(0)], *sent)))

    out = None
    for (first, span), own, other, received in zip(chunks, masked, others, arrived):
        operands = [own, other, plans[0], *received]
        specs = [rows, rows, weights] + [pl.BlockSpec(code_shape(span), lambda i: (0, 0))] * len(received)
        body = join_kernel
        aliases = {}
        if out is not None:
            body = partial(skip_operand, len(operands), body)
            aliases = {len(operands): 0}
            operands.append(out)
            specs.append(pl.BlockSpec(memory_space=pl.ANY))
        height = code_shape(span)[0] - span * block_rows
        out = pl.pallas_call(
            body,
            grid=(span,),
            in_specs=specs,
            out_specs=pl.BlockSpec((block_rows, tile_width), lambda i, first=first: (first + i, 0)),
            out_shape=jax.ShapeDtypeStruct((row_count, tile_width), jnp.bfloat16),
            scratch_shapes=[pltpu.VMEM((height * max(len(received), 1), tile_width), jnp.float32)],
            input_output_aliases=aliases,
            compiler_params=PARAMS,
            cost_estimate=cost(span),
            name="join_part",
        )(*operands)
    return out


def skip_operand(position, body, *refs):
    body(*refs[:position], *refs[position + 1 :])


def solution(mesh):
    return jax.shard_map(
        shards,
        mesh=mesh,
        in_specs=(
            P("row", "col"),
            P("row", "col"),
            P("row", "col", None, None, None),
            P("row", "col", None),
            P("row", "col"),
            P(None, "col"),
        ),
        out_specs=P("row", "col"),
        check_vma=False,
    )
```

```python
from functools import partial

import jax
import jax.numpy as jnp
from jax import lax
from jax.experimental import pallas as pl
from jax.experimental.pallas import tpu as pltpu
from jax.sharding import PartitionSpec as P

STEPS = 4
CORES = 2
HALVES = 2
CUTS = (0.0, 0.08, 0.42, 0.75, 0.92, 1.0)
CODE_TOP = 32767.0
FRACTION = 8192.0
META_ROWS = 16
PARAMS = pltpu.CompilerParams(vmem_limit_bytes=16 * 1024 * 1024)
SMEM = pl.BlockSpec(memory_space=pltpu.SMEM)
VMEM = pl.BlockSpec(memory_space=pltpu.VMEM)
HBM = pl.BlockSpec(memory_space=pltpu.HBM)


def pair_offsets(col_count):
    pairs = col_count // CORES
    offsets = set()
    for core in range(CORES):
        for step in range(STEPS):
            offsets.add(-((core - step) // CORES) % pairs)
    return sorted(offsets)


def row_chunks(block_count):
    marks = sorted({round(block_count * cut) for cut in CUTS})
    return [(first, last - first) for first, last in zip(marks, marks[1:])]


def pack_kernel(list_ref, count_ref, panel_ref, *piece_refs):
    peers = len(piece_refs)
    slots, tile_width = panel_ref.shape[2:4]
    share = slots * tile_width // peers
    place = lax.axis_index("row") // HALVES
    lane = lax.broadcasted_iota(jnp.int32, (META_ROWS, tile_width), 1)
    info = jnp.where(lane == slots, count_ref[0, 0], 0)
    for slot in range(slots):
        info = jnp.where(lane == slot, list_ref[0, 0, slot], info)
    info = info.astype(jnp.float32).astype(panel_ref.dtype)
    for shift, piece_ref in enumerate(piece_refs):
        first = lax.rem(place + shift, peers) * share
        start = pl.multiple_of(lax.rem(first, tile_width), META_ROWS)
        piece_ref[pl.ds(0, share), :] = panel_ref[0, 0, first // tile_width, pl.ds(start, share), :]
        piece_ref[pl.ds(share, META_ROWS), :] = info


def choose_kernel(col_peers, offsets, owner_ref, *refs):
    out_refs = refs[len(refs) - len(offsets) :]
    piece_refs = refs[: len(refs) - len(offsets)]
    peers = len(piece_refs)
    share = piece_refs[0].shape[0] - META_ROWS
    row = lax.axis_index("row")
    core = lax.rem(lax.axis_index("col"), CORES)
    sign = 1 - 2 * core
    line = lax.broadcasted_iota(jnp.int32, (META_ROWS, piece_refs[0].shape[1]), 0)
    for offset, out_ref in zip(offsets, out_refs):
        out_ref[...] = jnp.zeros_like(out_ref)
        for group, shift in enumerate((0, sign)):
            step = lax.rem(CORES * offset - shift + col_peers, col_peers)
            holder = owner_ref[0, jnp.minimum(step, STEPS - 1)]
            here = (step < STEPS) & (lax.rem(holder, HALVES) == lax.rem(row, HALVES))
            back = lax.rem(row // HALVES - holder // HALVES + peers, peers)
            for number, piece_ref in enumerate(piece_refs):

                @pl.when(here & (back == number))
                def _():
                    out_ref[pl.ds(group * share, share), :] = piece_ref[pl.ds(0, share), :]
                    rows = pl.ds(CORES * share, META_ROWS)
                    out_ref[rows, :] = jnp.where(line == group, piece_ref[pl.ds(share, META_ROWS), :], out_ref[rows, :])


def fill_kernel(slots, *refs):
    piece_refs, dense_ref = refs[:-1], refs[-1]
    peers = len(piece_refs)
    share = (piece_refs[0].shape[0] - META_ROWS) // CORES
    width, tile_width = dense_ref.shape[0] // CORES, dense_ref.shape[1]
    place = lax.axis_index("row") // HALVES
    table = piece_refs[0][pl.ds(CORES * share, META_ROWS), :].astype(jnp.float32)
    line = lax.broadcasted_iota(jnp.int32, table.shape, 0)
    lane = lax.broadcasted_iota(jnp.int32, table.shape, 1)

    def entry(group, spot):
        return jnp.max(jnp.where((line == group) & (lane == spot), table, 0.0)).astype(jnp.int32)

    dense_ref[...] = jnp.zeros_like(dense_ref)
    for group in range(CORES):
        count = entry(group, slots)
        starts = [group * width + entry(group, slot) * tile_width for slot in range(slots)]
        for shift, piece_ref in enumerate(piece_refs):
            first = lax.rem(place - shift + peers, peers) * share
            slot = first // tile_width
            start = starts[0]
            for other in range(1, slots):
                start = jnp.where(slot == other, starts[other], start)

            @pl.when(slot < count)
            def _():
                spot = pl.multiple_of(start + lax.rem(first, tile_width), META_ROWS)
                dense_ref[pl.ds(spot, share), :] = piece_ref[pl.ds(group * share, share), :]


def screened(mask_ref, block, rows_ref):
    tiles = mask_ref.shape[0]
    tile_width = rows_ref.shape[1] // tiles
    parts = []
    for tile in range(tiles):
        live = mask_ref[tile, block].astype(jnp.float32).astype(rows_ref.dtype)
        parts.append(rows_ref[:, pl.ds(tile * tile_width, tile_width)] * live)
    return jnp.concatenate(parts, axis=1)


def block_product(mask_refs, block, row_refs, dense_ref):
    width = row_refs[0].shape[1]
    return sum(
        jnp.dot(
            screened(mask_ref, block, rows_ref),
            dense_ref[pl.ds(group * width, width), :],
            preferred_element_type=jnp.float32,
        )
        for group, (mask_ref, rows_ref) in enumerate(zip(mask_refs, row_refs))
    )


def send_kernel(first, span, height, mask_ref, other_mask_ref, own_ref, other_ref, dense_ref, code_ref, scale_ref):
    scale_ref[...] = jnp.zeros_like(scale_ref)

    def body(own_block, other_block):
        step = pl.program_id(0)
        total = block_product((mask_ref, other_mask_ref), first + step, (own_block, other_block), dense_ref)
        top = jnp.max(jnp.abs(total), axis=0, keepdims=True)
        unit = jnp.where(top > 0, top, 1.0) * (1.0 / CODE_TOP)
        power = jnp.floor(jnp.log2(unit))
        fraction = jnp.ceil(unit * jnp.exp2(-power) * FRACTION)
        unit = fraction * jnp.exp2(power) * (1.0 / FRACTION)
        code = jnp.clip(jnp.round(total * (1.0 / unit)), -CODE_TOP, CODE_TOP)
        code_ref[pl.ds(pl.multiple_of(step * height, height), height), :] = code.astype(jnp.int32).astype(jnp.int16)
        scale_ref[pl.ds(2 * step, 1), :] = power
        scale_ref[pl.ds(2 * step + 1, 1), :] = fraction

    block = pl.BlockSpec((height, own_ref.shape[1]), lambda i: (first + i, 0))
    pltpu.emit_pipeline(body, grid=(span,), in_specs=[block, block])(own_ref, other_ref)
    rows = scale_ref.shape[0]
    code_ref[pl.ds(code_ref.shape[0] - rows, rows), :] = scale_ref[...].astype(jnp.int32).astype(jnp.int16)


def join_kernel(first, span, height, arrivals, mask_ref, other_mask_ref, own_ref, other_ref, dense_ref, *refs):
    code_refs, out_ref, scale_ref = refs[:arrivals], refs[-2], refs[-1]
    rows = scale_ref.shape[0] // max(arrivals, 1)
    for number, code_ref in enumerate(code_refs):
        scales = code_ref[pl.ds(code_ref.shape[0] - rows, rows), :].astype(jnp.int32).astype(jnp.float32)
        scale_ref[pl.ds(number * rows, rows), :] = scales

    def body(own_block, other_block, out_block):
        step = pl.program_id(0)
        total = block_product((mask_ref, other_mask_ref), first + step, (own_block, other_block), dense_ref)
        for number, code_ref in enumerate(code_refs):
            power = scale_ref[pl.ds(number * rows + 2 * step, 1), :]
            fraction = scale_ref[pl.ds(number * rows + 2 * step + 1, 1), :]
            code = code_ref[pl.ds(pl.multiple_of(step * height, height), height), :]
            unit = fraction * jnp.exp2(power) * (1.0 / FRACTION)
            total = total + code.astype(jnp.int32).astype(jnp.float32) * unit
        out_block[...] = total.astype(out_block.dtype)

    block = pl.BlockSpec((height, own_ref.shape[1]), lambda i: (first + i, 0))
    out_block = pl.BlockSpec((height, out_ref.shape[1]), lambda i: (first + i, 0))
    pltpu.emit_pipeline(
        body, grid=(span,), in_specs=[block, block], out_specs=[out_block]
    )(own_ref, other_ref, out_ref)


def after(value, *earlier):
    return lax.optimization_barrier((value, *earlier))[0]


def shards(amplitudes, pair_mask, integrals, tile_list, tile_count, owner):
    row_count, full_width = amplitudes.shape
    slots, tile_width = integrals.shape[2], integrals.shape[-1]
    block_count = pair_mask.shape[0]
    block_rows = row_count // block_count
    row_peers, col_peers = lax.axis_size("row"), lax.axis_size("col")
    peers = row_peers // HALVES
    share = slots * tile_width // peers
    offsets = pair_offsets(col_peers)
    chunks = row_chunks(block_count)

    def along(value, shift):
        return lax.ppermute(value, "row", [(r, (r + HALVES * shift) % row_peers) for r in range(row_peers)])

    def across(value, flip, down):
        pairs = []
        for r in range(row_peers):
            for c in range(col_peers):
                pairs.append((r * col_peers + c, (r ^ flip) * col_peers + (c - CORES * down) % col_peers))
        return lax.ppermute(value, ("row", "col"), pairs)

    swap = [(c, c ^ 1) for c in range(col_peers)]
    other = lax.ppermute(amplitudes, "col", swap)
    coupled = pair_mask.T
    other_coupled = lax.ppermute(coupled, "col", swap)

    pieces = pl.pallas_call(
        pack_kernel,
        in_specs=[SMEM, SMEM, VMEM],
        out_specs=[VMEM] * peers,
        out_shape=[jax.ShapeDtypeStruct((share + META_ROWS, tile_width), integrals.dtype)] * peers,
        compiler_params=PARAMS,
        name="pack",
    )(tile_list, tile_count, integrals)
    pieces = [piece if shift == 0 else along(piece, shift) for shift, piece in enumerate(pieces)]

    chosen = pl.pallas_call(
        partial(choose_kernel, col_peers, offsets),
        in_specs=[SMEM] + [VMEM] * peers,
        out_specs=[VMEM] * len(offsets),
        out_shape=[jax.ShapeDtypeStruct((CORES * share + META_ROWS, tile_width), integrals.dtype)] * len(offsets),
        compiler_params=PARAMS,
        name="choose",
    )(owner.T, *pieces)

    def weights_of(data):
        held = [data] + [along(data, shift) for shift in range(1, peers)]
        return pl.pallas_call(
            partial(fill_kernel, slots),
            in_specs=[VMEM] * peers,
            out_specs=VMEM,
            out_shape=jax.ShapeDtypeStruct((CORES * full_width, tile_width), integrals.dtype),
            compiler_params=PARAMS,
            name="fill",
        )(*held)

    plans = {}
    for offset, data in zip(offsets, chosen):
        if offset:
            plans[offset] = weights_of(across(data, 0, offset) + across(data, 1, offset))

    def cost(span):
        return pl.CostEstimate(
            flops=2 * span * block_rows * CORES * full_width * tile_width,
            bytes_accessed=span * block_rows * (CORES * full_width + tile_width) * 2,
            transcendentals=0,
        )

    arrived, sent = [], []
    for first, span in chunks:
        height = -(-2 * span // META_ROWS) * META_ROWS
        received = []
        earlier = sent[-1:] + [part for parts in arrived[:-1] for part in parts]
        for offset in offsets:
            if offset == 0:
                continue
            code = pl.pallas_call(
                partial(send_kernel, first, span, block_rows),
                in_specs=[SMEM, SMEM, HBM, HBM, VMEM],
                out_specs=VMEM,
                out_shape=jax.ShapeDtypeStruct((span * block_rows + height, tile_width), jnp.int16),
                scratch_shapes=[pltpu.VMEM((height, tile_width), jnp.float32)],
                compiler_params=PARAMS,
                cost_estimate=cost(span),
                name="send_part",
            )(coupled, other_coupled, amplitudes, other, after(plans[offset], *earlier))
            received.append(across(code, 0, -offset))
            sent.append(code)
        arrived.append(received)

    own = after(chosen[offsets.index(0)], *arrived[0])
    plans[0] = weights_of(own + across(own, 1, 0))

    out = None
    for (first, span), received in zip(chunks, arrived):
        height = -(-2 * span // META_ROWS) * META_ROWS
        operands = [coupled, other_coupled, amplitudes, other, plans[0], *received]
        specs = [SMEM, SMEM, HBM, HBM, VMEM] + [VMEM] * len(received)
        aliases = {}
        if out is not None:
            aliases = {len(operands): 0}
            operands.append(out)
            specs.append(HBM)
        out = pl.pallas_call(
            partial(join_kernel, first, span, block_rows, len(received)),
            in_specs=specs,
            out_specs=HBM,
            out_shape=jax.ShapeDtypeStruct((row_count, tile_width), jnp.bfloat16),
            scratch_shapes=[pltpu.VMEM((height * max(len(received), 1), tile_width), jnp.float32)],
            input_output_aliases=aliases,
            compiler_params=PARAMS,
            cost_estimate=cost(span),
            name="join_part",
        )(*operands)
    return out


def solution(mesh):
    return jax.shard_map(
        shards,
        mesh=mesh,
        in_specs=(
            P("row", "col"),
            P("row", "col"),
            P("row", "col", None, None, None),
            P("row", "col", None),
            P("row", "col"),
            P(None, "col"),
        ),
        out_specs=P("row", "col"),
        check_vma=False,
    )
```

```python
from functools import partial

import jax
import jax.numpy as jnp
from jax import lax
from jax.experimental import pallas as pl
from jax.experimental.pallas import tpu as pltpu
from jax.sharding import PartitionSpec as P

STEPS = 4
CORES = 2
HALVES = 2
CUTS = (0.0, 0.08, 0.33, 0.67, 0.92, 1.0)
CODE_TOP = 32767.0
FRACTION = 8192.0
META_ROWS = 16
PARAMS = pltpu.CompilerParams(vmem_limit_bytes=16 * 1024 * 1024)
SMEM = pl.BlockSpec(memory_space=pltpu.SMEM)
VMEM = pl.BlockSpec(memory_space=pltpu.VMEM)


def pair_offsets(col_count):
    pairs = col_count // CORES
    offsets = set()
    for core in range(CORES):
        for step in range(STEPS):
            offsets.add(-((core - step) // CORES) % pairs)
    return sorted(offsets)


def row_chunks(block_count):
    marks = sorted({round(block_count * cut) for cut in CUTS})
    return [(first, last - first) for first, last in zip(marks, marks[1:])]


def pack_kernel(table_ref, panel_ref, *piece_refs):
    peers = len(piece_refs)
    slots, tile_width = panel_ref.shape[2:4]
    share = slots * tile_width // peers
    place = lax.axis_index("row") // HALVES
    lane = lax.broadcasted_iota(jnp.int32, (META_ROWS, tile_width), 1)
    info = jnp.zeros((META_ROWS, tile_width), jnp.int32)
    for spot in range(slots + 1):
        info = jnp.where(lane == spot, table_ref[spot], info)
    info = info.astype(jnp.float32).astype(panel_ref.dtype)
    for shift, piece_ref in enumerate(piece_refs):
        first = lax.rem(place + shift, peers) * share
        start = pl.multiple_of(lax.rem(first, tile_width), META_ROWS)
        piece_ref[pl.ds(0, share), :] = panel_ref[0, 0, first // tile_width, pl.ds(start, share), :]
        piece_ref[pl.ds(share, META_ROWS), :] = info


def choose_kernel(col_peers, offsets, slots, table_ref, *refs):
    out_refs = refs[len(refs) - len(offsets) :]
    piece_refs = refs[: len(refs) - len(offsets)]
    peers = len(piece_refs)
    share = piece_refs[0].shape[0] - META_ROWS
    row = lax.axis_index("row")
    core = lax.rem(lax.axis_index("col"), CORES)
    sign = 1 - 2 * core
    line = lax.broadcasted_iota(jnp.int32, (META_ROWS, piece_refs[0].shape[1]), 0)
    for offset, out_ref in zip(offsets, out_refs):
        out_ref[...] = jnp.zeros_like(out_ref)
        for group, shift in enumerate((0, sign)):
            step = lax.rem(CORES * offset - shift + col_peers, col_peers)
            holder = table_ref[slots + 1 + jnp.minimum(step, STEPS - 1)]
            here = (step < STEPS) & (lax.rem(holder, HALVES) == lax.rem(row, HALVES))
            back = lax.rem(row // HALVES - holder // HALVES + peers, peers)
            for number, piece_ref in enumerate(piece_refs):

                @pl.when(here & (back == number))
                def _():
                    out_ref[pl.ds(group * share, share), :] = piece_ref[pl.ds(0, share), :]
                    rows = pl.ds(CORES * share, META_ROWS)
                    out_ref[rows, :] = jnp.where(line == group, piece_ref[pl.ds(share, META_ROWS), :], out_ref[rows, :])


def fill_kernel(slots, *refs):
    piece_refs, dense_ref = refs[:-1], refs[-1]
    peers = len(piece_refs)
    share = (piece_refs[0].shape[0] - META_ROWS) // CORES
    width, tile_width = dense_ref.shape[0] // CORES, dense_ref.shape[1]
    place = lax.axis_index("row") // HALVES
    table = piece_refs[0][pl.ds(CORES * share, META_ROWS), :].astype(jnp.float32)
    line = lax.broadcasted_iota(jnp.int32, table.shape, 0)
    lane = lax.broadcasted_iota(jnp.int32, table.shape, 1)

    def entry(group, spot):
        return jnp.max(jnp.where((line == group) & (lane == spot), table, 0.0)).astype(jnp.int32)

    dense_ref[...] = jnp.zeros_like(dense_ref)
    for group in range(CORES):
        count = entry(group, slots)
        starts = [group * width + entry(group, slot) * tile_width for slot in range(slots)]
        for shift, piece_ref in enumerate(piece_refs):
            first = lax.rem(place - shift + peers, peers) * share
            slot = first // tile_width
            start = starts[0]
            for other in range(1, slots):
                start = jnp.where(slot == other, starts[other], start)

            @pl.when(slot < count)
            def _():
                spot = pl.multiple_of(start + lax.rem(first, tile_width), META_ROWS)
                dense_ref[pl.ds(spot, share), :] = piece_ref[pl.ds(group * share, share), :]


def block_product(first, mask_ref, own_ref, other_ref, dense_ref):
    block = first + pl.program_id(0)
    width, tile_width = own_ref.shape[1], dense_ref.shape[1]
    total = None
    for group, rows_ref in enumerate((own_ref, other_ref)):
        parts = []
        for tile in range(width // tile_width):
            live = mask_ref[group * width // tile_width + tile, block].astype(jnp.float32).astype(rows_ref.dtype)
            parts.append(rows_ref[:, pl.ds(tile * tile_width, tile_width)] * live)
        weights = dense_ref[pl.ds(group * width, width), :]
        term = jnp.dot(jnp.concatenate(parts, axis=1), weights, preferred_element_type=jnp.float32)
        total = term if total is None else total + term
    return total


def send_kernel(first, mask_ref, own_ref, other_ref, dense_ref, code_ref, scale_ref):
    step, span = pl.program_id(0), pl.num_programs(0)
    height = own_ref.shape[0]
    total = block_product(first, mask_ref, own_ref, other_ref, dense_ref)
    top = jnp.max(jnp.abs(total), axis=0, keepdims=True)
    unit = jnp.where(top > 0, top, 1.0) * (1.0 / CODE_TOP)
    power = jnp.floor(jnp.log2(unit))
    fraction = jnp.ceil(unit * jnp.exp2(-power) * FRACTION)
    unit = fraction * jnp.exp2(power) * (1.0 / FRACTION)
    code = jnp.clip(jnp.round(total * (1.0 / unit)), -CODE_TOP, CODE_TOP)
    code_ref[pl.ds(pl.multiple_of(step * height, height), height), :] = code.astype(jnp.int32).astype(jnp.int16)
    scale_ref[pl.ds(2 * step, 1), :] = power
    scale_ref[pl.ds(2 * step + 1, 1), :] = fraction

    @pl.when(step == span - 1)
    def _():
        rows = scale_ref.shape[0]
        line = lax.broadcasted_iota(jnp.int32, scale_ref.shape, 0)
        kept = jnp.where(line < 2 * span, scale_ref[...], 0.0)
        code_ref[pl.ds(code_ref.shape[0] - rows, rows), :] = kept.astype(jnp.int32).astype(jnp.int16)


def join_kernel(first, mask_ref, own_ref, other_ref, dense_ref, *refs):
    code_refs, out_ref, scale_ref = refs[:-2], refs[-2], refs[-1]
    step = pl.program_id(0)
    height = own_ref.shape[0]
    rows = scale_ref.shape[0] // max(len(code_refs), 1)

    @pl.when(step == 0)
    def _():
        for number, code_ref in enumerate(code_refs):
            scales = code_ref[pl.ds(code_ref.shape[0] - rows, rows), :].astype(jnp.int32).astype(jnp.float32)
            scale_ref[pl.ds(number * rows, rows), :] = scales

    total = block_product(first, mask_ref, own_ref, other_ref, dense_ref)
    for number, code_ref in enumerate(code_refs):
        power = scale_ref[pl.ds(number * rows + 2 * step, 1), :]
        fraction = scale_ref[pl.ds(number * rows + 2 * step + 1, 1), :]
        code = code_ref[pl.ds(pl.multiple_of(step * height, height), height), :].astype(jnp.int32).astype(jnp.float32)
        total = total + code * (fraction * jnp.exp2(power) * (1.0 / FRACTION))
    out_ref[...] = total.astype(out_ref.dtype)


def after(value, *earlier):
    return lax.optimization_barrier((value, *earlier))[0]


def shards(amplitudes, pair_mask, integrals, tile_list, tile_count, owner):
    row_count, full_width = amplitudes.shape
    slots, tile_width = integrals.shape[2], integrals.shape[-1]
    block_count = pair_mask.shape[0]
    block_rows = row_count // block_count
    row_peers, col_peers = lax.axis_size("row"), lax.axis_size("col")
    peers = row_peers // HALVES
    share = slots * tile_width // peers
    offsets = pair_offsets(col_peers)
    chunks = row_chunks(block_count)

    def along(value, shift):
        return lax.ppermute(value, "row", [(r, (r + HALVES * shift) % row_peers) for r in range(row_peers)])

    def across(value, flip, down):
        pairs = []
        for r in range(row_peers):
            for c in range(col_peers):
                pairs.append((r * col_peers + c, (r ^ flip) * col_peers + (c - CORES * down) % col_peers))
        return lax.ppermute(value, ("row", "col"), pairs)

    swap = [(c, c ^ 1) for c in range(col_peers)]
    other = lax.ppermute(amplitudes, "col", swap)
    other_mask = lax.ppermute(pair_mask.T, "col", swap)
    masks = jnp.concatenate([pair_mask.T, other_mask])
    stored = pltpu.with_memory_space_constraint(amplitudes, pltpu.HBM)
    panels = pltpu.with_memory_space_constraint(integrals, pltpu.HBM)

    table = jnp.concatenate([tile_list[0, 0], tile_count[0], owner[:, 0]])

    pieces = pl.pallas_call(
        pack_kernel,
        in_specs=[SMEM, VMEM],
        out_specs=[VMEM] * peers,
        out_shape=[jax.ShapeDtypeStruct((share + META_ROWS, tile_width), integrals.dtype)] * peers,
        compiler_params=PARAMS,
        name="pack",
    )(table, panels)
    pieces = [piece if shift == 0 else along(piece, shift) for shift, piece in enumerate(pieces)]

    chosen = pl.pallas_call(
        partial(choose_kernel, col_peers, offsets, slots),
        in_specs=[SMEM] + [VMEM] * peers,
        out_specs=[VMEM] * len(offsets),
        out_shape=[jax.ShapeDtypeStruct((CORES * share + META_ROWS, tile_width), integrals.dtype)] * len(offsets),
        compiler_params=PARAMS,
        name="choose",
    )(after(table, masks), *pieces)

    def weights_of(data):
        held = [data] + [along(data, shift) for shift in range(1, peers)]
        return pl.pallas_call(
            partial(fill_kernel, slots),
            in_specs=[VMEM] * peers,
            out_specs=VMEM,
            out_shape=jax.ShapeDtypeStruct((CORES * full_width, tile_width), integrals.dtype),
            compiler_params=PARAMS,
            name="fill",
        )(*held)

    plans = {}
    for offset, data in zip(offsets, chosen):
        if offset:
            plans[offset] = weights_of(across(data, 0, offset) + across(data, 1, offset))

    def cost(span):
        return pl.CostEstimate(
            flops=2 * span * block_rows * CORES * full_width * tile_width,
            bytes_accessed=span * block_rows * (CORES * full_width + tile_width) * 2,
            transcendentals=0,
        )

    def chunk_specs(first, span):
        part = pl.BlockSpec((block_rows, full_width), lambda i: (first + i, 0))
        return [SMEM, part, part, pl.BlockSpec((CORES * full_width, tile_width), lambda i: (0, 0))]

    def code_shape(span):
        return (span * block_rows + -(-2 * span // META_ROWS) * META_ROWS, tile_width)

    arrived, sent = [], []
    for first, span in chunks:
        shape = code_shape(span)
        received = []
        earlier = sent[-1:] + [part for parts in arrived[:-1] for part in parts]
        for offset in offsets:
            if offset == 0:
                continue
            code = pl.pallas_call(
                partial(send_kernel, first),
                grid=(span,),
                in_specs=chunk_specs(first, span),
                out_specs=pl.BlockSpec(shape, lambda i: (0, 0)),
                out_shape=jax.ShapeDtypeStruct(shape, jnp.int16),
                scratch_shapes=[pltpu.VMEM((shape[0] - span * block_rows, tile_width), jnp.float32)],
                compiler_params=PARAMS,
                cost_estimate=cost(span),
                name="send_part",
            )(masks, stored, other, after(plans[offset], *earlier))
            received.append(across(code, 0, -offset))
            sent.append(code)
        arrived.append(received)

    own = after(chosen[offsets.index(0)], *arrived[0])
    plans[0] = weights_of(own + across(own, 1, 0))

    out = None
    for (first, span), received in zip(chunks, arrived):
        shape = code_shape(span)
        operands = [masks, stored, other, plans[0], *received]
        specs = chunk_specs(first, span) + [pl.BlockSpec(shape, lambda i: (0, 0))] * len(received)
        body, aliases = partial(join_kernel, first), {}
        if out is not None:
            body = partial(skip_operand, len(operands), body)
            aliases = {len(operands): 0}
            operands.append(out)
            specs.append(pl.BlockSpec(memory_space=pl.ANY))
        out = pl.pallas_call(
            body,
            grid=(span,),
            in_specs=specs,
            out_specs=pl.BlockSpec((block_rows, tile_width), lambda i, first=first: (first + i, 0)),
            out_shape=jax.ShapeDtypeStruct((row_count, tile_width), jnp.bfloat16),
            scratch_shapes=[
                pltpu.VMEM(((shape[0] - span * block_rows) * max(len(received), 1), tile_width), jnp.float32)
            ],
            input_output_aliases=aliases,
            compiler_params=PARAMS,
            cost_estimate=cost(span),
            name="join_part",
        )(*operands)
    return out


def skip_operand(position, body, *refs):
    body(*refs[:position], *refs[position + 1 :])


def solution(mesh):
    return jax.shard_map(
        shards,
        mesh=mesh,
        in_specs=(
            P("row", "col"),
            P("row", "col"),
            P("row", "col", None, None, None),
            P("row", "col", None),
            P("row", "col"),
            P(None, "col"),
        ),
        out_specs=P("row", "col"),
        check_vma=False,
    )
```

```python
from functools import partial

import jax
import jax.numpy as jnp
from jax import lax
from jax.experimental import pallas as pl
from jax.experimental.pallas import tpu as pltpu
from jax.sharding import PartitionSpec as P

STEPS = 4
CORES = 2
HALVES = 2
CUTS = (0.0, 0.167, 0.583, 0.917, 1.0)
CODE_TOP = 32767.0
FRACTION = 8192.0
META_ROWS = 16
PARAMS = pltpu.CompilerParams(vmem_limit_bytes=16 * 1024 * 1024)
SMEM = pl.BlockSpec(memory_space=pltpu.SMEM)
VMEM = pl.BlockSpec(memory_space=pltpu.VMEM)


def pair_offsets(col_count):
    pairs = col_count // CORES
    offsets = set()
    for core in range(CORES):
        for step in range(STEPS):
            offsets.add(-((core - step) // CORES) % pairs)
    return sorted(offsets)


def row_chunks(block_count):
    marks = sorted({round(block_count * cut) for cut in CUTS})
    return [(first, last - first) for first, last in zip(marks, marks[1:])]


def pack_kernel(table_ref, panel_ref, *piece_refs):
    peers = len(piece_refs)
    slots, tile_width = panel_ref.shape[2:4]
    share = slots * tile_width // peers
    place = lax.axis_index("row") // HALVES
    lane = lax.broadcasted_iota(jnp.int32, (META_ROWS, tile_width), 1)
    lane = lax.rem(lane, tile_width // HALVES)
    info = jnp.zeros((META_ROWS, tile_width), jnp.int32)
    for spot in range(slots + 1):
        info = jnp.where(lane == spot, table_ref[spot], info)
    info = info.astype(jnp.float32).astype(panel_ref.dtype)
    for shift, piece_ref in enumerate(piece_refs):
        first = lax.rem(place + shift, peers) * share
        start = pl.multiple_of(lax.rem(first, tile_width), META_ROWS)
        piece_ref[pl.ds(0, share), :] = panel_ref[0, 0, first // tile_width, pl.ds(start, share), :]
        piece_ref[pl.ds(share, META_ROWS), :] = info


def choose_kernel(col_peers, offsets, slots, peers, table_ref, *refs):
    piece_refs, out_refs = refs[:peers], list(refs[peers:])
    share, tile_width = piece_refs[0].shape[0] - META_ROWS, piece_refs[0].shape[1]
    half_width = tile_width // HALVES
    row = lax.axis_index("row")
    half = lax.rem(row, HALVES)
    core = lax.rem(lax.axis_index("col"), CORES)
    sign = 1 - 2 * core
    for offset in offsets:
        if offset:
            spots = [pl.multiple_of(part * half_width, half_width) for part in (half, 1 - half)]
            targets = [(out_refs.pop(0), pl.ds(spot, half_width)) for spot in spots]
        else:
            targets = [(out_refs.pop(0), pl.ds(0, tile_width))]
        for out_ref, _ in targets:
            out_ref[...] = jnp.zeros_like(out_ref)
        for group, shift in enumerate((0, sign)):
            step = lax.rem(CORES * offset - shift + col_peers, col_peers)
            holder = table_ref[slots + 1 + jnp.minimum(step, STEPS - 1)]
            here = (step < STEPS) & (lax.rem(holder, HALVES) == half)
            back = lax.rem(row // HALVES - holder // HALVES + peers, peers)
            for number, piece_ref in enumerate(piece_refs):

                @pl.when(here & (back == number))
                def _():
                    for out_ref, columns in targets:
                        line = lax.broadcasted_iota(jnp.int32, (META_ROWS, out_ref.shape[1]), 0)
                        out_ref[pl.ds(group * share, share), :] = piece_ref[pl.ds(0, share), columns]
                        rows = pl.ds(CORES * share, META_ROWS)
                        info = piece_ref[pl.ds(share, META_ROWS), columns]
                        out_ref[rows, :] = jnp.where(line == group, info, out_ref[rows, :])


def fill_kernel(slots, tile_width, *refs):
    piece_refs, dense_ref = refs[:-1], refs[-1]
    peers = len(piece_refs)
    share = (piece_refs[0].shape[0] - META_ROWS) // CORES
    width = dense_ref.shape[0] // CORES
    place = lax.axis_index("row") // HALVES
    table = piece_refs[0][pl.ds(CORES * share, META_ROWS), :].astype(jnp.float32)
    line = lax.broadcasted_iota(jnp.int32, table.shape, 0)
    lane = lax.broadcasted_iota(jnp.int32, table.shape, 1)

    def entry(group, spot):
        return jnp.max(jnp.where((line == group) & (lane == spot), table, 0.0)).astype(jnp.int32)

    dense_ref[...] = jnp.zeros_like(dense_ref)
    for group in range(CORES):
        count = entry(group, slots)
        starts = [group * width + entry(group, slot) * tile_width for slot in range(slots)]
        for shift, piece_ref in enumerate(piece_refs):
            first = lax.rem(place - shift + peers, peers) * share
            slot = first // tile_width
            start = starts[0]
            for other in range(1, slots):
                start = jnp.where(slot == other, starts[other], start)

            @pl.when(slot < count)
            def _():
                spot = pl.multiple_of(start + lax.rem(first, tile_width), META_ROWS)
                dense_ref[pl.ds(spot, share), :] = piece_ref[pl.ds(group * share, share), :]


def screen_kernel(tile_width, mask_ref, own_ref, other_ref, out_ref):
    block = pl.program_id(0)
    tiles = own_ref.shape[1] // tile_width
    for group, rows_ref in enumerate((own_ref, other_ref)):
        for tile in range(tiles):
            live = mask_ref[group * tiles + tile, block].astype(jnp.float32).astype(rows_ref.dtype)
            columns = pl.ds((group * tiles + tile) * tile_width, tile_width)
            out_ref[:, columns] = rows_ref[:, pl.ds(tile * tile_width, tile_width)] * live


def send_kernel(rows_ref, dense_ref, code_ref, scale_ref):
    step, span = pl.program_id(0), pl.num_programs(0)
    height = rows_ref.shape[0]
    total = jnp.dot(rows_ref[...], dense_ref[...], preferred_element_type=jnp.float32)
    top = jnp.max(jnp.abs(total), axis=0, keepdims=True)
    unit = jnp.where(top > 0, top, 1.0) * (1.0 / CODE_TOP)
    power = jnp.floor(jnp.log2(unit))
    fraction = jnp.ceil(unit * jnp.exp2(-power) * FRACTION)
    unit = fraction * jnp.exp2(power) * (1.0 / FRACTION)
    code = jnp.clip(jnp.round(total * (1.0 / unit)), -CODE_TOP, CODE_TOP)
    code_ref[pl.ds(pl.multiple_of(step * height, height), height), :] = code.astype(jnp.int32).astype(jnp.int16)
    scale_ref[pl.ds(2 * step, 1), :] = power
    scale_ref[pl.ds(2 * step + 1, 1), :] = fraction

    @pl.when(step == span - 1)
    def _():
        rows = scale_ref.shape[0]
        line = lax.broadcasted_iota(jnp.int32, scale_ref.shape, 0)
        kept = jnp.where(line < 2 * span, scale_ref[...], 0.0)
        code_ref[pl.ds(code_ref.shape[0] - rows, rows), :] = kept.astype(jnp.int32).astype(jnp.int16)


def join_kernel(skips, rows_ref, dense_ref, *refs):
    code_refs, out_ref, scale_ref = refs[:-2], refs[-2], refs[-1]
    step = pl.program_id(0)
    height = rows_ref.shape[0]
    tails = [code_ref.shape[0] % height for code_ref in code_refs]
    starts = [sum(tails[:number]) for number in range(len(tails))]
    first_half = lax.rem(lax.axis_index("row"), HALVES) == 0

    @pl.when(step == 0)
    def _():
        for code_ref, start, lines in zip(code_refs, starts, tails):
            scales = code_ref[pl.ds(code_ref.shape[0] - lines, lines), :].astype(jnp.int32).astype(jnp.float32)
            scale_ref[pl.ds(start, lines), :] = scales

    def decoded(number):
        block = skips[number] + step
        power = scale_ref[pl.ds(starts[number] + 2 * block, 1), :]
        fraction = scale_ref[pl.ds(starts[number] + 2 * block + 1, 1), :]
        code = code_refs[number][pl.ds(pl.multiple_of(block * height, height), height), :]
        return code.astype(jnp.int32).astype(jnp.float32) * (fraction * jnp.exp2(power) * (1.0 / FRACTION))

    total = jnp.dot(rows_ref[...], dense_ref[...], preferred_element_type=jnp.float32)
    for number in range(0, len(code_refs), HALVES):
        near, far = decoded(number), decoded(number + 1)
        left = jnp.where(first_half, near, far)
        right = jnp.where(first_half, far, near)
        total = total + jnp.concatenate([left, right], axis=1)
    out_ref[...] = total.astype(out_ref.dtype)


def after(value, *earlier):
    return lax.optimization_barrier((value, *earlier))[0]


def shards(amplitudes, pair_mask, integrals, tile_list, tile_count, owner):
    row_count, full_width = amplitudes.shape
    slots, tile_width = integrals.shape[2], integrals.shape[-1]
    half_width = tile_width // HALVES
    block_count = pair_mask.shape[0]
    block_rows = row_count // block_count
    row_peers, col_peers = lax.axis_size("row"), lax.axis_size("col")
    peers = row_peers // HALVES
    share = slots * tile_width // peers
    offsets = pair_offsets(col_peers)
    remote = [offset for offset in offsets if offset]
    chunks = row_chunks(block_count)

    def along(value, shift):
        return lax.ppermute(value, "row", [(r, (r + HALVES * shift) % row_peers) for r in range(row_peers)])

    def across(value, flip, down):
        pairs = []
        for r in range(row_peers):
            for c in range(col_peers):
                pairs.append((r * col_peers + c, (r ^ flip) * col_peers + (c - CORES * down) % col_peers))
        return lax.ppermute(value, ("row", "col"), pairs)

    swap = [(c, c ^ 1) for c in range(col_peers)]
    other = lax.ppermute(amplitudes, "col", swap)
    other_mask = lax.ppermute(pair_mask.T, "col", swap)
    masks = jnp.concatenate([pair_mask.T, other_mask])
    stored = pltpu.with_memory_space_constraint(amplitudes, pltpu.HBM)
    panels = pltpu.with_memory_space_constraint(integrals, pltpu.HBM)
    table = jnp.concatenate([tile_list[0, 0], tile_count[0], owner[:, 0]])

    pieces = pl.pallas_call(
        pack_kernel,
        in_specs=[SMEM, VMEM],
        out_specs=[VMEM] * peers,
        out_shape=[jax.ShapeDtypeStruct((share + META_ROWS, tile_width), integrals.dtype)] * peers,
        compiler_params=PARAMS,
        name="pack",
    )(table, panels)
    pieces = [piece if shift == 0 else along(piece, shift) for shift, piece in enumerate(pieces)]

    height = CORES * share + META_ROWS
    widths = []
    for offset in offsets:
        widths += [half_width] * HALVES if offset else [tile_width]
    chosen = list(
        pl.pallas_call(
            partial(choose_kernel, col_peers, offsets, slots, peers),
            in_specs=[SMEM] + [VMEM] * peers,
            out_specs=[VMEM] * len(widths),
            out_shape=[jax.ShapeDtypeStruct((height, width), integrals.dtype) for width in widths],
            compiler_params=PARAMS,
            name="choose",
        )(after(table, masks), *pieces)
    )

    def fill(held):
        return pl.pallas_call(
            partial(fill_kernel, slots, tile_width),
            in_specs=[VMEM] * peers,
            out_specs=VMEM,
            out_shape=jax.ShapeDtypeStruct((CORES * full_width, held[0].shape[1]), integrals.dtype),
            compiler_params=PARAMS,
            name="fill",
        )(*held)

    row_block = pl.BlockSpec((block_rows, full_width), lambda i: (i, 0))
    wide_block = pl.BlockSpec((block_rows, CORES * full_width), lambda i: (i, 0))
    def screen(latest):
        return pl.pallas_call(
            partial(screen_kernel, tile_width),
            grid=(block_count,),
            in_specs=[SMEM, row_block, row_block],
            out_specs=wide_block,
            out_shape=jax.ShapeDtypeStruct((row_count, CORES * full_width), amplitudes.dtype),
            compiler_params=PARAMS,
            cost_estimate=pl.CostEstimate(
                flops=CORES * row_count * full_width,
                bytes_accessed=4 * CORES * row_count * full_width,
                transcendentals=0,
            ),
            name="screen",
        )(after(masks, latest), stored, other)

    own = chosen.pop(0)
    own = own + across(own, 1, 0)
    near_weights, far_weights, screened = {}, {}, None
    for offset in remote:
        near, far = chosen.pop(0), chosen.pop(0)
        data = across(near, 0, offset) + across(far, 1, offset)
        held = [data] + [along(data, shift) for shift in range(1, peers)]
        if screened is None:
            screened = screen(held[-1])
        near_weights[offset] = fill([after(held[0], screened)] + held[1:])
        far_weights[offset] = across(near_weights[offset], 1, 0)

    def cost(span, width):
        return pl.CostEstimate(
            flops=2 * span * block_rows * CORES * full_width * width,
            bytes_accessed=span * block_rows * (CORES * full_width + width) * 2,
            transcendentals=0,
        )

    def code_shape(span):
        return (span * block_rows + -(-2 * span // META_ROWS) * META_ROWS, half_width)

    def scratch_rows(span):
        return code_shape(span)[0] - span * block_rows

    near_chunks = chunks[:-2] + [(chunks[-2][0], chunks[-2][1] + chunks[-1][1])] if len(chunks) > 1 else chunks
    rounds = [(half, first, span) for half, parts in enumerate((near_chunks, chunks)) for first, span in parts]
    arrived, sent = {}, []
    order = []
    for number, (half, first, span) in enumerate(rounds):
        earlier = sent[-1:] + [part for key in order[:-1] for part in arrived[key]]
        if number == 0:
            earlier.append(own)
        if number == len(near_chunks) - 1:
            earlier += list(far_weights.values())
        if number == len(rounds) - 2:
            earlier.append(own_weights)
        arrived[half, first] = []
        order.append((half, first))
        for offset in remote:
            weights = (near_weights, far_weights)[half][offset]
            code = pl.pallas_call(
                send_kernel,
                grid=(span,),
                in_specs=[
                    pl.BlockSpec((block_rows, CORES * full_width), lambda i, first=first: (first + i, 0)),
                    pl.BlockSpec((CORES * full_width, half_width), lambda i: (0, 0)),
                ],
                out_specs=pl.BlockSpec(code_shape(span), lambda i: (0, 0)),
                out_shape=jax.ShapeDtypeStruct(code_shape(span), jnp.int16),
                scratch_shapes=[pltpu.VMEM((scratch_rows(span), half_width), jnp.float32)],
                compiler_params=PARAMS,
                cost_estimate=cost(span, half_width),
                name="send_part",
            )(screened, after(weights, *earlier))
            arrived[half, first].append(across(code, 0, -offset))
            sent.append(code)
        if number == 0:
            own = after(own, *arrived[half, first])
            own_weights = fill([own] + [along(own, shift) for shift in range(1, peers)])

    out = None
    for first, span in chunks:
        near_first = max(start for start, _ in near_chunks if start <= first)
        received = [part for pair in zip(arrived[0, near_first], arrived[1, first]) for part in pair]
        skips = [first - near_first, 0] * len(remote)
        operands = [screened, own_weights, *received]
        specs = [
            pl.BlockSpec((block_rows, CORES * full_width), lambda i, first=first: (first + i, 0)),
            pl.BlockSpec((CORES * full_width, tile_width), lambda i: (0, 0)),
        ] + [pl.BlockSpec(part.shape, lambda i: (0, 0)) for part in received]
        body, aliases = partial(join_kernel, skips), {}
        if out is not None:
            body = partial(skip_operand, len(operands), body)
            aliases = {len(operands): 0}
            operands.append(out)
            specs.append(pl.BlockSpec(memory_space=pl.ANY))
        out = pl.pallas_call(
            body,
            grid=(span,),
            in_specs=specs,
            out_specs=pl.BlockSpec((block_rows, tile_width), lambda i, first=first: (first + i, 0)),
            out_shape=jax.ShapeDtypeStruct((row_count, tile_width), jnp.bfloat16),
            scratch_shapes=[
                pltpu.VMEM((sum(part.shape[0] % block_rows for part in received), half_width), jnp.float32)
            ],
            input_output_aliases=aliases,
            compiler_params=PARAMS,
            cost_estimate=cost(span, tile_width),
            name="join_part",
        )(*operands)
    return out


def skip_operand(position, body, *refs):
    body(*refs[:position], *refs[position + 1 :])


def solution(mesh):
    return jax.shard_map(
        shards,
        mesh=mesh,
        in_specs=(
            P("row", "col"),
            P("row", "col"),
            P("row", "col", None, None, None),
            P("row", "col", None),
            P("row", "col"),
            P(None, "col"),
        ),
        out_specs=P("row", "col"),
        check_vma=False,
    )
```

```python
from functools import partial

import jax
import jax.numpy as jnp
from jax import lax
from jax.experimental import pallas as pl
from jax.experimental.pallas import tpu as pltpu
from jax.sharding import PartitionSpec as P

STEPS = 4
CORES = 2
HALVES = 2
NEAR_CUTS = (0.0, 0.167, 0.583, 1.0)
FAR_CUTS = (0.0, 0.167, 0.583, 0.917, 1.0)
CODE_TOP = 32767.0
FRACTION = 8192.0
META_ROWS = 16
SCREEN_BLOCKS = 3
PARAMS = pltpu.CompilerParams(vmem_limit_bytes=16 * 1024 * 1024)
SMEM = pl.BlockSpec(memory_space=pltpu.SMEM)
VMEM = pl.BlockSpec(memory_space=pltpu.VMEM)


def pair_offsets(col_count):
    pairs = col_count // CORES
    offsets = set()
    for core in range(CORES):
        for step in range(STEPS):
            offsets.add(-((core - step) // CORES) % pairs)
    return sorted(offsets)


def row_chunks(block_count, cuts):
    marks = sorted({round(block_count * cut) for cut in cuts})
    return [(first, last - first) for first, last in zip(marks, marks[1:])]


def pack_kernel(table_ref, panel_ref, *piece_refs):
    peers = len(piece_refs)
    slots, tile_width = panel_ref.shape[2:4]
    share = slots * tile_width // peers
    place = lax.axis_index("row") // HALVES
    lane = lax.broadcasted_iota(jnp.int32, (META_ROWS, tile_width), 1)
    lane = lax.rem(lane, tile_width // HALVES)
    info = jnp.zeros((META_ROWS, tile_width), jnp.int32)
    for spot in range(slots + 1):
        info = jnp.where(lane == spot, table_ref[spot], info)
    info = info.astype(jnp.float32).astype(panel_ref.dtype)
    for shift, piece_ref in enumerate(piece_refs):
        first = lax.rem(place + shift, peers) * share
        start = pl.multiple_of(lax.rem(first, tile_width), META_ROWS)
        piece_ref[pl.ds(0, share), :] = panel_ref[0, 0, first // tile_width, pl.ds(start, share), :]
        piece_ref[pl.ds(share, META_ROWS), :] = info


def choose_kernel(col_peers, offsets, slots, peers, table_ref, *refs):
    piece_refs, out_refs = refs[:peers], list(refs[peers:])
    share, tile_width = piece_refs[0].shape[0] - META_ROWS, piece_refs[0].shape[1]
    half_width = tile_width // HALVES
    row = lax.axis_index("row")
    half = lax.rem(row, HALVES)
    core = lax.rem(lax.axis_index("col"), CORES)
    sign = 1 - 2 * core
    for offset in offsets:
        if offset:
            spots = [pl.multiple_of(part * half_width, half_width) for part in (half, 1 - half)]
            targets = [(out_refs.pop(0), pl.ds(spot, half_width)) for spot in spots]
        else:
            targets = [(out_refs.pop(0), pl.ds(0, tile_width))]
        for out_ref, _ in targets:
            out_ref[...] = jnp.zeros_like(out_ref)
        for group, shift in enumerate((0, sign)):
            step = lax.rem(CORES * offset - shift + col_peers, col_peers)
            holder = table_ref[slots + 1 + jnp.minimum(step, STEPS - 1)]
            here = (step < STEPS) & (lax.rem(holder, HALVES) == half)
            back = lax.rem(row // HALVES - holder // HALVES + peers, peers)
            for number, piece_ref in enumerate(piece_refs):

                @pl.when(here & (back == number))
                def _():
                    for out_ref, columns in targets:
                        line = lax.broadcasted_iota(jnp.int32, (META_ROWS, out_ref.shape[1]), 0)
                        out_ref[pl.ds(group * share, share), :] = piece_ref[pl.ds(0, share), columns]
                        rows = pl.ds(CORES * share, META_ROWS)
                        info = piece_ref[pl.ds(share, META_ROWS), columns]
                        out_ref[rows, :] = jnp.where(line == group, info, out_ref[rows, :])


def fill_kernel(slots, tile_width, *refs):
    piece_refs, dense_ref = refs[:-1], refs[-1]
    peers = len(piece_refs)
    share = (piece_refs[0].shape[0] - META_ROWS) // CORES
    width = dense_ref.shape[0] // CORES
    place = lax.axis_index("row") // HALVES
    table = piece_refs[0][pl.ds(CORES * share, META_ROWS), :].astype(jnp.float32)
    line = lax.broadcasted_iota(jnp.int32, table.shape, 0)
    lane = lax.broadcasted_iota(jnp.int32, table.shape, 1)

    def entry(group, spot):
        return jnp.max(jnp.where((line == group) & (lane == spot), table, 0.0)).astype(jnp.int32)

    dense_ref[...] = jnp.zeros_like(dense_ref)
    for group in range(CORES):
        count = entry(group, slots)
        starts = [group * width + entry(group, slot) * tile_width for slot in range(slots)]
        for shift, piece_ref in enumerate(piece_refs):
            first = lax.rem(place - shift + peers, peers) * share
            slot = first // tile_width
            start = starts[0]
            for other in range(1, slots):
                start = jnp.where(slot == other, starts[other], start)

            @pl.when(slot < count)
            def _():
                spot = pl.multiple_of(start + lax.rem(first, tile_width), META_ROWS)
                dense_ref[pl.ds(spot, share), :] = piece_ref[pl.ds(group * share, share), :]


def screen_kernel(tile_width, block_rows, mask_ref, own_ref, other_ref, out_ref):
    blocks, tiles = own_ref.shape[0] // block_rows, own_ref.shape[1] // tile_width
    for number in range(blocks):
        block = pl.program_id(0) * blocks + number
        lines = pl.ds(number * block_rows, block_rows)
        for group, rows_ref in enumerate((own_ref, other_ref)):
            for tile in range(tiles):
                live = mask_ref[group * tiles + tile, block].astype(jnp.float32).astype(rows_ref.dtype)
                columns = pl.ds((group * tiles + tile) * tile_width, tile_width)
                out_ref[lines, columns] = rows_ref[lines, pl.ds(tile * tile_width, tile_width)] * live


def send_kernel(rows_ref, dense_ref, code_ref, scale_ref):
    step, span = pl.program_id(0), pl.num_programs(0)
    height = rows_ref.shape[0]
    total = jnp.dot(rows_ref[...], dense_ref[...], preferred_element_type=jnp.float32)
    top = jnp.max(jnp.abs(total), axis=0, keepdims=True)
    unit = jnp.where(top > 0, top, 1.0) * (1.0 / CODE_TOP)
    power = jnp.floor(jnp.log2(unit))
    fraction = jnp.ceil(unit * jnp.exp2(-power) * FRACTION)
    unit = fraction * jnp.exp2(power) * (1.0 / FRACTION)
    code = jnp.clip(jnp.round(total * (1.0 / unit)), -CODE_TOP, CODE_TOP)
    code_ref[pl.ds(pl.multiple_of(step * height, height), height), :] = code.astype(jnp.int32).astype(jnp.int16)
    scale_ref[pl.ds(2 * step, 1), :] = power
    scale_ref[pl.ds(2 * step + 1, 1), :] = fraction

    @pl.when(step == span - 1)
    def _():
        rows = scale_ref.shape[0]
        line = lax.broadcasted_iota(jnp.int32, scale_ref.shape, 0)
        kept = jnp.where(line < 2 * span, scale_ref[...], 0.0)
        code_ref[pl.ds(code_ref.shape[0] - rows, rows), :] = kept.astype(jnp.int32).astype(jnp.int16)


def join_kernel(skips, rows_ref, dense_ref, *refs):
    code_refs, out_ref, scale_ref = refs[:-2], refs[-2], refs[-1]
    step = pl.program_id(0)
    height = rows_ref.shape[0]
    tails = [code_ref.shape[0] % height for code_ref in code_refs]
    starts = [sum(tails[:number]) for number in range(len(tails))]
    first_half = lax.rem(lax.axis_index("row"), HALVES) == 0

    @pl.when(step == 0)
    def _():
        for code_ref, start, lines in zip(code_refs, starts, tails):
            scales = code_ref[pl.ds(code_ref.shape[0] - lines, lines), :].astype(jnp.int32).astype(jnp.float32)
            scale_ref[pl.ds(start, lines), :] = scales

    def decoded(number):
        block = skips[number] + step
        power = scale_ref[pl.ds(starts[number] + 2 * block, 1), :]
        fraction = scale_ref[pl.ds(starts[number] + 2 * block + 1, 1), :]
        code = code_refs[number][pl.ds(pl.multiple_of(block * height, height), height), :]
        return code.astype(jnp.int32).astype(jnp.float32) * (fraction * jnp.exp2(power) * (1.0 / FRACTION))

    total = jnp.dot(rows_ref[...], dense_ref[...], preferred_element_type=jnp.float32)
    for number in range(0, len(code_refs), HALVES):
        near, far = decoded(number), decoded(number + 1)
        left = jnp.where(first_half, near, far)
        right = jnp.where(first_half, far, near)
        total = total + jnp.concatenate([left, right], axis=1)
    out_ref[...] = total.astype(out_ref.dtype)


def after(value, *earlier):
    return lax.optimization_barrier((value, *earlier))[0]


def shards(amplitudes, pair_mask, integrals, tile_list, tile_count, owner):
    row_count, full_width = amplitudes.shape
    slots, tile_width = integrals.shape[2], integrals.shape[-1]
    half_width = tile_width // HALVES
    block_count = pair_mask.shape[0]
    block_rows = row_count // block_count
    row_peers, col_peers = lax.axis_size("row"), lax.axis_size("col")
    peers = row_peers // HALVES
    share = slots * tile_width // peers
    offsets = pair_offsets(col_peers)
    remote = [offset for offset in offsets if offset]
    near_chunks, far_chunks = row_chunks(block_count, NEAR_CUTS), row_chunks(block_count, FAR_CUTS)
    chunks = row_chunks(block_count, NEAR_CUTS + FAR_CUTS)

    def along(value, shift):
        return lax.ppermute(value, "row", [(r, (r + HALVES * shift) % row_peers) for r in range(row_peers)])

    def across(value, flip, down):
        pairs = []
        for r in range(row_peers):
            for c in range(col_peers):
                pairs.append((r * col_peers + c, (r ^ flip) * col_peers + (c - CORES * down) % col_peers))
        return lax.ppermute(value, ("row", "col"), pairs)

    swap = [(c, c ^ 1) for c in range(col_peers)]
    other = lax.ppermute(amplitudes, "col", swap)
    other_mask = lax.ppermute(pair_mask.T, "col", swap)
    masks = jnp.concatenate([pair_mask.T, other_mask])
    stored = pltpu.with_memory_space_constraint(amplitudes, pltpu.HBM)
    panels = pltpu.with_memory_space_constraint(integrals, pltpu.HBM)
    table = jnp.concatenate([tile_list[0, 0], tile_count[0], owner[:, 0]])

    pieces = pl.pallas_call(
        pack_kernel,
        in_specs=[SMEM, VMEM],
        out_specs=[VMEM] * peers,
        out_shape=[jax.ShapeDtypeStruct((share + META_ROWS, tile_width), integrals.dtype)] * peers,
        compiler_params=PARAMS,
        name="pack",
    )(table, panels)
    pieces = [piece if shift == 0 else along(piece, shift) for shift, piece in enumerate(pieces)]

    height = CORES * share + META_ROWS
    widths = []
    for offset in offsets:
        widths += [half_width] * HALVES if offset else [tile_width]
    chosen = list(
        pl.pallas_call(
            partial(choose_kernel, col_peers, offsets, slots, peers),
            in_specs=[SMEM] + [VMEM] * peers,
            out_specs=[VMEM] * len(widths),
            out_shape=[jax.ShapeDtypeStruct((height, width), integrals.dtype) for width in widths],
            compiler_params=PARAMS,
            name="choose",
        )(after(table, masks), *pieces)
    )

    def fill(held):
        return pl.pallas_call(
            partial(fill_kernel, slots, tile_width),
            in_specs=[VMEM] * peers,
            out_specs=VMEM,
            out_shape=jax.ShapeDtypeStruct((CORES * full_width, held[0].shape[1]), integrals.dtype),
            compiler_params=PARAMS,
            name="fill",
        )(*held)

    together = SCREEN_BLOCKS if block_count % SCREEN_BLOCKS == 0 else 1
    row_block = pl.BlockSpec((together * block_rows, full_width), lambda i: (i, 0))
    wide_block = pl.BlockSpec((together * block_rows, CORES * full_width), lambda i: (i, 0))
    def screen(*earlier):
        return pl.pallas_call(
            partial(screen_kernel, tile_width, block_rows),
            grid=(block_count // together,),
            in_specs=[SMEM, row_block, row_block],
            out_specs=wide_block,
            out_shape=jax.ShapeDtypeStruct((row_count, CORES * full_width), amplitudes.dtype),
            compiler_params=PARAMS,
            cost_estimate=pl.CostEstimate(
                flops=CORES * row_count * full_width,
                bytes_accessed=4 * CORES * row_count * full_width,
                transcendentals=0,
            ),
            name="screen",
        )(after(masks, *earlier), stored, other)

    own = chosen.pop(0)
    own = own + across(own, 1, 0)
    near_weights, far_weights, screened = {}, {}, None
    for offset in remote:
        near, far = chosen.pop(0), chosen.pop(0)
        data = across(near, 0, offset) + across(far, 1, offset)
        held = [data] + [along(data, shift) for shift in range(1, peers)]
        if screened is None:
            screened = screen(held[-1], own)
        near_weights[offset] = fill([after(held[0], screened)] + held[1:])
        far_weights[offset] = across(near_weights[offset], 1, 0)

    def cost(span, width):
        return pl.CostEstimate(
            flops=2 * span * block_rows * CORES * full_width * width,
            bytes_accessed=span * block_rows * (CORES * full_width + width) * 2,
            transcendentals=0,
        )

    def code_shape(span):
        return (span * block_rows + -(-2 * span // META_ROWS) * META_ROWS, half_width)

    def scratch_rows(span):
        return code_shape(span)[0] - span * block_rows

    rounds = [(half, first, span) for half, parts in enumerate((near_chunks, far_chunks)) for first, span in parts]
    arrived, sent = {}, []
    order = []
    for number, (half, first, span) in enumerate(rounds):
        ahead = 1
        earlier = sent[-1:] + [part for key in order[:-ahead] for part in arrived[key]]
        if number == len(near_chunks) - 1:
            earlier += list(far_weights.values())
        if number == len(rounds) - 2:
            earlier.append(own_weights)
        arrived[half, first] = []
        order.append((half, first))
        for offset in remote:
            weights = (near_weights, far_weights)[half][offset]
            code = pl.pallas_call(
                send_kernel,
                grid=(span,),
                in_specs=[
                    pl.BlockSpec((block_rows, CORES * full_width), lambda i, first=first: (first + i, 0)),
                    pl.BlockSpec((CORES * full_width, half_width), lambda i: (0, 0)),
                ],
                out_specs=pl.BlockSpec(code_shape(span), lambda i: (0, 0)),
                out_shape=jax.ShapeDtypeStruct(code_shape(span), jnp.int16),
                scratch_shapes=[pltpu.VMEM((scratch_rows(span), half_width), jnp.float32)],
                compiler_params=PARAMS,
                cost_estimate=cost(span, half_width),
                name="send_part",
            )(screened, after(weights, *earlier))
            arrived[half, first].append(across(code, 0, -offset))
            sent.append(code)
        if number == 0:
            own = after(own, *arrived[half, first])
            own_weights = fill([own] + [along(own, shift) for shift in range(1, peers)])

    out = None
    for first, span in chunks:
        near_first = max(start for start, _ in near_chunks if start <= first)
        far_first = max(start for start, _ in far_chunks if start <= first)
        received = [part for pair in zip(arrived[0, near_first], arrived[1, far_first]) for part in pair]
        skips = [first - near_first, first - far_first] * len(remote)
        operands = [screened, own_weights, *received]
        specs = [
            pl.BlockSpec((block_rows, CORES * full_width), lambda i, first=first: (first + i, 0)),
            pl.BlockSpec((CORES * full_width, tile_width), lambda i: (0, 0)),
        ] + [pl.BlockSpec(part.shape, lambda i: (0, 0)) for part in received]
        body, aliases = partial(join_kernel, skips), {}
        if out is not None:
            body = partial(skip_operand, len(operands), body)
            aliases = {len(operands): 0}
            operands.append(out)
            specs.append(pl.BlockSpec(memory_space=pl.ANY))
        out = pl.pallas_call(
            body,
            grid=(span,),
            in_specs=specs,
            out_specs=pl.BlockSpec((block_rows, tile_width), lambda i, first=first: (first + i, 0)),
            out_shape=jax.ShapeDtypeStruct((row_count, tile_width), jnp.bfloat16),
            scratch_shapes=[
                pltpu.VMEM((sum(part.shape[0] % block_rows for part in received), half_width), jnp.float32)
            ],
            input_output_aliases=aliases,
            compiler_params=PARAMS,
            cost_estimate=cost(span, tile_width),
            name="join_part",
        )(*operands)
    return out


def skip_operand(position, body, *refs):
    body(*refs[:position], *refs[position + 1 :])


def solution(mesh):
    return jax.shard_map(
        shards,
        mesh=mesh,
        in_specs=(
            P("row", "col"),
            P("row", "col"),
            P("row", "col", None, None, None),
            P("row", "col", None),
            P("row", "col"),
            P(None, "col"),
        ),
        out_specs=P("row", "col"),
        check_vma=False,
    )
```

```python
from functools import partial

import jax
import jax.numpy as jnp
from jax import lax
from jax.experimental import pallas as pl
from jax.experimental.pallas import tpu as pltpu
from jax.sharding import PartitionSpec as P

STEPS = 4
CORES = 2
HALVES = 2
NEAR_CUTS = (0.0, 0.167, 0.583, 1.0)
FAR_CUTS = (0.0, 0.167, 0.583, 0.917, 1.0)
CODE_TOP = 32767.0
FRACTION = 8192.0
META_ROWS = 16
SCREEN_BLOCKS = 3
PARAMS = pltpu.CompilerParams(vmem_limit_bytes=16 * 1024 * 1024)
SMEM = pl.BlockSpec(memory_space=pltpu.SMEM)
VMEM = pl.BlockSpec(memory_space=pltpu.VMEM)
HBM = pl.BlockSpec(memory_space=pltpu.HBM)


def pair_offsets(col_count):
    pairs = col_count // CORES
    offsets = set()
    for core in range(CORES):
        for step in range(STEPS):
            offsets.add(-((core - step) // CORES) % pairs)
    return sorted(offsets)


def row_chunks(block_count, cuts):
    marks = sorted({round(block_count * cut) for cut in cuts})
    return [(first, last - first) for first, last in zip(marks, marks[1:])]


def pack_kernel(table_ref, panel_ref, *piece_refs):
    peers = len(piece_refs)
    slots, tile_width = panel_ref.shape[2:4]
    share = slots * tile_width // peers
    place = lax.axis_index("row") // HALVES
    lane = lax.broadcasted_iota(jnp.int32, (META_ROWS, tile_width), 1)
    lane = lax.rem(lane, tile_width // HALVES)
    info = jnp.zeros((META_ROWS, tile_width), jnp.int32)
    for spot in range(slots + 1):
        info = jnp.where(lane == spot, table_ref[spot], info)
    info = info.astype(jnp.float32).astype(panel_ref.dtype)
    for shift, piece_ref in enumerate(piece_refs):
        first = lax.rem(place + shift, peers) * share
        start = pl.multiple_of(lax.rem(first, tile_width), META_ROWS)
        piece_ref[pl.ds(0, share), :] = panel_ref[0, 0, first // tile_width, pl.ds(start, share), :]
        piece_ref[pl.ds(share, META_ROWS), :] = info


def choose_kernel(col_peers, offsets, slots, peers, table_ref, *refs):
    piece_refs, out_refs = refs[:peers], list(refs[peers:])
    share, tile_width = piece_refs[0].shape[0] - META_ROWS, piece_refs[0].shape[1]
    half_width = tile_width // HALVES
    row = lax.axis_index("row")
    half = lax.rem(row, HALVES)
    core = lax.rem(lax.axis_index("col"), CORES)
    sign = 1 - 2 * core
    for offset in offsets:
        if offset:
            spots = [pl.multiple_of(part * half_width, half_width) for part in (half, 1 - half)]
            targets = [(out_refs.pop(0), pl.ds(spot, half_width)) for spot in spots]
        else:
            targets = [(out_refs.pop(0), pl.ds(0, tile_width))]
        for out_ref, _ in targets:
            out_ref[...] = jnp.zeros_like(out_ref)
        for group, shift in enumerate((0, sign)):
            step = lax.rem(CORES * offset - shift + col_peers, col_peers)
            holder = table_ref[slots + 1 + jnp.minimum(step, STEPS - 1)]
            here = (step < STEPS) & (lax.rem(holder, HALVES) == half)
            back = lax.rem(row // HALVES - holder // HALVES + peers, peers)
            for number, piece_ref in enumerate(piece_refs):

                @pl.when(here & (back == number))
                def _():
                    for out_ref, columns in targets:
                        line = lax.broadcasted_iota(jnp.int32, (META_ROWS, out_ref.shape[1]), 0)
                        out_ref[pl.ds(group * share, share), :] = piece_ref[pl.ds(0, share), columns]
                        rows = pl.ds(CORES * share, META_ROWS)
                        info = piece_ref[pl.ds(share, META_ROWS), columns]
                        out_ref[rows, :] = jnp.where(line == group, info, out_ref[rows, :])


def fill_kernel(slots, tile_width, *refs):
    piece_refs, dense_ref = refs[:-1], refs[-1]
    peers = len(piece_refs)
    share = (piece_refs[0].shape[0] - META_ROWS) // CORES
    width = dense_ref.shape[0] // CORES
    place = lax.axis_index("row") // HALVES
    table = piece_refs[0][pl.ds(CORES * share, META_ROWS), :].astype(jnp.float32)
    line = lax.broadcasted_iota(jnp.int32, table.shape, 0)
    lane = lax.broadcasted_iota(jnp.int32, table.shape, 1)

    def entry(group, spot):
        return jnp.max(jnp.where((line == group) & (lane == spot), table, 0.0)).astype(jnp.int32)

    dense_ref[...] = jnp.zeros_like(dense_ref)
    for group in range(CORES):
        count = entry(group, slots)
        starts = [group * width + entry(group, slot) * tile_width for slot in range(slots)]
        for shift, piece_ref in enumerate(piece_refs):
            first = lax.rem(place - shift + peers, peers) * share
            slot = first // tile_width
            start = starts[0]
            for other in range(1, slots):
                start = jnp.where(slot == other, starts[other], start)

            @pl.when(slot < count)
            def _():
                spot = pl.multiple_of(start + lax.rem(first, tile_width), META_ROWS)
                dense_ref[pl.ds(spot, share), :] = piece_ref[pl.ds(group * share, share), :]


def screen_kernel(tile_width, block_rows, mask_ref, own_ref, other_ref, out_ref):
    full_width = own_ref.shape[1]
    tiles = full_width // tile_width
    block_count = own_ref.shape[0] // block_rows
    together = SCREEN_BLOCKS if block_count % SCREEN_BLOCKS == 0 else 1

    def body(own_block):
        for number in range(together):
            block = pl.program_id(0) * together + number
            lines = pl.ds(pl.multiple_of(block * block_rows, block_rows), block_rows)
            for tile in range(CORES * tiles):
                live = mask_ref[tile, block].astype(jnp.float32).astype(own_block.dtype)
                if tile < tiles:
                    part = own_block[pl.ds(number * block_rows, block_rows), pl.ds(tile * tile_width, tile_width)]
                else:
                    part = other_ref[lines, pl.ds((tile - tiles) * tile_width, tile_width)]
                out_ref[lines, pl.ds(tile * tile_width, tile_width)] = part * live

    pltpu.emit_pipeline(
        body,
        grid=(block_count // together,),
        in_specs=[pl.BlockSpec((together * block_rows, full_width), lambda i: (i, 0))],
    )(own_ref)


def send_kernel(first, span, height, rows_ref, dense_ref, code_ref, scale_ref):
    scale_ref[...] = jnp.zeros_like(scale_ref)

    @pl.loop(0, span)
    def _(step):
        lines = pl.ds(pl.multiple_of((first + step) * height, height), height)
        total = jnp.dot(rows_ref[lines, :], dense_ref[...], preferred_element_type=jnp.float32)
        top = jnp.max(jnp.abs(total), axis=0, keepdims=True)
        unit = jnp.where(top > 0, top, 1.0) * (1.0 / CODE_TOP)
        power = jnp.floor(jnp.log2(unit))
        fraction = jnp.ceil(unit * jnp.exp2(-power) * FRACTION)
        unit = fraction * jnp.exp2(power) * (1.0 / FRACTION)
        code = jnp.clip(jnp.round(total * (1.0 / unit)), -CODE_TOP, CODE_TOP)
        code_ref[pl.ds(pl.multiple_of(step * height, height), height), :] = code.astype(jnp.int32).astype(jnp.int16)
        scale_ref[pl.ds(2 * step, 1), :] = power
        scale_ref[pl.ds(2 * step + 1, 1), :] = fraction

    tail = scale_ref.shape[0]
    code_ref[pl.ds(code_ref.shape[0] - tail, tail), :] = scale_ref[...].astype(jnp.int32).astype(jnp.int16)


def join_kernel(first, span, height, skips, rows_ref, dense_ref, *refs):
    code_refs, (out_ref, scale_ref, done_ref, sems) = refs[: len(skips)], refs[-4:]
    tails = [code_ref.shape[0] % height for code_ref in code_refs]
    starts = [sum(tails[:number]) for number in range(len(tails))]
    first_half = lax.rem(lax.axis_index("row"), HALVES) == 0
    for code_ref, start, tail in zip(code_refs, starts, tails):
        scales = code_ref[pl.ds(code_ref.shape[0] - tail, tail), :].astype(jnp.int32).astype(jnp.float32)
        scale_ref[pl.ds(start, tail), :] = scales

    def copy(step):
        lines = pl.ds(pl.multiple_of((first + step) * height, height), height)
        return pltpu.make_async_copy(done_ref.at[step], out_ref.at[lines, :], sems.at[step])

    @pl.loop(0, span)
    def _(step):
        def decoded(number):
            block = skips[number] + step
            power = scale_ref[pl.ds(starts[number] + 2 * block, 1), :]
            fraction = scale_ref[pl.ds(starts[number] + 2 * block + 1, 1), :]
            code = code_refs[number][pl.ds(pl.multiple_of(block * height, height), height), :]
            return code.astype(jnp.int32).astype(jnp.float32) * (fraction * jnp.exp2(power) * (1.0 / FRACTION))

        lines = pl.ds(pl.multiple_of((first + step) * height, height), height)
        total = jnp.dot(rows_ref[lines, :], dense_ref[...], preferred_element_type=jnp.float32)
        for number in range(0, len(code_refs), HALVES):
            near, far = decoded(number), decoded(number + 1)
            left = jnp.where(first_half, near, far)
            right = jnp.where(first_half, far, near)
            total = total + jnp.concatenate([left, right], axis=1)
        done_ref[step] = total.astype(done_ref.dtype)
        copy(step).start()

    for step in range(span):
        copy(step).wait()


def after(value, *earlier):
    return lax.optimization_barrier((value, *earlier))[0]


def shards(amplitudes, pair_mask, integrals, tile_list, tile_count, owner):
    row_count, full_width = amplitudes.shape
    slots, tile_width = integrals.shape[2], integrals.shape[-1]
    half_width = tile_width // HALVES
    block_count = pair_mask.shape[0]
    block_rows = row_count // block_count
    row_peers, col_peers = lax.axis_size("row"), lax.axis_size("col")
    peers = row_peers // HALVES
    share = slots * tile_width // peers
    offsets = pair_offsets(col_peers)
    remote = [offset for offset in offsets if offset]
    near_chunks, far_chunks = row_chunks(block_count, NEAR_CUTS), row_chunks(block_count, FAR_CUTS)
    chunks = row_chunks(block_count, NEAR_CUTS + FAR_CUTS)

    def along(value, shift):
        return lax.ppermute(value, "row", [(r, (r + HALVES * shift) % row_peers) for r in range(row_peers)])

    def across(value, flip, down):
        pairs = []
        for r in range(row_peers):
            for c in range(col_peers):
                pairs.append((r * col_peers + c, (r ^ flip) * col_peers + (c - CORES * down) % col_peers))
        return lax.ppermute(value, ("row", "col"), pairs)

    swap = [(c, c ^ 1) for c in range(col_peers)]
    other = lax.ppermute(amplitudes, "col", swap)
    other_mask = lax.ppermute(pair_mask.T, "col", swap)
    masks = jnp.concatenate([pair_mask.T, other_mask])
    stored = pltpu.with_memory_space_constraint(amplitudes, pltpu.HBM)
    panels = pltpu.with_memory_space_constraint(integrals, pltpu.HBM)
    table = jnp.concatenate([tile_list[0, 0], tile_count[0], owner[:, 0]])

    pieces = pl.pallas_call(
        pack_kernel,
        in_specs=[SMEM, VMEM],
        out_specs=[VMEM] * peers,
        out_shape=[jax.ShapeDtypeStruct((share + META_ROWS, tile_width), integrals.dtype)] * peers,
        compiler_params=PARAMS,
        name="pack",
    )(table, panels)
    pieces = [piece if shift == 0 else along(piece, shift) for shift, piece in enumerate(pieces)]

    height = CORES * share + META_ROWS
    widths = []
    for offset in offsets:
        widths += [half_width] * HALVES if offset else [tile_width]
    chosen = list(
        pl.pallas_call(
            partial(choose_kernel, col_peers, offsets, slots, peers),
            in_specs=[SMEM] + [VMEM] * peers,
            out_specs=[VMEM] * len(widths),
            out_shape=[jax.ShapeDtypeStruct((height, width), integrals.dtype) for width in widths],
            compiler_params=PARAMS,
            name="choose",
        )(after(table, masks), *pieces)
    )

    def fill(held):
        return pl.pallas_call(
            partial(fill_kernel, slots, tile_width),
            in_specs=[VMEM] * peers,
            out_specs=VMEM,
            out_shape=jax.ShapeDtypeStruct((CORES * full_width, held[0].shape[1]), integrals.dtype),
            compiler_params=PARAMS,
            name="fill",
        )(*held)

    def screen(*earlier):
        return pl.pallas_call(
            partial(screen_kernel, tile_width, block_rows),
            in_specs=[SMEM, HBM, VMEM],
            out_specs=VMEM,
            out_shape=jax.ShapeDtypeStruct((row_count, CORES * full_width), amplitudes.dtype),
            compiler_params=PARAMS,
            cost_estimate=pl.CostEstimate(
                flops=CORES * row_count * full_width,
                bytes_accessed=4 * CORES * row_count * full_width,
                transcendentals=0,
            ),
            name="screen",
        )(after(masks, *earlier), stored, other)

    own = chosen.pop(0)
    own = own + across(own, 1, 0)
    near_weights, far_weights, screened = {}, {}, None
    for offset in remote:
        near, far = chosen.pop(0), chosen.pop(0)
        data = across(near, 0, offset) + across(far, 1, offset)
        held = [data] + [along(data, shift) for shift in range(1, peers)]
        if screened is None:
            screened = screen(held[-1], own)
        near_weights[offset] = fill([after(held[0], screened)] + held[1:])
        far_weights[offset] = across(near_weights[offset], 1, 0)

    def cost(span, width):
        return pl.CostEstimate(
            flops=2 * span * block_rows * CORES * full_width * width,
            bytes_accessed=span * block_rows * (CORES * full_width + width) * 2,
            transcendentals=0,
        )

    def code_shape(span):
        return (span * block_rows + -(-2 * span // META_ROWS) * META_ROWS, half_width)

    def scratch_rows(span):
        return code_shape(span)[0] - span * block_rows

    rounds = [(half, first, span) for half, parts in enumerate((near_chunks, far_chunks)) for first, span in parts]
    arrived, sent = {}, []
    order = []
    for number, (half, first, span) in enumerate(rounds):
        ahead = 1
        earlier = sent[-1:] + [part for key in order[:-ahead] for part in arrived[key]]
        if number == len(near_chunks) - 1:
            earlier += list(far_weights.values())
        if number == len(rounds) - 2:
            earlier.append(own_weights)
        arrived[half, first] = []
        order.append((half, first))
        for offset in remote:
            weights = (near_weights, far_weights)[half][offset]
            code = pl.pallas_call(
                partial(send_kernel, first, span, block_rows),
                in_specs=[VMEM, VMEM],
                out_specs=VMEM,
                out_shape=jax.ShapeDtypeStruct(code_shape(span), jnp.int16),
                scratch_shapes=[pltpu.VMEM((scratch_rows(span), half_width), jnp.float32)],
                compiler_params=PARAMS,
                cost_estimate=cost(span, half_width),
                name="send_part",
            )(screened, after(weights, *earlier))
            arrived[half, first].append(across(code, 0, -offset))
            sent.append(code)
        if number == 0:
            own = after(own, *arrived[half, first])
            own_weights = fill([own] + [along(own, shift) for shift in range(1, peers)])

    out = None
    for first, span in chunks:
        near_first = max(start for start, _ in near_chunks if start <= first)
        far_first = max(start for start, _ in far_chunks if start <= first)
        received = [part for pair in zip(arrived[0, near_first], arrived[1, far_first]) for part in pair]
        skips = [first - near_first, first - far_first] * len(remote)
        operands = [screened, own_weights, *received]
        specs = [VMEM] * len(operands)
        aliases = {}
        if out is not None:
            aliases = {len(operands): 0}
            operands.append(out)
            specs.append(HBM)
        out = pl.pallas_call(
            partial(join_kernel, first, span, block_rows, skips),
            in_specs=specs,
            out_specs=HBM,
            out_shape=jax.ShapeDtypeStruct((row_count, tile_width), jnp.bfloat16),
            scratch_shapes=[
                pltpu.VMEM((sum(part.shape[0] % block_rows for part in received), half_width), jnp.float32),
                pltpu.VMEM((span, block_rows, tile_width), jnp.bfloat16),
                pltpu.SemaphoreType.DMA((span,)),
            ],
            input_output_aliases=aliases,
            compiler_params=PARAMS,
            cost_estimate=cost(span, tile_width),
            name="join_part",
        )(*operands)
    return out


def solution(mesh):
    return jax.shard_map(
        shards,
        mesh=mesh,
        in_specs=(
            P("row", "col"),
            P("row", "col"),
            P("row", "col", None, None, None),
            P("row", "col", None),
            P("row", "col"),
            P(None, "col"),
        ),
        out_specs=P("row", "col"),
        check_vma=False,
    )
```

```python
from functools import partial

import jax
import jax.numpy as jnp
from jax import lax
from jax.experimental import pallas as pl
from jax.experimental.pallas import tpu as pltpu
from jax.sharding import PartitionSpec as P

STEPS = 4
CORES = 2
HALVES = 2
NEAR_CUTS = (0.0, 0.167, 0.583, 1.0)
FAR_CUTS = (0.0, 0.167, 0.583, 0.917, 1.0)
CODE_TOP = 32767.0
FRACTION = 8192.0
META_ROWS = 16
SCREEN_BLOCKS = 3
PARAMS = pltpu.CompilerParams(vmem_limit_bytes=16 * 1024 * 1024)
SMEM = pl.BlockSpec(memory_space=pltpu.SMEM)
VMEM = pl.BlockSpec(memory_space=pltpu.VMEM)
HBM = pl.BlockSpec(memory_space=pltpu.HBM)


def pair_offsets(col_count):
    pairs = col_count // CORES
    offsets = set()
    for core in range(CORES):
        for step in range(STEPS):
            offsets.add(-((core - step) // CORES) % pairs)
    return sorted(offsets)


def row_chunks(block_count, cuts):
    marks = sorted({round(block_count * cut) for cut in cuts})
    return [(first, last - first) for first, last in zip(marks, marks[1:])]


def pack_kernel(list_ref, count_ref, panel_ref, *piece_refs):
    peers = len(piece_refs)
    slots, tile_width = panel_ref.shape[2:4]
    share = slots * tile_width // peers
    place = lax.axis_index("row") // HALVES
    lane = lax.broadcasted_iota(jnp.int32, (META_ROWS, tile_width), 1)
    lane = lax.rem(lane, tile_width // HALVES)
    info = jnp.where(lane == slots, count_ref[0, 0], 0)
    for slot in range(slots):
        info = jnp.where(lane == slot, jnp.broadcast_to(list_ref[0, :, slot : slot + 1], lane.shape), info)
    info = info.astype(jnp.float32).astype(panel_ref.dtype)
    for shift, piece_ref in enumerate(piece_refs):
        first = lax.rem(place + shift, peers) * share
        start = pl.multiple_of(lax.rem(first, tile_width), META_ROWS)
        piece_ref[pl.ds(0, share), :] = panel_ref[0, 0, first // tile_width, pl.ds(start, share), :]
        piece_ref[pl.ds(share, META_ROWS), :] = info


def choose_kernel(col_peers, offsets, peers, plan_ref, *refs):
    piece_refs, out_refs = refs[:peers], list(refs[peers:])
    share, tile_width = piece_refs[0].shape[0] - META_ROWS, piece_refs[0].shape[1]
    half_width = tile_width // HALVES
    row = lax.axis_index("row")
    half = lax.rem(row, HALVES)
    core = lax.rem(lax.axis_index("col"), CORES)
    sign = 1 - 2 * core
    for offset in offsets:
        if offset:
            spots = [pl.multiple_of(part * half_width, half_width) for part in (half, 1 - half)]
            targets = [(out_refs.pop(0), pl.ds(spot, half_width)) for spot in spots]
        else:
            targets = [(out_refs.pop(0), pl.ds(0, tile_width))]
        for out_ref, _ in targets:
            out_ref[...] = jnp.zeros_like(out_ref)
        for group, shift in enumerate((0, sign)):
            step = lax.rem(CORES * offset - shift + col_peers, col_peers)
            holder = plan_ref[plan_ref.shape[0] - 1, jnp.minimum(step, STEPS - 1)]
            here = (step < STEPS) & (lax.rem(holder, HALVES) == half)
            back = lax.rem(row // HALVES - holder // HALVES + peers, peers)
            for number, piece_ref in enumerate(piece_refs):

                @pl.when(here & (back == number))
                def _():
                    for out_ref, columns in targets:
                        line = lax.broadcasted_iota(jnp.int32, (META_ROWS, out_ref.shape[1]), 0)
                        out_ref[pl.ds(group * share, share), :] = piece_ref[pl.ds(0, share), columns]
                        rows = pl.ds(CORES * share, META_ROWS)
                        info = piece_ref[pl.ds(share, META_ROWS), columns]
                        out_ref[rows, :] = jnp.where(line == group, info, out_ref[rows, :])


def fill_kernel(slots, tile_width, *refs):
    piece_refs, dense_ref = refs[:-1], refs[-1]
    peers = len(piece_refs)
    share = (piece_refs[0].shape[0] - META_ROWS) // CORES
    width = dense_ref.shape[0] // CORES
    place = lax.axis_index("row") // HALVES
    table = piece_refs[0][pl.ds(CORES * share, META_ROWS), :].astype(jnp.float32)
    line = lax.broadcasted_iota(jnp.int32, table.shape, 0)
    lane = lax.broadcasted_iota(jnp.int32, table.shape, 1)

    def entry(group, spot):
        return jnp.max(jnp.where((line == group) & (lane == spot), table, 0.0)).astype(jnp.int32)

    dense_ref[...] = jnp.zeros_like(dense_ref)
    for group in range(CORES):
        count = entry(group, slots)
        starts = [group * width + entry(group, slot) * tile_width for slot in range(slots)]
        for shift, piece_ref in enumerate(piece_refs):
            first = lax.rem(place - shift + peers, peers) * share
            slot = first // tile_width
            start = starts[0]
            for other in range(1, slots):
                start = jnp.where(slot == other, starts[other], start)

            @pl.when(slot < count)
            def _():
                spot = pl.multiple_of(start + lax.rem(first, tile_width), META_ROWS)
                dense_ref[pl.ds(spot, share), :] = piece_ref[pl.ds(group * share, share), :]


def screen_kernel(tile_width, block_rows, mask_ref, own_ref, other_ref, out_ref):
    full_width = own_ref.shape[1]
    tiles = full_width // tile_width
    block_count = own_ref.shape[0] // block_rows
    together = SCREEN_BLOCKS if block_count % SCREEN_BLOCKS == 0 else 1

    def body(own_block):
        for number in range(together):
            block = pl.program_id(0) * together + number
            lines = pl.ds(pl.multiple_of(block * block_rows, block_rows), block_rows)
            for tile in range(CORES * tiles):
                live = mask_ref[tile, block].astype(jnp.float32).astype(own_block.dtype)
                if tile < tiles:
                    part = own_block[pl.ds(number * block_rows, block_rows), pl.ds(tile * tile_width, tile_width)]
                else:
                    part = other_ref[lines, pl.ds((tile - tiles) * tile_width, tile_width)]
                out_ref[lines, pl.ds(tile * tile_width, tile_width)] = part * live

    pltpu.emit_pipeline(
        body,
        grid=(block_count // together,),
        in_specs=[pl.BlockSpec((together * block_rows, full_width), lambda i: (i, 0))],
    )(own_ref)


def send_kernel(first, span, height, rows_ref, dense_ref, code_ref, scale_ref):
    scale_ref[...] = jnp.zeros_like(scale_ref)
    sums = jnp.dot(rows_ref[pl.ds(first * height, span * height), :], dense_ref[...], preferred_element_type=jnp.float32)
    for step in range(span):
        total = sums[step * height : (step + 1) * height]
        top = jnp.max(jnp.abs(total), axis=0, keepdims=True)
        unit = jnp.where(top > 0, top, 1.0) * (1.0 / CODE_TOP)
        power = jnp.floor(jnp.log2(unit))
        fraction = jnp.ceil(unit * jnp.exp2(-power) * FRACTION)
        unit = fraction * jnp.exp2(power) * (1.0 / FRACTION)
        code = jnp.clip(jnp.round(total * (1.0 / unit)), -CODE_TOP, CODE_TOP)
        code_ref[pl.ds(step * height, height), :] = code.astype(jnp.int32).astype(jnp.int16)
        scale_ref[pl.ds(2 * step, 1), :] = power
        scale_ref[pl.ds(2 * step + 1, 1), :] = fraction
    tail = scale_ref.shape[0]
    code_ref[pl.ds(code_ref.shape[0] - tail, tail), :] = scale_ref[...].astype(jnp.int32).astype(jnp.int16)


def join_kernel(first, span, height, skips, rows_ref, dense_ref, *refs):
    code_refs, (out_ref, scale_ref, done_ref, sems) = refs[: len(skips)], refs[-4:]
    tails = [code_ref.shape[0] % height for code_ref in code_refs]
    starts = [sum(tails[:number]) for number in range(len(tails))]
    first_half = lax.rem(lax.axis_index("row"), HALVES) == 0
    for code_ref, start, tail in zip(code_refs, starts, tails):
        scales = code_ref[pl.ds(code_ref.shape[0] - tail, tail), :].astype(jnp.int32).astype(jnp.float32)
        scale_ref[pl.ds(start, tail), :] = scales

    def decoded(number, step):
        block = skips[number] + step
        power = scale_ref[pl.ds(starts[number] + 2 * block, 1), :]
        fraction = scale_ref[pl.ds(starts[number] + 2 * block + 1, 1), :]
        code = code_refs[number][pl.ds(block * height, height), :]
        return code.astype(jnp.int32).astype(jnp.float32) * (fraction * jnp.exp2(power) * (1.0 / FRACTION))

    sums = jnp.dot(rows_ref[pl.ds(first * height, span * height), :], dense_ref[...], preferred_element_type=jnp.float32)
    copies = []
    for step in range(span):
        total = sums[step * height : (step + 1) * height]
        for number in range(0, len(code_refs), HALVES):
            near, far = decoded(number, step), decoded(number + 1, step)
            left = jnp.where(first_half, near, far)
            right = jnp.where(first_half, far, near)
            total = total + jnp.concatenate([left, right], axis=1)
        done_ref[step] = total.astype(done_ref.dtype)
        lines = pl.ds((first + step) * height, height)
        copies.append(pltpu.make_async_copy(done_ref.at[step], out_ref.at[lines, :], sems.at[step]))
        copies[-1].start()
    for copy in copies:
        copy.wait()


def after(value, *earlier):
    return lax.optimization_barrier((value, *earlier))[0]


def shards(amplitudes, pair_mask, integrals, tile_list, tile_count, owner):
    row_count, full_width = amplitudes.shape
    slots, tile_width = integrals.shape[2], integrals.shape[-1]
    half_width = tile_width // HALVES
    block_count = pair_mask.shape[0]
    block_rows = row_count // block_count
    row_peers, col_peers = lax.axis_size("row"), lax.axis_size("col")
    peers = row_peers // HALVES
    share = slots * tile_width // peers
    offsets = pair_offsets(col_peers)
    remote = [offset for offset in offsets if offset]
    near_chunks, far_chunks = row_chunks(block_count, NEAR_CUTS), row_chunks(block_count, FAR_CUTS)
    chunks = row_chunks(block_count, NEAR_CUTS + FAR_CUTS)

    def along(value, shift):
        return lax.ppermute(value, "row", [(r, (r + HALVES * shift) % row_peers) for r in range(row_peers)])

    def across(value, flip, down):
        pairs = []
        for r in range(row_peers):
            for c in range(col_peers):
                pairs.append((r * col_peers + c, (r ^ flip) * col_peers + (c - CORES * down) % col_peers))
        return lax.ppermute(value, ("row", "col"), pairs)

    swap = [(c, c ^ 1) for c in range(col_peers)]
    other = lax.ppermute(amplitudes, "col", swap)
    other_mask = lax.ppermute(pair_mask.T, "col", swap)
    length = max(block_count, STEPS)
    plan = jnp.concatenate(
        [jnp.pad(part, ((0, 0), (0, length - part.shape[1]))) for part in (pair_mask.T, other_mask, owner.T)]
    )
    in_hbm = partial(pltpu.with_memory_space_constraint, memory_space=pltpu.HBM)

    pieces = pl.pallas_call(
        pack_kernel,
        in_specs=[VMEM, SMEM, VMEM],
        out_specs=[VMEM] * peers,
        out_shape=[jax.ShapeDtypeStruct((share + META_ROWS, tile_width), integrals.dtype)] * peers,
        compiler_params=PARAMS,
        name="pack",
    )(in_hbm(tile_list), tile_count, in_hbm(integrals))
    pieces = [piece if shift == 0 else along(piece, shift) for shift, piece in enumerate(pieces)]

    height = CORES * share + META_ROWS
    widths = []
    for offset in offsets:
        widths += [half_width] * HALVES if offset else [tile_width]
    chosen = list(
        pl.pallas_call(
            partial(choose_kernel, col_peers, offsets, peers),
            in_specs=[SMEM] + [VMEM] * peers,
            out_specs=[VMEM] * len(widths),
            out_shape=[jax.ShapeDtypeStruct((height, width), integrals.dtype) for width in widths],
            compiler_params=PARAMS,
            name="choose",
        )(plan, *pieces)
    )

    def fill(held):
        return pl.pallas_call(
            partial(fill_kernel, slots, tile_width),
            in_specs=[VMEM] * peers,
            out_specs=VMEM,
            out_shape=jax.ShapeDtypeStruct((CORES * full_width, held[0].shape[1]), integrals.dtype),
            compiler_params=PARAMS,
            name="fill",
        )(*held)

    def screen(*earlier):
        return pl.pallas_call(
            partial(screen_kernel, tile_width, block_rows),
            in_specs=[SMEM, HBM, VMEM],
            out_specs=VMEM,
            out_shape=jax.ShapeDtypeStruct((row_count, CORES * full_width), amplitudes.dtype),
            compiler_params=PARAMS,
            cost_estimate=pl.CostEstimate(
                flops=CORES * row_count * full_width,
                bytes_accessed=4 * CORES * row_count * full_width,
                transcendentals=0,
            ),
            name="screen",
        )(after(plan, *earlier), in_hbm(amplitudes), other)

    own = chosen.pop(0)
    own = own + across(own, 1, 0)
    near_weights, far_weights, screened = {}, {}, None
    for offset in remote:
        near, far = chosen.pop(0), chosen.pop(0)
        data = across(near, 0, offset) + across(far, 1, offset)
        held = [data] + [along(data, shift) for shift in range(1, peers)]
        if screened is None:
            screened = screen(held[-1], own)
        near_weights[offset] = fill([after(held[0], screened)] + held[1:])
        far_weights[offset] = across(near_weights[offset], 1, 0)

    def cost(span, width):
        return pl.CostEstimate(
            flops=2 * span * block_rows * CORES * full_width * width,
            bytes_accessed=span * block_rows * (CORES * full_width + width) * 2,
            transcendentals=0,
        )

    def code_shape(span):
        return (span * block_rows + -(-2 * span // META_ROWS) * META_ROWS, half_width)

    def scratch_rows(span):
        return code_shape(span)[0] - span * block_rows

    rounds = [(half, first, span) for half, parts in enumerate((near_chunks, far_chunks)) for first, span in parts]
    arrived, sent = {}, []
    order = []
    for number, (half, first, span) in enumerate(rounds):
        ahead = 2 if number in (3, 4) else 1
        earlier = sent[-1:] + [part for key in order[:-ahead] for part in arrived[key]]
        if number == len(near_chunks) - 1:
            earlier += list(far_weights.values())
        if number == len(rounds) - 2:
            earlier.append(own_weights)
        arrived[half, first] = []
        order.append((half, first))
        for offset in remote:
            weights = (near_weights, far_weights)[half][offset]
            code = pl.pallas_call(
                partial(send_kernel, first, span, block_rows),
                in_specs=[VMEM, VMEM],
                out_specs=VMEM,
                out_shape=jax.ShapeDtypeStruct(code_shape(span), jnp.int16),
                scratch_shapes=[pltpu.VMEM((scratch_rows(span), half_width), jnp.float32)],
                compiler_params=PARAMS,
                cost_estimate=cost(span, half_width),
                name="send_part",
            )(screened, after(weights, *earlier))
            arrived[half, first].append(across(code, 0, -offset))
            sent.append(code)
        if number == 0:
            own = after(own, *arrived[half, first])
            own_weights = fill([own] + [along(own, shift) for shift in range(1, peers)])

    out = None
    for first, span in chunks:
        near_first = max(start for start, _ in near_chunks if start <= first)
        far_first = max(start for start, _ in far_chunks if start <= first)
        received = [part for pair in zip(arrived[0, near_first], arrived[1, far_first]) for part in pair]
        skips = [first - near_first, first - far_first] * len(remote)
        operands = [screened, own_weights, *received]
        specs = [VMEM] * len(operands)
        aliases = {}
        if out is not None:
            aliases = {len(operands): 0}
            operands.append(out)
            specs.append(HBM)
        out = pl.pallas_call(
            partial(join_kernel, first, span, block_rows, skips),
            in_specs=specs,
            out_specs=HBM,
            out_shape=jax.ShapeDtypeStruct((row_count, tile_width), jnp.bfloat16),
            scratch_shapes=[
                pltpu.VMEM((sum(part.shape[0] % block_rows for part in received), half_width), jnp.float32),
                pltpu.VMEM((span, block_rows, tile_width), jnp.bfloat16),
                pltpu.SemaphoreType.DMA((span,)),
            ],
            input_output_aliases=aliases,
            compiler_params=PARAMS,
            cost_estimate=cost(span, tile_width),
            name="join_part",
        )(*operands)
    return out


def solution(mesh):
    return jax.shard_map(
        shards,
        mesh=mesh,
        in_specs=(
            P("row", "col"),
            P("row", "col"),
            P("row", "col", None, None, None),
            P("row", "col", None),
            P("row", "col"),
            P(None, "col"),
        ),
        out_specs=P("row", "col"),
        check_vma=False,
    )
```

```python
from functools import partial

import jax
import jax.numpy as jnp
from jax import lax
from jax.experimental import pallas as pl
from jax.experimental.pallas import tpu as pltpu
from jax.sharding import PartitionSpec as P

STEPS = 4
CORES = 2
HALVES = 2
NEAR_CUTS = (0.0, 0.2, 0.6, 1.0)
FAR_CUTS = (0.0, 0.2, 0.6, 1.0)
WHOLE_CUTS = (0.833, 1.0)
CODE_TOP = 32767.0
FRACTION = 8192.0
META_ROWS = 16
SCREEN_BLOCKS = 3
PARAMS = pltpu.CompilerParams(vmem_limit_bytes=16 * 1024 * 1024)
SMEM = pl.BlockSpec(memory_space=pltpu.SMEM)
VMEM = pl.BlockSpec(memory_space=pltpu.VMEM)
HBM = pl.BlockSpec(memory_space=pltpu.HBM)


def pair_offsets(col_count):
    pairs = col_count // CORES
    offsets = set()
    for core in range(CORES):
        for step in range(STEPS):
            offsets.add(-((core - step) // CORES) % pairs)
    return sorted(offsets)


def row_chunks(block_count, cuts):
    marks = sorted({round(block_count * cut) for cut in cuts})
    return [(first, last - first) for first, last in zip(marks, marks[1:])]


def pack_kernel(list_ref, count_ref, panel_ref, *piece_refs):
    peers = len(piece_refs)
    slots, tile_width = panel_ref.shape[2:4]
    share = slots * tile_width // peers
    place = lax.axis_index("row") // HALVES
    lane = lax.broadcasted_iota(jnp.int32, (META_ROWS, tile_width), 1)
    lane = lax.rem(lane, tile_width // HALVES)
    info = jnp.where(lane == slots, count_ref[0, 0], 0)
    for slot in range(slots):
        info = jnp.where(lane == slot, jnp.broadcast_to(list_ref[0, :, slot : slot + 1], lane.shape), info)
    info = info.astype(jnp.float32).astype(panel_ref.dtype)
    for shift, piece_ref in enumerate(piece_refs):
        first = lax.rem(place + shift, peers) * share
        start = pl.multiple_of(lax.rem(first, tile_width), META_ROWS)
        piece_ref[pl.ds(0, share), :] = panel_ref[0, 0, first // tile_width, pl.ds(start, share), :]
        piece_ref[pl.ds(share, META_ROWS), :] = info


def choose_kernel(col_peers, offsets, peers, owner_ref, *refs):
    piece_refs, out_refs = refs[:peers], list(refs[peers:])
    share, tile_width = piece_refs[0].shape[0] - META_ROWS, piece_refs[0].shape[1]
    half_width = tile_width // HALVES
    row = lax.axis_index("row")
    half = lax.rem(row, HALVES)
    core = lax.rem(lax.axis_index("col"), CORES)
    sign = 1 - 2 * core
    for offset in offsets:
        targets = [(out_refs.pop(0), pl.ds(0, tile_width))]
        if offset:
            spots = [pl.multiple_of(part * half_width, half_width) for part in (half, 1 - half)]
            targets += [(out_refs.pop(0), pl.ds(spot, half_width)) for spot in spots]
        for out_ref, _ in targets:
            out_ref[...] = jnp.zeros_like(out_ref)
        for group, shift in enumerate((0, sign)):
            step = lax.rem(CORES * offset - shift + col_peers, col_peers)
            holder = owner_ref[0, jnp.minimum(step, STEPS - 1)]
            here = (step < STEPS) & (lax.rem(holder, HALVES) == half)
            back = lax.rem(row // HALVES - holder // HALVES + peers, peers)
            for number, piece_ref in enumerate(piece_refs):

                @pl.when(here & (back == number))
                def _():
                    for out_ref, columns in targets:
                        line = lax.broadcasted_iota(jnp.int32, (META_ROWS, out_ref.shape[1]), 0)
                        out_ref[pl.ds(group * share, share), :] = piece_ref[pl.ds(0, share), columns]
                        rows = pl.ds(CORES * share, META_ROWS)
                        info = piece_ref[pl.ds(share, META_ROWS), columns]
                        out_ref[rows, :] = jnp.where(line == group, info, out_ref[rows, :])


def fill_kernel(slots, tile_width, *refs):
    piece_refs, dense_ref = refs[:-1], refs[-1]
    peers = len(piece_refs)
    share = (piece_refs[0].shape[0] - META_ROWS) // CORES
    width = dense_ref.shape[0] // CORES
    place = lax.axis_index("row") // HALVES
    table = piece_refs[0][pl.ds(CORES * share, META_ROWS), :].astype(jnp.float32)
    line = lax.broadcasted_iota(jnp.int32, table.shape, 0)
    lane = lax.broadcasted_iota(jnp.int32, table.shape, 1)

    def entry(group, spot):
        return jnp.max(jnp.where((line == group) & (lane == spot), table, 0.0)).astype(jnp.int32)

    dense_ref[...] = jnp.zeros_like(dense_ref)
    for group in range(CORES):
        count = entry(group, slots)
        starts = [group * width + entry(group, slot) * tile_width for slot in range(slots)]
        for shift, piece_ref in enumerate(piece_refs):
            first = lax.rem(place - shift + peers, peers) * share
            slot = first // tile_width
            start = starts[0]
            for other in range(1, slots):
                start = jnp.where(slot == other, starts[other], start)

            @pl.when(slot < count)
            def _():
                spot = pl.multiple_of(start + lax.rem(first, tile_width), META_ROWS)
                dense_ref[pl.ds(spot, share), :] = piece_ref[pl.ds(group * share, share), :]


def screen_kernel(tile_width, block_rows, mask_ref, own_ref, other_ref, out_ref):
    full_width = own_ref.shape[1]
    tiles = full_width // tile_width
    block_count = own_ref.shape[0] // block_rows
    together = SCREEN_BLOCKS if block_count % SCREEN_BLOCKS == 0 else 1

    def body(own_block):
        for number in range(together):
            block = pl.program_id(0) * together + number
            lines = pl.ds(pl.multiple_of(block * block_rows, block_rows), block_rows)
            for tile in range(CORES * tiles):
                live = mask_ref[tile, block].astype(jnp.float32).astype(own_block.dtype)
                if tile < tiles:
                    part = own_block[pl.ds(number * block_rows, block_rows), pl.ds(tile * tile_width, tile_width)]
                else:
                    part = other_ref[lines, pl.ds((tile - tiles) * tile_width, tile_width)]
                out_ref[lines, pl.ds(tile * tile_width, tile_width)] = part * live

    pltpu.emit_pipeline(
        body,
        grid=(block_count // together,),
        in_specs=[pl.BlockSpec((together * block_rows, full_width), lambda i: (i, 0))],
    )(own_ref)


def send_kernel(first, span, height, rows_ref, dense_ref, code_ref, scale_ref):
    scale_ref[...] = jnp.zeros_like(scale_ref)
    sums = jnp.dot(rows_ref[pl.ds(first * height, span * height), :], dense_ref[...], preferred_element_type=jnp.float32)
    for step in range(span):
        total = sums[step * height : (step + 1) * height]
        top = jnp.max(jnp.abs(total), axis=0, keepdims=True)
        unit = jnp.where(top > 0, top, 1.0) * (1.0 / CODE_TOP)
        power = jnp.floor(jnp.log2(unit))
        fraction = jnp.ceil(unit * jnp.exp2(-power) * FRACTION)
        unit = fraction * jnp.exp2(power) * (1.0 / FRACTION)
        code = jnp.clip(jnp.round(total * (1.0 / unit)), -CODE_TOP, CODE_TOP)
        code_ref[pl.ds(step * height, height), :] = code.astype(jnp.int32).astype(jnp.int16)
        scale_ref[pl.ds(2 * step, 1), :] = power
        scale_ref[pl.ds(2 * step + 1, 1), :] = fraction
    tail = scale_ref.shape[0]
    code_ref[pl.ds(code_ref.shape[0] - tail, tail), :] = scale_ref[...].astype(jnp.int32).astype(jnp.int16)


def join_kernel(first, span, height, skips, rows_ref, dense_ref, *refs):
    code_refs, (out_ref, scale_ref, done_ref, sems) = refs[: len(skips)], refs[-4:]
    tails = [code_ref.shape[0] % height for code_ref in code_refs]
    starts = [sum(tails[:number]) for number in range(len(tails))]
    first_half = lax.rem(lax.axis_index("row"), HALVES) == 0
    for code_ref, start, tail in zip(code_refs, starts, tails):
        scales = code_ref[pl.ds(code_ref.shape[0] - tail, tail), :].astype(jnp.int32).astype(jnp.float32)
        scale_ref[pl.ds(start, tail), :] = scales

    def decoded(number, step):
        block = skips[number] + step
        power = scale_ref[pl.ds(starts[number] + 2 * block, 1), :]
        fraction = scale_ref[pl.ds(starts[number] + 2 * block + 1, 1), :]
        code = code_refs[number][pl.ds(block * height, height), :]
        return code.astype(jnp.int32).astype(jnp.float32) * (fraction * jnp.exp2(power) * (1.0 / FRACTION))

    sums = jnp.dot(rows_ref[pl.ds(first * height, span * height), :], dense_ref[...], preferred_element_type=jnp.float32)
    copies = []
    for step in range(span):
        total = sums[step * height : (step + 1) * height]
        for number in range(0, len(code_refs), HALVES):
            near, far = decoded(number, step), decoded(number + 1, step)
            left = jnp.where(first_half, near, far)
            right = jnp.where(first_half, far, near)
            total = total + jnp.concatenate([left, right], axis=1)
        done_ref[step] = total.astype(done_ref.dtype)
        lines = pl.ds((first + step) * height, height)
        copies.append(pltpu.make_async_copy(done_ref.at[step], out_ref.at[lines, :], sems.at[step]))
        copies[-1].start()
    for copy in copies:
        copy.wait()


def whole_kernel(first, span, height, rows_ref, dense_ref, *refs):
    prior, (out_ref, done_ref, sem) = refs[:-3], refs[-3:]
    total = jnp.dot(rows_ref[pl.ds(first * height, span * height), :], dense_ref[...], preferred_element_type=jnp.float32)
    for number in range(0, len(prior) - 1, 4):
        plan_ref, part_refs, weights_ref = prior[number], prior[number + 1 : number + 3], prior[number + 3]
        width, tile_width = part_refs[0].shape[1], weights_ref.shape[1]
        for group, part_ref in enumerate(part_refs):
            screened = []
            for block in range(span):
                lines = pl.ds(block * height, height)
                parts = []
                for tile in range(width // tile_width):
                    line = group * (width // tile_width) + tile
                    live = plan_ref[line, first + block].astype(jnp.float32).astype(part_ref.dtype)
                    parts.append(part_ref[lines, pl.ds(tile * tile_width, tile_width)] * live)
                screened.append(jnp.concatenate(parts, axis=1))
            rows = jnp.concatenate(screened, axis=0)
            weights = weights_ref[pl.ds(group * width, width), :]
            total = total + jnp.dot(rows, weights, preferred_element_type=jnp.float32)
    done_ref[...] = total.astype(done_ref.dtype)
    copy = pltpu.make_async_copy(done_ref, out_ref.at[pl.ds(first * height, span * height), :], sem)
    copy.start()
    copy.wait()


def after(value, *earlier):
    return lax.optimization_barrier((value, *earlier))[0]


def shards(amplitudes, pair_mask, integrals, tile_list, tile_count, owner):
    row_count, full_width = amplitudes.shape
    slots, tile_width = integrals.shape[2], integrals.shape[-1]
    half_width = tile_width // HALVES
    block_count = pair_mask.shape[0]
    block_rows = row_count // block_count
    row_peers, col_peers = lax.axis_size("row"), lax.axis_size("col")
    peers = row_peers // HALVES
    share = slots * tile_width // peers
    offsets = pair_offsets(col_peers)
    remote = [offset for offset in offsets if offset]
    whole_chunks = row_chunks(block_count, WHOLE_CUTS)
    coded_count = whole_chunks[0][0]
    near_chunks, far_chunks = row_chunks(coded_count, NEAR_CUTS), row_chunks(coded_count, FAR_CUTS)
    chunks = row_chunks(coded_count, NEAR_CUTS + FAR_CUTS)

    def along(value, shift):
        return lax.ppermute(value, "row", [(r, (r + HALVES * shift) % row_peers) for r in range(row_peers)])

    def across(value, flip, down):
        pairs = []
        for r in range(row_peers):
            for c in range(col_peers):
                pairs.append((r * col_peers + c, (r ^ flip) * col_peers + (c - CORES * down) % col_peers))
        return lax.ppermute(value, ("row", "col"), pairs)

    swap = [(c, c ^ 1) for c in range(col_peers)]
    other = lax.ppermute(amplitudes, "col", swap)
    in_hbm = partial(pltpu.with_memory_space_constraint, memory_space=pltpu.HBM)

    def whole_rows(first, span, *earlier):
        part = amplitudes[first * block_rows : (first + span) * block_rows]
        part = after(part, *earlier) if earlier else part
        return [across(part, 0, -offset) for offset in remote]

    whole = [whole_rows(*whole_chunks[0])]

    pieces = pl.pallas_call(
        pack_kernel,
        in_specs=[VMEM, SMEM, VMEM],
        out_specs=[VMEM] * peers,
        out_shape=[jax.ShapeDtypeStruct((share + META_ROWS, tile_width), integrals.dtype)] * peers,
        compiler_params=PARAMS,
        name="pack",
    )(in_hbm(tile_list), tile_count, in_hbm(integrals))
    pieces = [piece if shift == 0 else along(piece, shift) for shift, piece in enumerate(pieces)]

    height = CORES * share + META_ROWS
    widths = []
    for offset in offsets:
        widths += [tile_width] + [half_width] * HALVES * (offset > 0)
    chosen = list(
        pl.pallas_call(
            partial(choose_kernel, col_peers, offsets, peers),
            in_specs=[SMEM] + [VMEM] * peers,
            out_specs=[VMEM] * len(widths),
            out_shape=[jax.ShapeDtypeStruct((height, width), integrals.dtype) for width in widths],
            compiler_params=PARAMS,
            name="choose",
        )(after(owner.T, other), *pieces)
    )

    other_mask = lax.ppermute(after(pair_mask.T, chosen[0]), "col", swap)
    plan = jnp.concatenate([pair_mask.T, other_mask])

    def fill(held):
        return pl.pallas_call(
            partial(fill_kernel, slots, tile_width),
            in_specs=[VMEM] * peers,
            out_specs=VMEM,
            out_shape=jax.ShapeDtypeStruct((CORES * full_width, held[0].shape[1]), integrals.dtype),
            compiler_params=PARAMS,
            name="fill",
        )(*held)

    def screen(*earlier):
        return pl.pallas_call(
            partial(screen_kernel, tile_width, block_rows),
            in_specs=[SMEM, HBM, VMEM],
            out_specs=VMEM,
            out_shape=jax.ShapeDtypeStruct((row_count, CORES * full_width), amplitudes.dtype),
            compiler_params=PARAMS,
            cost_estimate=pl.CostEstimate(
                flops=CORES * row_count * full_width,
                bytes_accessed=4 * CORES * row_count * full_width,
                transcendentals=0,
            ),
            name="screen",
        )(after(plan, *earlier), in_hbm(amplitudes), other)

    own = chosen.pop(0)
    own = own + across(own, 1, 0)
    plans = [across(plan, 0, -offset) for offset in remote]
    distant = []
    near_weights, far_weights, screened = {}, {}, None
    for offset in remote:
        full, near, far = chosen.pop(0), chosen.pop(0), chosen.pop(0)
        distant.append(full + across(full, 1, 0))
        data = across(near, 0, offset) + across(far, 1, offset)
        held = [data] + [along(data, shift) for shift in range(1, peers)]
        if screened is None:
            whole = [[(part, lax.ppermute(after(part, data), "col", swap)) for part in parts] for parts in whole]
            siblings = [sibling for parts in whole for _, sibling in parts]
            screened = screen(held[-1], own)
        near_weights[offset] = fill([after(held[0], screened, *siblings)] + held[1:])
        far_weights[offset] = across(near_weights[offset], 1, 0)

    def cost(span, width):
        return pl.CostEstimate(
            flops=2 * span * block_rows * CORES * full_width * width,
            bytes_accessed=span * block_rows * (CORES * full_width + width) * 2,
            transcendentals=0,
        )

    def code_shape(span):
        return (span * block_rows + -(-2 * span // META_ROWS) * META_ROWS, half_width)

    def scratch_rows(span):
        return code_shape(span)[0] - span * block_rows

    rounds = [(half, first, span) for half, parts in enumerate((near_chunks, far_chunks)) for first, span in parts]
    arrived, sent = {}, []
    order = []
    for number, (half, first, span) in enumerate(rounds):
        ahead = 2 if number in (3, 4) else 1
        earlier = sent[-1:] + [part for key in order[:-ahead] for part in arrived[key]]
        if number == len(near_chunks) - 1:
            earlier += list(far_weights.values())
        if number == len(rounds) - 2:
            earlier.append(own_weights)
        arrived[half, first] = []
        order.append((half, first))
        for offset in remote:
            weights = (near_weights, far_weights)[half][offset]
            code = pl.pallas_call(
                partial(send_kernel, first, span, block_rows),
                in_specs=[VMEM, VMEM],
                out_specs=VMEM,
                out_shape=jax.ShapeDtypeStruct(code_shape(span), jnp.int16),
                scratch_shapes=[pltpu.VMEM((scratch_rows(span), half_width), jnp.float32)],
                compiler_params=PARAMS,
                cost_estimate=cost(span, half_width),
                name="send_part",
            )(screened, after(weights, *earlier))
            arrived[half, first].append(across(code, 0, -offset))
            sent.append(code)
        if number == 0:
            own = after(own, *arrived[half, first])
            own_held = [own] + [along(own, shift) for shift in range(1, peers)]
            own_weights = fill(own_held)
            distant_weights = []
            for data in distant:
                data = after(data, own_held[-1])
                distant_weights.append(fill([data] + [along(data, shift) for shift in range(1, peers)]))

    def joined(out, first, span):
        near_first = max(start for start, _ in near_chunks if start <= first)
        far_first = max(start for start, _ in far_chunks if start <= first)
        received = [part for pair in zip(arrived[0, near_first], arrived[1, far_first]) for part in pair]
        skips = [first - near_first, first - far_first] * len(remote)
        operands = [screened, own_weights, *received]
        specs = [VMEM] * len(operands)
        aliases = {}
        if out is not None:
            aliases = {len(operands): 0}
            operands.append(out)
            specs.append(HBM)
        return pl.pallas_call(
            partial(join_kernel, first, span, block_rows, skips),
            in_specs=specs,
            out_specs=HBM,
            out_shape=jax.ShapeDtypeStruct((row_count, tile_width), jnp.bfloat16),
            scratch_shapes=[
                pltpu.VMEM((sum(part.shape[0] % block_rows for part in received), half_width), jnp.float32),
                pltpu.VMEM((span, block_rows, tile_width), jnp.bfloat16),
                pltpu.SemaphoreType.DMA((span,)),
            ],
            input_output_aliases=aliases,
            compiler_params=PARAMS,
            cost_estimate=cost(span, tile_width),
            name="join_part",
        )(*operands)

    def joined_whole(out, first, span, parts):
        operands, specs = [screened, own_weights], [VMEM, VMEM]
        for plan_part, (same, sibling), weights in zip(plans, parts, distant_weights):
            operands += [plan_part, same, sibling, weights]
            specs += [SMEM, VMEM, VMEM, VMEM]
        return pl.pallas_call(
            partial(whole_kernel, first, span, block_rows),
            in_specs=specs + [HBM],
            out_specs=HBM,
            out_shape=jax.ShapeDtypeStruct((row_count, tile_width), jnp.bfloat16),
            scratch_shapes=[pltpu.VMEM((span * block_rows, tile_width), jnp.bfloat16), pltpu.SemaphoreType.DMA(())],
            input_output_aliases={len(operands): 0},
            compiler_params=PARAMS,
            cost_estimate=cost(CORES * span, tile_width),
            name="join_whole",
        )(*operands, out)

    out = None
    for first, span in chunks[:-1]:
        out = joined(out, first, span)
    for (first, span), parts in zip(whole_chunks, whole):
        out = joined_whole(out, first, span, parts)
    out = joined(out, *chunks[-1])
    return out


def solution(mesh):
    return jax.shard_map(
        shards,
        mesh=mesh,
        in_specs=(
            P("row", "col"),
            P("row", "col"),
            P("row", "col", None, None, None),
            P("row", "col", None),
            P("row", "col"),
            P(None, "col"),
        ),
        out_specs=P("row", "col"),
        check_vma=False,
    )
```

```python
from functools import partial

import jax
import jax.numpy as jnp
from jax import lax
from jax.experimental import pallas as pl
from jax.experimental.pallas import tpu as pltpu
from jax.sharding import PartitionSpec as P

STEPS = 4
CORES = 2
HALVES = 2
NEAR_CUTS = (0.0, 0.167, 0.583, 1.0)
FAR_CUTS = (0.0, 0.167, 0.583, 0.917, 1.0)
CODE_TOP = 32767.0
FRACTION = 8192.0
META_ROWS = 16
SCREEN_PARTS = 4
PARAMS = pltpu.CompilerParams(vmem_limit_bytes=16 * 1024 * 1024)
SMEM = pl.BlockSpec(memory_space=pltpu.SMEM)
VMEM = pl.BlockSpec(memory_space=pltpu.VMEM)
HBM = pl.BlockSpec(memory_space=pltpu.HBM)


def pair_offsets(col_count):
    pairs = col_count // CORES
    offsets = set()
    for core in range(CORES):
        for step in range(STEPS):
            offsets.add(-((core - step) // CORES) % pairs)
    return sorted(offsets)


def partner(place, number, peers):
    return place ^ number if peers & (peers - 1) == 0 else lax.rem(place + peers - number, peers)


def row_chunks(block_count, cuts):
    marks = sorted({round(block_count * cut) for cut in cuts})
    return [(first, last - first) for first, last in zip(marks, marks[1:])]


def pack_kernel(list_ref, count_ref, panel_ref, *piece_refs):
    peers = len(piece_refs)
    slots, tile_width = panel_ref.shape[2:4]
    share = slots * tile_width // peers
    place = lax.axis_index("row") // HALVES
    lane = lax.broadcasted_iota(jnp.int32, (META_ROWS, tile_width), 1)
    lane = lax.rem(lane, tile_width // HALVES)
    info = jnp.where(lane == slots, count_ref[0, 0], 0)
    for slot in range(slots):
        info = jnp.where(lane == slot, jnp.broadcast_to(list_ref[0, :, slot : slot + 1], lane.shape), info)
    info = info.astype(jnp.float32).astype(panel_ref.dtype)
    for shift, piece_ref in enumerate(piece_refs):
        first = partner(place, shift if peers & (peers - 1) == 0 else peers - shift, peers) * share
        start = pl.multiple_of(lax.rem(first, tile_width), META_ROWS)
        piece_ref[pl.ds(0, share), :] = panel_ref[0, 0, first // tile_width, pl.ds(start, share), :]
        piece_ref[pl.ds(share, META_ROWS), :] = info


def choose_kernel(col_peers, offsets, peers, plan_ref, *refs):
    piece_refs, out_refs = refs[:peers], list(refs[peers:])
    share, tile_width = piece_refs[0].shape[0] - META_ROWS, piece_refs[0].shape[1]
    half_width = tile_width // HALVES
    row = lax.axis_index("row")
    half = lax.rem(row, HALVES)
    core = lax.rem(lax.axis_index("col"), CORES)
    sign = 1 - 2 * core
    for offset in offsets:
        if offset:
            spots = [pl.multiple_of(part * half_width, half_width) for part in (half, 1 - half)]
            targets = [(out_refs.pop(0), pl.ds(spot, half_width)) for spot in spots]
        else:
            targets = [(out_refs.pop(0), pl.ds(0, tile_width))]
        for out_ref, _ in targets:
            out_ref[...] = jnp.zeros_like(out_ref)
        for group, shift in enumerate((0, sign)):
            step = lax.rem(CORES * offset - shift + col_peers, col_peers)
            holder = plan_ref[plan_ref.shape[0] - 1, jnp.minimum(step, STEPS - 1)]
            here = (step < STEPS) & (lax.rem(holder, HALVES) == half)
            for number, piece_ref in enumerate(piece_refs):

                @pl.when(here & (partner(row // HALVES, number, peers) == holder // HALVES))
                def _():
                    for out_ref, columns in targets:
                        line = lax.broadcasted_iota(jnp.int32, (META_ROWS, out_ref.shape[1]), 0)
                        out_ref[pl.ds(group * share, share), :] = piece_ref[pl.ds(0, share), columns]
                        rows = pl.ds(CORES * share, META_ROWS)
                        info = piece_ref[pl.ds(share, META_ROWS), columns]
                        out_ref[rows, :] = jnp.where(line == group, info, out_ref[rows, :])


def fill_kernel(slots, tile_width, *refs):
    piece_refs, dense_ref = refs[:-1], refs[-1]
    peers = len(piece_refs)
    share = (piece_refs[0].shape[0] - META_ROWS) // CORES
    width = dense_ref.shape[0] // CORES
    place = lax.axis_index("row") // HALVES
    table = piece_refs[0][pl.ds(CORES * share, META_ROWS), :].astype(jnp.float32)
    line = lax.broadcasted_iota(jnp.int32, table.shape, 0)
    lane = lax.broadcasted_iota(jnp.int32, table.shape, 1)

    def entry(group, spot):
        return jnp.max(jnp.where((line == group) & (lane == spot), table, 0.0)).astype(jnp.int32)

    dense_ref[...] = jnp.zeros_like(dense_ref)
    for group in range(CORES):
        count = entry(group, slots)
        starts = [group * width + entry(group, slot) * tile_width for slot in range(slots)]
        for shift, piece_ref in enumerate(piece_refs):
            first = partner(place, shift, peers) * share
            slot = first // tile_width
            start = starts[0]
            for other in range(1, slots):
                start = jnp.where(slot == other, starts[other], start)

            @pl.when(slot < count)
            def _():
                spot = pl.multiple_of(start + lax.rem(first, tile_width), META_ROWS)
                dense_ref[pl.ds(spot, share), :] = piece_ref[pl.ds(group * share, share), :]


def screen_kernel(tile_width, block_rows, mask_ref, own_ref, other_ref, out_ref, sems):
    full_width = own_ref.shape[1]
    tiles = full_width // tile_width
    parts = sems.shape[0]
    blocks = own_ref.shape[0] // block_rows // parts
    copies = []
    for part in range(parts):
        lines = pl.ds(part * blocks * block_rows, blocks * block_rows)
        copies.append(
            pltpu.make_async_copy(own_ref.at[lines, :], out_ref.at[lines, pl.ds(0, full_width)], sems.at[part])
        )
        copies[-1].start()

    def screen(source_ref, group, block):
        lines = pl.ds(pl.multiple_of(block * block_rows, block_rows), block_rows)
        for tile in range(tiles):
            live = mask_ref[group * tiles + tile, block].astype(jnp.float32).astype(out_ref.dtype)
            part = source_ref[lines, pl.ds(tile * tile_width, tile_width)]
            out_ref[lines, pl.ds((group * tiles + tile) * tile_width, tile_width)] = part * live

    @pl.loop(0, parts * blocks)
    def _(block):
        screen(other_ref, 1, block)

    for part in range(parts):
        copies[part].wait()

        @pl.loop(part * blocks, (part + 1) * blocks)
        def _(block):
            screen(out_ref, 0, block)


def send_kernel(first, span, height, rows_ref, dense_ref, code_ref, scale_ref):
    scale_ref[...] = jnp.zeros_like(scale_ref)
    sums = jnp.dot(rows_ref[pl.ds(first * height, span * height), :], dense_ref[...], preferred_element_type=jnp.float32)
    for step in range(span):
        total = sums[step * height : (step + 1) * height]
        top = jnp.max(jnp.abs(total), axis=0, keepdims=True)
        unit = jnp.where(top > 0, top, 1.0) * (1.0 / CODE_TOP)
        power = jnp.floor(jnp.log2(unit))
        fraction = jnp.ceil(unit * jnp.exp2(-power) * FRACTION)
        unit = fraction * jnp.exp2(power) * (1.0 / FRACTION)
        code = jnp.clip(jnp.round(total * (1.0 / unit)), -CODE_TOP, CODE_TOP)
        code_ref[pl.ds(step * height, height), :] = code.astype(jnp.int32).astype(jnp.int16)
        scale_ref[pl.ds(2 * step, 1), :] = power
        scale_ref[pl.ds(2 * step + 1, 1), :] = fraction
    tail = scale_ref.shape[0]
    code_ref[pl.ds(code_ref.shape[0] - tail, tail), :] = scale_ref[...].astype(jnp.int32).astype(jnp.int16)


def join_kernel(first, span, height, skips, rows_ref, dense_ref, *refs):
    code_refs, (out_ref, scale_ref, done_ref, sems) = refs[: len(skips)], refs[-4:]
    tails = [code_ref.shape[0] % height for code_ref in code_refs]
    starts = [sum(tails[:number]) for number in range(len(tails))]
    first_half = lax.rem(lax.axis_index("row"), HALVES) == 0
    for code_ref, start, tail in zip(code_refs, starts, tails):
        scales = code_ref[pl.ds(code_ref.shape[0] - tail, tail), :].astype(jnp.int32).astype(jnp.float32)
        scale_ref[pl.ds(start, tail), :] = scales

    def decoded(number, step):
        block = skips[number] + step
        power = scale_ref[pl.ds(starts[number] + 2 * block, 1), :]
        fraction = scale_ref[pl.ds(starts[number] + 2 * block + 1, 1), :]
        code = code_refs[number][pl.ds(block * height, height), :]
        return code.astype(jnp.int32).astype(jnp.float32) * (fraction * jnp.exp2(power) * (1.0 / FRACTION))

    sums = jnp.dot(rows_ref[pl.ds(first * height, span * height), :], dense_ref[...], preferred_element_type=jnp.float32)
    copies = []
    for step in range(span):
        total = sums[step * height : (step + 1) * height]
        for number in range(0, len(code_refs), HALVES):
            near, far = decoded(number, step), decoded(number + 1, step)
            left = jnp.where(first_half, near, far)
            right = jnp.where(first_half, far, near)
            total = total + jnp.concatenate([left, right], axis=1)
        done_ref[step] = total.astype(done_ref.dtype)
        lines = pl.ds((first + step) * height, height)
        copies.append(pltpu.make_async_copy(done_ref.at[step], out_ref.at[lines, :], sems.at[step]))
        copies[-1].start()
    for copy in copies:
        copy.wait()


def after(value, *earlier):
    return lax.optimization_barrier((value, *earlier))[0]


def shards(amplitudes, pair_mask, integrals, tile_list, tile_count, owner):
    row_count, full_width = amplitudes.shape
    slots, tile_width = integrals.shape[2], integrals.shape[-1]
    half_width = tile_width // HALVES
    block_count = pair_mask.shape[0]
    block_rows = row_count // block_count
    row_peers, col_peers = lax.axis_size("row"), lax.axis_size("col")
    peers = row_peers // HALVES
    share = slots * tile_width // peers
    offsets = pair_offsets(col_peers)
    remote = [offset for offset in offsets if offset]
    near_chunks, far_chunks = row_chunks(block_count, NEAR_CUTS), row_chunks(block_count, FAR_CUTS)
    chunks = row_chunks(block_count, NEAR_CUTS + FAR_CUTS)

    def along(value, shift):
        pairs = []
        for r in range(row_peers):
            source = r // HALVES ^ shift if peers & (peers - 1) == 0 else (r // HALVES - shift) % peers
            pairs.append((source * HALVES + r % HALVES, r))
        return lax.ppermute(value, "row", pairs)

    def across(value, flip, down):
        pairs = []
        for r in range(row_peers):
            for c in range(col_peers):
                pairs.append((r * col_peers + c, (r ^ flip) * col_peers + (c - CORES * down) % col_peers))
        return lax.ppermute(value, ("row", "col"), pairs)

    swap = [(c, c ^ 1) for c in range(col_peers)]
    other = lax.ppermute(amplitudes, "col", swap)
    other_mask = lax.ppermute(pair_mask.T, "col", swap)
    length = max(block_count, STEPS)
    plan = jnp.concatenate(
        [jnp.pad(part, ((0, 0), (0, length - part.shape[1]))) for part in (pair_mask.T, other_mask, owner.T)]
    )
    in_hbm = partial(pltpu.with_memory_space_constraint, memory_space=pltpu.HBM)

    pieces = pl.pallas_call(
        pack_kernel,
        in_specs=[VMEM, SMEM, VMEM],
        out_specs=[VMEM] * peers,
        out_shape=[jax.ShapeDtypeStruct((share + META_ROWS, tile_width), integrals.dtype)] * peers,
        compiler_params=PARAMS,
        name="pack",
    )(in_hbm(tile_list), tile_count, in_hbm(integrals))
    pieces = [piece if shift == 0 else along(piece, shift) for shift, piece in enumerate(pieces)]

    height = CORES * share + META_ROWS
    widths = []
    for offset in offsets:
        widths += [half_width] * HALVES if offset else [tile_width]
    chosen = list(
        pl.pallas_call(
            partial(choose_kernel, col_peers, offsets, peers),
            in_specs=[SMEM] + [VMEM] * peers,
            out_specs=[VMEM] * len(widths),
            out_shape=[jax.ShapeDtypeStruct((height, width), integrals.dtype) for width in widths],
            compiler_params=PARAMS,
            name="choose",
        )(plan, *pieces)
    )

    def fill(held):
        return pl.pallas_call(
            partial(fill_kernel, slots, tile_width),
            in_specs=[VMEM] * peers,
            out_specs=VMEM,
            out_shape=jax.ShapeDtypeStruct((CORES * full_width, held[0].shape[1]), integrals.dtype),
            compiler_params=PARAMS,
            name="fill",
        )(*held)

    def screen(*earlier):
        return pl.pallas_call(
            partial(screen_kernel, tile_width, block_rows),
            in_specs=[SMEM, HBM, VMEM],
            out_specs=VMEM,
            out_shape=jax.ShapeDtypeStruct((row_count, CORES * full_width), amplitudes.dtype),
            compiler_params=PARAMS,
            cost_estimate=pl.CostEstimate(
                flops=CORES * row_count * full_width,
                bytes_accessed=4 * CORES * row_count * full_width,
                transcendentals=0,
            ),
            scratch_shapes=[pltpu.SemaphoreType.DMA((SCREEN_PARTS if block_count % SCREEN_PARTS == 0 else 1,))],
            name="screen",
        )(after(plan, *earlier), in_hbm(amplitudes), other)

    own = chosen.pop(0)
    own = own + across(own, 1, 0)
    near_weights, far_weights, screened = {}, {}, None
    for offset in remote:
        near, far = chosen.pop(0), chosen.pop(0)
        data = across(near, 0, offset) + across(far, 1, offset)
        held = [data] + [along(data, shift) for shift in range(1, peers)]
        if screened is None:
            screened = screen(held[-1], own)
        near_weights[offset] = fill([after(held[0], screened)] + held[1:])
        far_weights[offset] = across(near_weights[offset], 1, 0)

    def cost(span, width):
        return pl.CostEstimate(
            flops=2 * span * block_rows * CORES * full_width * width,
            bytes_accessed=span * block_rows * (CORES * full_width + width) * 2,
            transcendentals=0,
        )

    def code_shape(span):
        return (span * block_rows + -(-2 * span // META_ROWS) * META_ROWS, half_width)

    def scratch_rows(span):
        return code_shape(span)[0] - span * block_rows

    rounds = [(half, first, span) for half, parts in enumerate((near_chunks, far_chunks)) for first, span in parts]
    arrived, sent = {}, []
    order = []
    for number, (half, first, span) in enumerate(rounds):
        ahead = 2 if number in (3, 4) else 1
        earlier = sent[-1:] + [part for key in order[:-ahead] for part in arrived[key]]
        if number == len(near_chunks) - 1:
            earlier += list(far_weights.values())
        if number == len(rounds) - 2:
            earlier.append(own_weights)
        arrived[half, first] = []
        order.append((half, first))
        for offset in remote:
            weights = (near_weights, far_weights)[half][offset]
            code = pl.pallas_call(
                partial(send_kernel, first, span, block_rows),
                in_specs=[VMEM, VMEM],
                out_specs=VMEM,
                out_shape=jax.ShapeDtypeStruct(code_shape(span), jnp.int16),
                scratch_shapes=[pltpu.VMEM((scratch_rows(span), half_width), jnp.float32)],
                compiler_params=PARAMS,
                cost_estimate=cost(span, half_width),
                name="send_part",
            )(screened, after(weights, *earlier))
            arrived[half, first].append(across(code, 0, -offset))
            sent.append(code)
        if number == 0:
            own = after(own, *arrived[half, first])
            own_weights = fill([own] + [along(own, shift) for shift in range(1, peers)])

    out = None
    for first, span in chunks:
        near_first = max(start for start, _ in near_chunks if start <= first)
        far_first = max(start for start, _ in far_chunks if start <= first)
        received = [part for pair in zip(arrived[0, near_first], arrived[1, far_first]) for part in pair]
        skips = [first - near_first, first - far_first] * len(remote)
        operands = [screened, own_weights, *received]
        specs = [VMEM] * len(operands)
        aliases = {}
        if out is not None:
            aliases = {len(operands): 0}
            operands.append(out)
            specs.append(HBM)
        out = pl.pallas_call(
            partial(join_kernel, first, span, block_rows, skips),
            in_specs=specs,
            out_specs=HBM,
            out_shape=jax.ShapeDtypeStruct((row_count, tile_width), jnp.bfloat16),
            scratch_shapes=[
                pltpu.VMEM((sum(part.shape[0] % block_rows for part in received), half_width), jnp.float32),
                pltpu.VMEM((span, block_rows, tile_width), jnp.bfloat16),
                pltpu.SemaphoreType.DMA((span,)),
            ],
            input_output_aliases=aliases,
            compiler_params=PARAMS,
            cost_estimate=cost(span, tile_width),
            name="join_part",
        )(*operands)
    return out


def solution(mesh):
    return jax.shard_map(
        shards,
        mesh=mesh,
        in_specs=(
            P("row", "col"),
            P("row", "col"),
            P("row", "col", None, None, None),
            P("row", "col", None),
            P("row", "col"),
            P(None, "col"),
        ),
        out_specs=P("row", "col"),
        check_vma=False,
    )
```

```python
from functools import partial

import jax
import jax.numpy as jnp
from jax import lax
from jax.experimental import pallas as pl
from jax.experimental.pallas import tpu as pltpu
from jax.sharding import PartitionSpec as P

STEPS = 4
CORES = 2
HALVES = 2
NEAR_CUTS = (0.0, 0.167, 0.583, 1.0)
FAR_CUTS = (0.0, 0.167, 0.583, 0.917, 1.0)
CODE_TOP = 32767.0
FRACTION = 8192.0
META_ROWS = 16
SCREEN_PARTS = 4
PARAMS = pltpu.CompilerParams(vmem_limit_bytes=16 * 1024 * 1024)
SMEM = pl.BlockSpec(memory_space=pltpu.SMEM)
VMEM = pl.BlockSpec(memory_space=pltpu.VMEM)
HBM = pl.BlockSpec(memory_space=pltpu.HBM)


def pair_offsets(col_count):
    pairs = col_count // CORES
    offsets = set()
    for core in range(CORES):
        for step in range(STEPS):
            offsets.add(-((core - step) // CORES) % pairs)
    return sorted(offsets)


def partner(place, number, peers):
    return place ^ number if peers & (peers - 1) == 0 else lax.rem(place + peers - number, peers)


def row_chunks(block_count, cuts):
    marks = sorted({round(block_count * cut) for cut in cuts})
    return [(first, last - first) for first, last in zip(marks, marks[1:])]


def pack_kernel(list_ref, count_ref, panel_ref, *piece_refs):
    peers = len(piece_refs)
    slots, tile_width = panel_ref.shape[2:4]
    share = slots * tile_width // peers
    place = lax.axis_index("row") // HALVES
    lane = lax.broadcasted_iota(jnp.int32, (META_ROWS, tile_width), 1)
    lane = lax.rem(lane, tile_width // HALVES)
    info = jnp.where(lane == slots, count_ref[0, 0], 0)
    for slot in range(slots):
        info = jnp.where(lane == slot, jnp.broadcast_to(list_ref[0, :, slot : slot + 1], lane.shape), info)
    info = info.astype(jnp.float32).astype(panel_ref.dtype)
    for shift, piece_ref in enumerate(piece_refs):
        first = partner(place, shift if peers & (peers - 1) == 0 else peers - shift, peers) * share
        start = pl.multiple_of(lax.rem(first, tile_width), META_ROWS)
        piece_ref[pl.ds(0, share), :] = panel_ref[0, 0, first // tile_width, pl.ds(start, share), :]
        piece_ref[pl.ds(share, META_ROWS), :] = info


def choose_kernel(col_peers, offsets, peers, plan_ref, *refs):
    piece_refs, out_refs = refs[:peers], list(refs[peers:])
    share, tile_width = piece_refs[0].shape[0] - META_ROWS, piece_refs[0].shape[1]
    half_width = tile_width // HALVES
    row = lax.axis_index("row")
    half = lax.rem(row, HALVES)
    core = lax.rem(lax.axis_index("col"), CORES)
    sign = 1 - 2 * core
    for offset in offsets:
        if offset:
            spots = [pl.multiple_of(part * half_width, half_width) for part in (half, 1 - half)]
            targets = [(out_refs.pop(0), pl.ds(spot, half_width)) for spot in spots]
        else:
            targets = [(out_refs.pop(0), pl.ds(0, tile_width))]
        for out_ref, _ in targets:
            out_ref[...] = jnp.zeros_like(out_ref)
        for group, shift in enumerate((0, sign)):
            step = lax.rem(CORES * offset - shift + col_peers, col_peers)
            holder = plan_ref[plan_ref.shape[0] - 1, jnp.minimum(step, STEPS - 1)]
            here = (step < STEPS) & (lax.rem(holder, HALVES) == half)
            for number, piece_ref in enumerate(piece_refs):

                @pl.when(here & (partner(row // HALVES, number, peers) == holder // HALVES))
                def _():
                    for out_ref, columns in targets:
                        line = lax.broadcasted_iota(jnp.int32, (META_ROWS, out_ref.shape[1]), 0)
                        out_ref[pl.ds(group * share, share), :] = piece_ref[pl.ds(0, share), columns]
                        rows = pl.ds(CORES * share, META_ROWS)
                        info = piece_ref[pl.ds(share, META_ROWS), columns]
                        out_ref[rows, :] = jnp.where(line == group, info, out_ref[rows, :])


def fill_kernel(slots, tile_width, *refs):
    piece_refs, dense_ref = refs[:-1], refs[-1]
    peers = len(piece_refs)
    share = (piece_refs[0].shape[0] - META_ROWS) // CORES
    width = dense_ref.shape[0] // CORES
    place = lax.axis_index("row") // HALVES
    table = piece_refs[0][pl.ds(CORES * share, META_ROWS), :].astype(jnp.float32)
    line = lax.broadcasted_iota(jnp.int32, table.shape, 0)
    lane = lax.broadcasted_iota(jnp.int32, table.shape, 1)

    def entry(group, spot):
        return jnp.max(jnp.where((line == group) & (lane == spot), table, 0.0)).astype(jnp.int32)

    dense_ref[...] = jnp.zeros_like(dense_ref)
    for group in range(CORES):
        count = entry(group, slots)
        starts = [group * width + entry(group, slot) * tile_width for slot in range(slots)]
        for shift, piece_ref in enumerate(piece_refs):
            first = partner(place, shift, peers) * share
            slot = first // tile_width
            start = starts[0]
            for other in range(1, slots):
                start = jnp.where(slot == other, starts[other], start)

            @pl.when(slot < count)
            def _():
                spot = pl.multiple_of(start + lax.rem(first, tile_width), META_ROWS)
                dense_ref[pl.ds(spot, share), :] = piece_ref[pl.ds(group * share, share), :]


def screen_kernel(tile_width, block_rows, mask_ref, own_ref, other_ref, out_ref, sems):
    full_width = own_ref.shape[1]
    tiles = full_width // tile_width
    parts = sems.shape[0]
    blocks = own_ref.shape[0] // block_rows // parts
    copies = []
    for part in range(parts):
        lines = pl.ds(part * blocks * block_rows, blocks * block_rows)
        copies.append(
            pltpu.make_async_copy(own_ref.at[lines, :], out_ref.at[lines, pl.ds(0, full_width)], sems.at[part])
        )
        copies[-1].start()

    def screen(source_ref, group, block):
        lines = pl.ds(pl.multiple_of(block * block_rows, block_rows), block_rows)
        for tile in range(tiles):
            live = mask_ref[group * tiles + tile, block].astype(jnp.float32).astype(out_ref.dtype)
            part = source_ref[lines, pl.ds(tile * tile_width, tile_width)]
            out_ref[lines, pl.ds((group * tiles + tile) * tile_width, tile_width)] = part * live

    @pl.loop(0, parts * blocks)
    def _(block):
        screen(other_ref, 1, block)

    for part in range(parts):
        copies[part].wait()

        @pl.loop(part * blocks, (part + 1) * blocks)
        def _(block):
            screen(out_ref, 0, block)


def send_kernel(first, span, height, rows_ref, dense_ref, code_ref, scale_ref):
    scale_ref[...] = jnp.zeros_like(scale_ref)
    sums = jnp.dot(rows_ref[pl.ds(first * height, span * height), :], dense_ref[...], preferred_element_type=jnp.float32)
    for step in range(span):
        total = sums[step * height : (step + 1) * height]
        top = jnp.max(jnp.abs(total), axis=0, keepdims=True)
        unit = jnp.where(top > 0, top, 1.0) * (1.0 / CODE_TOP)
        power = jnp.floor(jnp.log2(unit))
        fraction = jnp.ceil(unit * jnp.exp2(-power) * FRACTION)
        unit = fraction * jnp.exp2(power) * (1.0 / FRACTION)
        code = jnp.clip(jnp.round(total * (1.0 / unit)), -CODE_TOP, CODE_TOP)
        code_ref[pl.ds(step * height, height), :] = code.astype(jnp.int32).astype(jnp.int16)
        scale_ref[pl.ds(2 * step, 1), :] = power
        scale_ref[pl.ds(2 * step + 1, 1), :] = fraction
    tail = scale_ref.shape[0]
    code_ref[pl.ds(code_ref.shape[0] - tail, tail), :] = scale_ref[...].astype(jnp.int32).astype(jnp.int16)


def join_kernel(first, span, height, skips, rows_ref, dense_ref, *refs):
    code_refs, (out_ref, scale_ref, done_ref, sems) = refs[: len(skips)], refs[-4:]
    tails = [code_ref.shape[0] % height for code_ref in code_refs]
    starts = [sum(tails[:number]) for number in range(len(tails))]
    first_half = lax.rem(lax.axis_index("row"), HALVES) == 0
    for code_ref, start, tail in zip(code_refs, starts, tails):
        scales = code_ref[pl.ds(code_ref.shape[0] - tail, tail), :].astype(jnp.int32).astype(jnp.float32)
        scale_ref[pl.ds(start, tail), :] = scales

    def decoded(number, step):
        block = skips[number] + step
        power = scale_ref[pl.ds(starts[number] + 2 * block, 1), :]
        fraction = scale_ref[pl.ds(starts[number] + 2 * block + 1, 1), :]
        code = code_refs[number][pl.ds(block * height, height), :]
        return code.astype(jnp.int32).astype(jnp.float32) * (fraction * jnp.exp2(power) * (1.0 / FRACTION))

    sums = jnp.dot(rows_ref[pl.ds(first * height, span * height), :], dense_ref[...], preferred_element_type=jnp.float32)
    copies = []
    for step in range(span):
        total = sums[step * height : (step + 1) * height]
        for number in range(0, len(code_refs), HALVES):
            near, far = decoded(number, step), decoded(number + 1, step)
            left = jnp.where(first_half, near, far)
            right = jnp.where(first_half, far, near)
            total = total + jnp.concatenate([left, right], axis=1)
        done_ref[step] = total.astype(done_ref.dtype)
        lines = pl.ds((first + step) * height, height)
        copies.append(pltpu.make_async_copy(done_ref.at[step], out_ref.at[lines, :], sems.at[step]))
        copies[-1].start()
    for copy in copies:
        copy.wait()


def after(value, *earlier):
    return lax.optimization_barrier((value, *earlier))[0]


def shards(amplitudes, pair_mask, integrals, tile_list, tile_count, owner):
    row_count, full_width = amplitudes.shape
    slots, tile_width = integrals.shape[2], integrals.shape[-1]
    half_width = tile_width // HALVES
    block_count = pair_mask.shape[0]
    block_rows = row_count // block_count
    row_peers, col_peers = lax.axis_size("row"), lax.axis_size("col")
    peers = row_peers // HALVES
    share = slots * tile_width // peers
    offsets = pair_offsets(col_peers)
    remote = [offset for offset in offsets if offset]
    near_chunks, far_chunks = row_chunks(block_count, NEAR_CUTS), row_chunks(block_count, FAR_CUTS)
    chunks = row_chunks(block_count, NEAR_CUTS + FAR_CUTS)

    def along(value, shift):
        pairs = []
        for r in range(row_peers):
            source = r // HALVES ^ shift if peers & (peers - 1) == 0 else (r // HALVES - shift) % peers
            pairs.append((source * HALVES + r % HALVES, r))
        return lax.ppermute(value, "row", pairs)

    def across(value, flip, down):
        pairs = []
        for r in range(row_peers):
            for c in range(col_peers):
                pairs.append((r * col_peers + c, (r ^ flip) * col_peers + (c - CORES * down) % col_peers))
        return lax.ppermute(value, ("row", "col"), pairs)

    swap = [(c, c ^ 1) for c in range(col_peers)]
    other = lax.ppermute(amplitudes, "col", swap)
    other_mask = lax.ppermute(pair_mask.T, "col", swap)
    length = max(block_count, STEPS)
    plan = jnp.concatenate(
        [jnp.pad(part, ((0, 0), (0, length - part.shape[1]))) for part in (pair_mask.T, other_mask, owner.T)]
    )
    in_hbm = partial(pltpu.with_memory_space_constraint, memory_space=pltpu.HBM)

    pieces = pl.pallas_call(
        pack_kernel,
        in_specs=[VMEM, SMEM, VMEM],
        out_specs=[VMEM] * peers,
        out_shape=[jax.ShapeDtypeStruct((share + META_ROWS, tile_width), integrals.dtype)] * peers,
        compiler_params=PARAMS,
        name="pack",
    )(in_hbm(tile_list), tile_count, in_hbm(integrals))
    pieces = [piece if shift == 0 else along(piece, shift) for shift, piece in enumerate(pieces)]

    height = CORES * share + META_ROWS
    widths = []
    for offset in offsets:
        widths += [half_width] * HALVES if offset else [tile_width]
    chosen = list(
        pl.pallas_call(
            partial(choose_kernel, col_peers, offsets, peers),
            in_specs=[SMEM] + [VMEM] * peers,
            out_specs=[VMEM] * len(widths),
            out_shape=[jax.ShapeDtypeStruct((height, width), integrals.dtype) for width in widths],
            compiler_params=PARAMS,
            name="choose",
        )(plan, *pieces)
    )

    def fill(held):
        return pl.pallas_call(
            partial(fill_kernel, slots, tile_width),
            in_specs=[VMEM] * peers,
            out_specs=VMEM,
            out_shape=jax.ShapeDtypeStruct((CORES * full_width, held[0].shape[1]), integrals.dtype),
            compiler_params=PARAMS,
            name="fill",
        )(*held)

    def screen(*earlier):
        return pl.pallas_call(
            partial(screen_kernel, tile_width, block_rows),
            in_specs=[SMEM, HBM, VMEM],
            out_specs=VMEM,
            out_shape=jax.ShapeDtypeStruct((row_count, CORES * full_width), amplitudes.dtype),
            compiler_params=PARAMS,
            cost_estimate=pl.CostEstimate(
                flops=CORES * row_count * full_width,
                bytes_accessed=4 * CORES * row_count * full_width,
                transcendentals=0,
            ),
            scratch_shapes=[pltpu.SemaphoreType.DMA((SCREEN_PARTS if block_count % SCREEN_PARTS == 0 else 1,))],
            name="screen",
        )(after(plan, *earlier), in_hbm(amplitudes), other)

    own = chosen.pop(0)
    own = own + across(own, 1, 0)
    near_weights, far_weights, screened = {}, {}, None
    for offset in remote:
        near, far = chosen.pop(0), chosen.pop(0)
        data = across(near, 0, offset) + across(far, 1, offset)
        held = [data] + [along(data, shift) for shift in range(1, peers)]
        if screened is None:
            screened = screen(held[1], own)
        near_weights[offset] = fill([after(held[0], screened)] + held[1:])
        far_weights[offset] = across(near_weights[offset], 1, 0)

    def cost(span, width):
        return pl.CostEstimate(
            flops=2 * span * block_rows * CORES * full_width * width,
            bytes_accessed=span * block_rows * (CORES * full_width + width) * 2,
            transcendentals=0,
        )

    def code_shape(span):
        return (span * block_rows + -(-2 * span // META_ROWS) * META_ROWS, half_width)

    def scratch_rows(span):
        return code_shape(span)[0] - span * block_rows

    rounds = [(half, first, span) for half, parts in enumerate((near_chunks, far_chunks)) for first, span in parts]
    arrived, sent = {}, []
    order = []
    for number, (half, first, span) in enumerate(rounds):
        ahead = 2 if number in (3, 4) else 1
        earlier = sent[-1:] + [part for key in order[:-ahead] for part in arrived[key]]
        if number == len(near_chunks) - 1:
            earlier += list(far_weights.values())
        if number == len(rounds) - 2:
            earlier.append(own_weights)
        arrived[half, first] = []
        order.append((half, first))
        for offset in remote:
            weights = (near_weights, far_weights)[half][offset]
            code = pl.pallas_call(
                partial(send_kernel, first, span, block_rows),
                in_specs=[VMEM, VMEM],
                out_specs=VMEM,
                out_shape=jax.ShapeDtypeStruct(code_shape(span), jnp.int16),
                scratch_shapes=[pltpu.VMEM((scratch_rows(span), half_width), jnp.float32)],
                compiler_params=PARAMS,
                cost_estimate=cost(span, half_width),
                name="send_part",
            )(screened, after(weights, *earlier))
            arrived[half, first].append(across(code, 0, -offset))
            sent.append(code)
        if number == 0:
            own = after(own, *arrived[half, first])
            own_weights = fill([own] + [along(own, shift) for shift in range(1, peers)])

    out = None
    for first, span in chunks:
        near_first = max(start for start, _ in near_chunks if start <= first)
        far_first = max(start for start, _ in far_chunks if start <= first)
        received = [part for pair in zip(arrived[0, near_first], arrived[1, far_first]) for part in pair]
        skips = [first - near_first, first - far_first] * len(remote)
        operands = [screened, own_weights, *received]
        specs = [VMEM] * len(operands)
        aliases = {}
        if out is not None:
            aliases = {len(operands): 0}
            operands.append(out)
            specs.append(HBM)
        out = pl.pallas_call(
            partial(join_kernel, first, span, block_rows, skips),
            in_specs=specs,
            out_specs=HBM,
            out_shape=jax.ShapeDtypeStruct((row_count, tile_width), jnp.bfloat16),
            scratch_shapes=[
                pltpu.VMEM((sum(part.shape[0] % block_rows for part in received), half_width), jnp.float32),
                pltpu.VMEM((span, block_rows, tile_width), jnp.bfloat16),
                pltpu.SemaphoreType.DMA((span,)),
            ],
            input_output_aliases=aliases,
            compiler_params=PARAMS,
            cost_estimate=cost(span, tile_width),
            name="join_part",
        )(*operands)
    return out


def solution(mesh):
    return jax.shard_map(
        shards,
        mesh=mesh,
        in_specs=(
            P("row", "col"),
            P("row", "col"),
            P("row", "col", None, None, None),
            P("row", "col", None),
            P("row", "col"),
            P(None, "col"),
        ),
        out_specs=P("row", "col"),
        check_vma=False,
    )
```

```python
from functools import partial

import jax
import jax.numpy as jnp
from jax import lax
from jax.experimental import pallas as pl
from jax.experimental.pallas import tpu as pltpu
from jax.sharding import PartitionSpec as P

STEPS = 4
CORES = 2
HALVES = 2
NEAR_CUTS = (0.0, 0.25, 0.667, 1.0)
FAR_CUTS = (0.0, 0.167, 0.583, 0.917, 1.0)
CODE_TOP = 32767.0
FRACTION = 8192.0
META_ROWS = 8
TILE_ROWS = 16
SCREEN_PARTS = 4
PARAMS = pltpu.CompilerParams(vmem_limit_bytes=16 * 1024 * 1024)
SMEM = pl.BlockSpec(memory_space=pltpu.SMEM)
VMEM = pl.BlockSpec(memory_space=pltpu.VMEM)
HBM = pl.BlockSpec(memory_space=pltpu.HBM)


def pair_offsets(col_count):
    pairs = col_count // CORES
    offsets = set()
    for core in range(CORES):
        for step in range(STEPS):
            offsets.add(-((core - step) // CORES) % pairs)
    return sorted(offsets)


def partner(place, number, peers):
    return place ^ number if peers & (peers - 1) == 0 else lax.rem(place + peers - number, peers)


def row_chunks(block_count, cuts):
    marks = sorted({round(block_count * cut) for cut in cuts})
    return [(first, last - first) for first, last in zip(marks, marks[1:])]


def pack_kernel(list_ref, count_ref, panel_ref, *piece_refs):
    peers = len(piece_refs)
    slots, tile_width = panel_ref.shape[2:4]
    share = slots * tile_width // peers
    place = lax.axis_index("row") // HALVES
    lane = lax.broadcasted_iota(jnp.int32, (META_ROWS, tile_width), 1)
    lane = lax.rem(lane, tile_width // HALVES)
    info = jnp.where(lane == slots, count_ref[0, 0], 0)
    for slot in range(slots):
        info = jnp.where(lane == slot, jnp.broadcast_to(list_ref[0, :, slot : slot + 1], lane.shape), info)
    info = info.astype(jnp.float32).astype(panel_ref.dtype)
    for shift, piece_ref in enumerate(piece_refs):
        first = partner(place, shift if peers & (peers - 1) == 0 else peers - shift, peers) * share
        start = pl.multiple_of(lax.rem(first, tile_width), TILE_ROWS)
        piece_ref[pl.ds(0, share), :] = panel_ref[0, 0, first // tile_width, pl.ds(start, share), :]
        piece_ref[pl.ds(share, META_ROWS), :] = info


def choose_kernel(col_peers, offsets, peers, plan_ref, *refs):
    piece_refs, out_refs = refs[:peers], list(refs[peers:])
    share, tile_width = piece_refs[0].shape[0] - META_ROWS, piece_refs[0].shape[1]
    half_width = tile_width // HALVES
    row = lax.axis_index("row")
    half = lax.rem(row, HALVES)
    core = lax.rem(lax.axis_index("col"), CORES)
    sign = 1 - 2 * core
    for offset in offsets:
        if offset:
            spots = [pl.multiple_of(part * half_width, half_width) for part in (half, 1 - half)]
            targets = [(out_refs.pop(0), pl.ds(spot, half_width)) for spot in spots]
        else:
            targets = [(out_refs.pop(0), pl.ds(0, tile_width))]
        for out_ref, _ in targets:
            out_ref[...] = jnp.zeros_like(out_ref)
        for group, shift in enumerate((0, sign)):
            step = lax.rem(CORES * offset - shift + col_peers, col_peers)
            holder = plan_ref[plan_ref.shape[0] - 1, jnp.minimum(step, STEPS - 1)]
            here = (step < STEPS) & (lax.rem(holder, HALVES) == half)
            for number, piece_ref in enumerate(piece_refs):

                @pl.when(here & (partner(row // HALVES, number, peers) == holder // HALVES))
                def _():
                    for out_ref, columns in targets:
                        line = lax.broadcasted_iota(jnp.int32, (META_ROWS, out_ref.shape[1]), 0)
                        out_ref[pl.ds(group * share, share), :] = piece_ref[pl.ds(0, share), columns]
                        rows = pl.ds(CORES * share, META_ROWS)
                        info = piece_ref[pl.ds(share, META_ROWS), columns]
                        out_ref[rows, :] = jnp.where(line == group, info, out_ref[rows, :])


def fill_kernel(slots, tile_width, *refs):
    piece_refs, dense_ref = refs[:-1], refs[-1]
    peers = len(piece_refs)
    share = (piece_refs[0].shape[0] - META_ROWS) // CORES
    width = dense_ref.shape[0] // CORES
    place = lax.axis_index("row") // HALVES
    table = piece_refs[0][pl.ds(CORES * share, META_ROWS), :].astype(jnp.float32)
    line = lax.broadcasted_iota(jnp.int32, table.shape, 0)
    lane = lax.broadcasted_iota(jnp.int32, table.shape, 1)

    def entry(group, spot):
        return jnp.max(jnp.where((line == group) & (lane == spot), table, 0.0)).astype(jnp.int32)

    dense_ref[...] = jnp.zeros_like(dense_ref)
    for group in range(CORES):
        count = entry(group, slots)
        starts = [group * width + entry(group, slot) * tile_width for slot in range(slots)]
        for shift, piece_ref in enumerate(piece_refs):
            first = partner(place, shift, peers) * share
            slot = first // tile_width
            start = starts[0]
            for other in range(1, slots):
                start = jnp.where(slot == other, starts[other], start)

            @pl.when(slot < count)
            def _():
                spot = pl.multiple_of(start + lax.rem(first, tile_width), TILE_ROWS)
                dense_ref[pl.ds(spot, share), :] = piece_ref[pl.ds(group * share, share), :]


def screen_kernel(tile_width, block_rows, mask_ref, own_ref, other_ref, out_ref, sems):
    full_width = own_ref.shape[1]
    tiles = full_width // tile_width
    parts = sems.shape[0]
    blocks = own_ref.shape[0] // block_rows // parts
    copies = []
    for part in range(parts):
        lines = pl.ds(part * blocks * block_rows, blocks * block_rows)
        copies.append(
            pltpu.make_async_copy(own_ref.at[lines, :], out_ref.at[lines, pl.ds(0, full_width)], sems.at[part])
        )
        copies[-1].start()

    def screen(source_ref, group, block):
        lines = pl.ds(pl.multiple_of(block * block_rows, block_rows), block_rows)
        for tile in range(tiles):
            live = mask_ref[group * tiles + tile, block].astype(jnp.float32).astype(out_ref.dtype)
            part = source_ref[lines, pl.ds(tile * tile_width, tile_width)]
            out_ref[lines, pl.ds((group * tiles + tile) * tile_width, tile_width)] = part * live

    @pl.loop(0, parts * blocks)
    def _(block):
        screen(other_ref, 1, block)

    for part in range(parts):
        copies[part].wait()

        @pl.loop(part * blocks, (part + 1) * blocks)
        def _(block):
            screen(out_ref, 0, block)


def send_kernel(first, span, height, rows_ref, dense_ref, code_ref, scale_ref):
    scale_ref[...] = jnp.zeros_like(scale_ref)
    sums = jnp.dot(rows_ref[pl.ds(first * height, span * height), :], dense_ref[...], preferred_element_type=jnp.float32)
    for step in range(span):
        total = sums[step * height : (step + 1) * height]
        top = jnp.max(jnp.abs(total), axis=0, keepdims=True)
        unit = jnp.where(top > 0, top, 1.0) * (1.0 / CODE_TOP)
        power = jnp.floor(jnp.log2(unit))
        fraction = jnp.ceil(unit * jnp.exp2(-power) * FRACTION)
        unit = fraction * jnp.exp2(power) * (1.0 / FRACTION)
        code = jnp.clip(jnp.round(total * (1.0 / unit)), -CODE_TOP, CODE_TOP)
        code_ref[pl.ds(step * height, height), :] = code.astype(jnp.int32).astype(jnp.int16)
        scale_ref[pl.ds(2 * step, 1), :] = power
        scale_ref[pl.ds(2 * step + 1, 1), :] = fraction
    tail = scale_ref.shape[0]
    code_ref[pl.ds(code_ref.shape[0] - tail, tail), :] = scale_ref[...].astype(jnp.int32).astype(jnp.int16)


def join_kernel(first, span, height, skips, rows_ref, dense_ref, *refs):
    code_refs, (out_ref, scale_ref, done_ref, sems) = refs[: len(skips)], refs[-4:]
    tails = [code_ref.shape[0] % height for code_ref in code_refs]
    starts = [sum(tails[:number]) for number in range(len(tails))]
    first_half = lax.rem(lax.axis_index("row"), HALVES) == 0
    for code_ref, start, tail in zip(code_refs, starts, tails):
        scales = code_ref[pl.ds(code_ref.shape[0] - tail, tail), :].astype(jnp.int32).astype(jnp.float32)
        scale_ref[pl.ds(start, tail), :] = scales

    def decoded(number, step):
        block = skips[number] + step
        power = scale_ref[pl.ds(starts[number] + 2 * block, 1), :]
        fraction = scale_ref[pl.ds(starts[number] + 2 * block + 1, 1), :]
        code = code_refs[number][pl.ds(block * height, height), :]
        return code.astype(jnp.int32).astype(jnp.float32) * (fraction * jnp.exp2(power) * (1.0 / FRACTION))

    sums = jnp.dot(rows_ref[pl.ds(first * height, span * height), :], dense_ref[...], preferred_element_type=jnp.float32)
    copies = []
    for step in range(span):
        total = sums[step * height : (step + 1) * height]
        for number in range(0, len(code_refs), HALVES):
            near, far = decoded(number, step), decoded(number + 1, step)
            left = jnp.where(first_half, near, far)
            right = jnp.where(first_half, far, near)
            total = total + jnp.concatenate([left, right], axis=1)
        done_ref[step] = total.astype(done_ref.dtype)
        lines = pl.ds((first + step) * height, height)
        copies.append(pltpu.make_async_copy(done_ref.at[step], out_ref.at[lines, :], sems.at[step]))
        copies[-1].start()
    for copy in copies:
        copy.wait()


def after(value, *earlier):
    return lax.optimization_barrier((value, *earlier))[0]


def shards(amplitudes, pair_mask, integrals, tile_list, tile_count, owner):
    row_count, full_width = amplitudes.shape
    slots, tile_width = integrals.shape[2], integrals.shape[-1]
    half_width = tile_width // HALVES
    block_count = pair_mask.shape[0]
    block_rows = row_count // block_count
    row_peers, col_peers = lax.axis_size("row"), lax.axis_size("col")
    peers = row_peers // HALVES
    share = slots * tile_width // peers
    offsets = pair_offsets(col_peers)
    remote = [offset for offset in offsets if offset]
    near_chunks, far_chunks = row_chunks(block_count, NEAR_CUTS), row_chunks(block_count, FAR_CUTS)
    chunks = row_chunks(block_count, NEAR_CUTS + FAR_CUTS)

    def along(value, shift):
        pairs = []
        for r in range(row_peers):
            source = r // HALVES ^ shift if peers & (peers - 1) == 0 else (r // HALVES - shift) % peers
            pairs.append((source * HALVES + r % HALVES, r))
        return lax.ppermute(value, "row", pairs)

    def across(value, flip, down):
        pairs = []
        for r in range(row_peers):
            for c in range(col_peers):
                pairs.append((r * col_peers + c, (r ^ flip) * col_peers + (c - CORES * down) % col_peers))
        return lax.ppermute(value, ("row", "col"), pairs)

    swap = [(c, c ^ 1) for c in range(col_peers)]
    other = lax.ppermute(amplitudes, "col", swap)
    other_mask = lax.ppermute(pair_mask.T, "col", swap)
    length = max(block_count, STEPS)
    plan = jnp.concatenate(
        [jnp.pad(part, ((0, 0), (0, length - part.shape[1]))) for part in (pair_mask.T, other_mask, owner.T)]
    )
    in_hbm = partial(pltpu.with_memory_space_constraint, memory_space=pltpu.HBM)

    pieces = pl.pallas_call(
        pack_kernel,
        in_specs=[VMEM, SMEM, VMEM],
        out_specs=[VMEM] * peers,
        out_shape=[jax.ShapeDtypeStruct((share + META_ROWS, tile_width), integrals.dtype)] * peers,
        compiler_params=PARAMS,
        name="pack",
    )(in_hbm(tile_list), tile_count, in_hbm(integrals))
    pieces = [piece if shift == 0 else along(piece, shift) for shift, piece in enumerate(pieces)]

    height = CORES * share + META_ROWS
    widths = []
    for offset in offsets:
        widths += [half_width] * HALVES if offset else [tile_width]
    chosen = list(
        pl.pallas_call(
            partial(choose_kernel, col_peers, offsets, peers),
            in_specs=[SMEM] + [VMEM] * peers,
            out_specs=[VMEM] * len(widths),
            out_shape=[jax.ShapeDtypeStruct((height, width), integrals.dtype) for width in widths],
            compiler_params=PARAMS,
            name="choose",
        )(plan, *pieces)
    )

    def fill(held):
        return pl.pallas_call(
            partial(fill_kernel, slots, tile_width),
            in_specs=[VMEM] * peers,
            out_specs=VMEM,
            out_shape=jax.ShapeDtypeStruct((CORES * full_width, held[0].shape[1]), integrals.dtype),
            compiler_params=PARAMS,
            name="fill",
        )(*held)

    def screen(*earlier):
        return pl.pallas_call(
            partial(screen_kernel, tile_width, block_rows),
            in_specs=[SMEM, HBM, VMEM],
            out_specs=VMEM,
            out_shape=jax.ShapeDtypeStruct((row_count, CORES * full_width), amplitudes.dtype),
            compiler_params=PARAMS,
            cost_estimate=pl.CostEstimate(
                flops=CORES * row_count * full_width,
                bytes_accessed=4 * CORES * row_count * full_width,
                transcendentals=0,
            ),
            scratch_shapes=[pltpu.SemaphoreType.DMA((SCREEN_PARTS if block_count % SCREEN_PARTS == 0 else 1,))],
            name="screen",
        )(after(plan, *earlier), in_hbm(amplitudes), other)

    own = chosen.pop(0)
    own = own + across(own, 1, 0)
    near_weights, far_weights, screened = {}, {}, None
    for offset in remote:
        near, far = chosen.pop(0), chosen.pop(0)
        data = across(near, 0, offset) + across(far, 1, offset)
        held = [data] + [along(data, shift) for shift in range(1, peers)]
        if screened is None:
            screened = screen(held[1], own)
        near_weights[offset] = fill([after(held[0], screened)] + held[1:])

    def cost(span, width):
        return pl.CostEstimate(
            flops=2 * span * block_rows * CORES * full_width * width,
            bytes_accessed=span * block_rows * (CORES * full_width + width) * 2,
            transcendentals=0,
        )

    def code_shape(span):
        return (span * block_rows + -(-2 * span // TILE_ROWS) * TILE_ROWS, half_width)

    def scratch_rows(span):
        return code_shape(span)[0] - span * block_rows

    rounds = [(half, first, span) for half, parts in enumerate((near_chunks, far_chunks)) for first, span in parts]
    arrived, sent = {}, []
    order = []
    for number, (half, first, span) in enumerate(rounds):
        ahead = 1
        earlier = sent[-1:] + [part for key in order[:-ahead] for part in arrived[key]]
        if number == len(rounds) - 2:
            earlier.append(own_weights)
        arrived[half, first] = []
        order.append((half, first))
        for offset in remote:
            weights = (near_weights, far_weights)[half][offset]
            code = pl.pallas_call(
                partial(send_kernel, first, span, block_rows),
                in_specs=[VMEM, VMEM],
                out_specs=VMEM,
                out_shape=jax.ShapeDtypeStruct(code_shape(span), jnp.int16),
                scratch_shapes=[pltpu.VMEM((scratch_rows(span), half_width), jnp.float32)],
                compiler_params=PARAMS,
                cost_estimate=cost(span, half_width),
                name="send_part",
            )(screened, after(weights, *earlier))
            arrived[half, first].append(across(code, 0, -offset))
            sent.append(code)
        if number == 1:
            for offset, code in zip(remote, sent[-len(remote) :]):
                far_weights[offset] = across(after(near_weights[offset], code), 1, 0)
        if number == 0:
            own = after(own, *arrived[half, first])
            own_weights = fill([own] + [along(own, shift) for shift in range(1, peers)])

    out = None
    for first, span in chunks:
        near_first = max(start for start, _ in near_chunks if start <= first)
        far_first = max(start for start, _ in far_chunks if start <= first)
        received = [part for pair in zip(arrived[0, near_first], arrived[1, far_first]) for part in pair]
        skips = [first - near_first, first - far_first] * len(remote)
        operands = [screened, own_weights, *received]
        specs = [VMEM] * len(operands)
        aliases = {}
        if out is not None:
            aliases = {len(operands): 0}
            operands.append(out)
            specs.append(HBM)
        out = pl.pallas_call(
            partial(join_kernel, first, span, block_rows, skips),
            in_specs=specs,
            out_specs=HBM,
            out_shape=jax.ShapeDtypeStruct((row_count, tile_width), jnp.bfloat16),
            scratch_shapes=[
                pltpu.VMEM((sum(part.shape[0] % block_rows for part in received), half_width), jnp.float32),
                pltpu.VMEM((span, block_rows, tile_width), jnp.bfloat16),
                pltpu.SemaphoreType.DMA((span,)),
            ],
            input_output_aliases=aliases,
            compiler_params=PARAMS,
            cost_estimate=cost(span, tile_width),
            name="join_part",
        )(*operands)
    return out


def solution(mesh):
    return jax.shard_map(
        shards,
        mesh=mesh,
        in_specs=(
            P("row", "col"),
            P("row", "col"),
            P("row", "col", None, None, None),
            P("row", "col", None),
            P("row", "col"),
            P(None, "col"),
        ),
        out_specs=P("row", "col"),
        check_vma=False,
    )
```

```python
from functools import partial

import jax
import jax.numpy as jnp
from jax import lax
from jax.experimental import pallas as pl
from jax.experimental.pallas import tpu as pltpu
from jax.sharding import PartitionSpec as P

STEPS = 4
CORES = 2
HALVES = 2
NEAR_CUTS = (0.0, 0.167, 0.583, 1.0)
FAR_CUTS = (0.0, 0.167, 0.583, 0.917, 1.0)
CODE_TOP = 32767.0
FRACTION = 8192.0
META_ROWS = 8
TILE_ROWS = 16
SCREEN_PARTS = 4
PARAMS = pltpu.CompilerParams(vmem_limit_bytes=16 * 1024 * 1024)
SMEM = pl.BlockSpec(memory_space=pltpu.SMEM)
VMEM = pl.BlockSpec(memory_space=pltpu.VMEM)
HBM = pl.BlockSpec(memory_space=pltpu.HBM)


def pair_offsets(col_count):
    pairs = col_count // CORES
    offsets = set()
    for core in range(CORES):
        for step in range(STEPS):
            offsets.add(-((core - step) // CORES) % pairs)
    return sorted(offsets)


def partner(place, number, peers):
    return place ^ number if peers & (peers - 1) == 0 else lax.rem(place + peers - number, peers)


def row_chunks(block_count, cuts):
    marks = sorted({round(block_count * cut) for cut in cuts})
    return [(first, last - first) for first, last in zip(marks, marks[1:])]


def pack_kernel(list_ref, count_ref, panel_ref, *piece_refs):
    peers = len(piece_refs)
    slots, tile_width = panel_ref.shape[2:4]
    share = slots * tile_width // peers
    place = lax.axis_index("row") // HALVES
    lane = lax.broadcasted_iota(jnp.int32, (META_ROWS, tile_width), 1)
    lane = lax.rem(lane, tile_width // HALVES)
    info = jnp.where(lane == slots, count_ref[0, 0], 0)
    for slot in range(slots):
        info = jnp.where(lane == slot, jnp.broadcast_to(list_ref[0, :, slot : slot + 1], lane.shape), info)
    info = info.astype(jnp.float32).astype(panel_ref.dtype)
    for shift, piece_ref in enumerate(piece_refs):
        first = partner(place, shift if peers & (peers - 1) == 0 else peers - shift, peers) * share
        start = pl.multiple_of(lax.rem(first, tile_width), TILE_ROWS)
        piece_ref[pl.ds(0, share), :] = panel_ref[0, 0, first // tile_width, pl.ds(start, share), :]
        piece_ref[pl.ds(share, META_ROWS), :] = info


def choose_kernel(col_peers, offsets, peers, plan_ref, *refs):
    piece_refs, out_refs = refs[:peers], list(refs[peers:])
    share, tile_width = piece_refs[0].shape[0] - META_ROWS, piece_refs[0].shape[1]
    half_width = tile_width // HALVES
    row = lax.axis_index("row")
    half = lax.rem(row, HALVES)
    core = lax.rem(lax.axis_index("col"), CORES)
    sign = 1 - 2 * core
    for offset in offsets:
        if offset:
            spots = [pl.multiple_of(part * half_width, half_width) for part in (half, 1 - half)]
            targets = [(out_refs.pop(0), pl.ds(spot, half_width)) for spot in spots]
        else:
            targets = [(out_refs.pop(0), pl.ds(0, tile_width))]
        for out_ref, _ in targets:
            out_ref[...] = jnp.zeros_like(out_ref)
        for group, shift in enumerate((0, sign)):
            step = lax.rem(CORES * offset - shift + col_peers, col_peers)
            holder = plan_ref[plan_ref.shape[0] - 1, jnp.minimum(step, STEPS - 1)]
            here = (step < STEPS) & (lax.rem(holder, HALVES) == half)
            for number, piece_ref in enumerate(piece_refs):

                @pl.when(here & (partner(row // HALVES, number, peers) == holder // HALVES))
                def _():
                    for out_ref, columns in targets:
                        line = lax.broadcasted_iota(jnp.int32, (META_ROWS, out_ref.shape[1]), 0)
                        out_ref[pl.ds(group * share, share), :] = piece_ref[pl.ds(0, share), columns]
                        rows = pl.ds(CORES * share, META_ROWS)
                        info = piece_ref[pl.ds(share, META_ROWS), columns]
                        out_ref[rows, :] = jnp.where(line == group, info, out_ref[rows, :])


def fill_kernel(slots, tile_width, *refs):
    piece_refs, dense_ref = refs[:-1], refs[-1]
    peers = len(piece_refs)
    share = (piece_refs[0].shape[0] - META_ROWS) // CORES
    width = dense_ref.shape[0] // CORES
    place = lax.axis_index("row") // HALVES
    table = piece_refs[0][pl.ds(CORES * share, META_ROWS), :].astype(jnp.float32)
    line = lax.broadcasted_iota(jnp.int32, table.shape, 0)
    lane = lax.broadcasted_iota(jnp.int32, table.shape, 1)

    def entry(group, spot):
        return jnp.max(jnp.where((line == group) & (lane == spot), table, 0.0)).astype(jnp.int32)

    dense_ref[...] = jnp.zeros_like(dense_ref)
    for group in range(CORES):
        count = entry(group, slots)
        starts = [group * width + entry(group, slot) * tile_width for slot in range(slots)]
        for shift, piece_ref in enumerate(piece_refs):
            first = partner(place, shift, peers) * share
            slot = first // tile_width
            start = starts[0]
            for other in range(1, slots):
                start = jnp.where(slot == other, starts[other], start)

            @pl.when(slot < count)
            def _():
                spot = pl.multiple_of(start + lax.rem(first, tile_width), TILE_ROWS)
                dense_ref[pl.ds(spot, share), :] = piece_ref[pl.ds(group * share, share), :]


def screen_kernel(tile_width, block_rows, mask_ref, own_ref, other_ref, out_ref, sems):
    full_width = own_ref.shape[1]
    tiles = full_width // tile_width
    parts = sems.shape[0]
    blocks = own_ref.shape[0] // block_rows // parts
    copies = []
    for part in range(parts):
        lines = pl.ds(part * blocks * block_rows, blocks * block_rows)
        copies.append(
            pltpu.make_async_copy(own_ref.at[lines, :], out_ref.at[lines, pl.ds(0, full_width)], sems.at[part])
        )
        copies[-1].start()

    def screen(source_ref, group, block):
        lines = pl.ds(pl.multiple_of(block * block_rows, block_rows), block_rows)
        for tile in range(tiles):
            live = mask_ref[group * tiles + tile, block].astype(jnp.float32).astype(out_ref.dtype)
            part = source_ref[lines, pl.ds(tile * tile_width, tile_width)]
            out_ref[lines, pl.ds((group * tiles + tile) * tile_width, tile_width)] = part * live

    @pl.loop(0, parts * blocks)
    def _(block):
        screen(other_ref, 1, block)

    for part in range(parts):
        copies[part].wait()

        @pl.loop(part * blocks, (part + 1) * blocks)
        def _(block):
            screen(out_ref, 0, block)


def send_kernel(first, span, height, rows_ref, dense_ref, code_ref, scale_ref):
    scale_ref[...] = jnp.zeros_like(scale_ref)
    sums = jnp.dot(rows_ref[pl.ds(first * height, span * height), :], dense_ref[...], preferred_element_type=jnp.float32)
    for step in range(span):
        total = sums[step * height : (step + 1) * height]
        top = jnp.max(jnp.abs(total), axis=0, keepdims=True)
        unit = jnp.where(top > 0, top, 1.0) * (1.0 / CODE_TOP)
        power = jnp.floor(jnp.log2(unit))
        fraction = jnp.ceil(unit * jnp.exp2(-power) * FRACTION)
        unit = fraction * jnp.exp2(power) * (1.0 / FRACTION)
        code = jnp.clip(jnp.round(total * (1.0 / unit)), -CODE_TOP, CODE_TOP)
        code_ref[pl.ds(step * height, height), :] = code.astype(jnp.int32).astype(jnp.int16)
        scale_ref[pl.ds(2 * step, 1), :] = power
        scale_ref[pl.ds(2 * step + 1, 1), :] = fraction
    tail = scale_ref.shape[0]
    code_ref[pl.ds(code_ref.shape[0] - tail, tail), :] = scale_ref[...].astype(jnp.int32).astype(jnp.int16)


def join_kernel(first, span, height, skips, rows_ref, dense_ref, *refs):
    code_refs, (out_ref, scale_ref, done_ref, sems) = refs[: len(skips)], refs[-4:]
    tails = [code_ref.shape[0] % height for code_ref in code_refs]
    starts = [sum(tails[:number]) for number in range(len(tails))]
    first_half = lax.rem(lax.axis_index("row"), HALVES) == 0
    for code_ref, start, tail in zip(code_refs, starts, tails):
        scales = code_ref[pl.ds(code_ref.shape[0] - tail, tail), :].astype(jnp.int32).astype(jnp.float32)
        scale_ref[pl.ds(start, tail), :] = scales

    def decoded(number, step):
        block = skips[number] + step
        power = scale_ref[pl.ds(starts[number] + 2 * block, 1), :]
        fraction = scale_ref[pl.ds(starts[number] + 2 * block + 1, 1), :]
        code = code_refs[number][pl.ds(block * height, height), :]
        return code.astype(jnp.int32).astype(jnp.float32) * (fraction * jnp.exp2(power) * (1.0 / FRACTION))

    sums = jnp.dot(rows_ref[pl.ds(first * height, span * height), :], dense_ref[...], preferred_element_type=jnp.float32)
    copies = []
    for step in range(span):
        total = sums[step * height : (step + 1) * height]
        for number in range(0, len(code_refs), HALVES):
            near, far = decoded(number, step), decoded(number + 1, step)
            left = jnp.where(first_half, near, far)
            right = jnp.where(first_half, far, near)
            total = total + jnp.concatenate([left, right], axis=1)
        done_ref[step] = total.astype(done_ref.dtype)
        lines = pl.ds((first + step) * height, height)
        copies.append(pltpu.make_async_copy(done_ref.at[step], out_ref.at[lines, :], sems.at[step]))
        copies[-1].start()
    for copy in copies:
        copy.wait()


def after(value, *earlier):
    return lax.optimization_barrier((value, *earlier))[0]


def shards(amplitudes, pair_mask, integrals, tile_list, tile_count, owner):
    row_count, full_width = amplitudes.shape
    slots, tile_width = integrals.shape[2], integrals.shape[-1]
    half_width = tile_width // HALVES
    block_count = pair_mask.shape[0]
    block_rows = row_count // block_count
    row_peers, col_peers = lax.axis_size("row"), lax.axis_size("col")
    peers = row_peers // HALVES
    share = slots * tile_width // peers
    offsets = pair_offsets(col_peers)
    remote = [offset for offset in offsets if offset]
    near_chunks, far_chunks = row_chunks(block_count, NEAR_CUTS), row_chunks(block_count, FAR_CUTS)
    chunks = row_chunks(block_count, NEAR_CUTS + FAR_CUTS)

    def along(value, shift):
        pairs = []
        for r in range(row_peers):
            source = r // HALVES ^ shift if peers & (peers - 1) == 0 else (r // HALVES - shift) % peers
            pairs.append((source * HALVES + r % HALVES, r))
        return lax.ppermute(value, "row", pairs)

    def across(value, flip, down):
        pairs = []
        for r in range(row_peers):
            for c in range(col_peers):
                pairs.append((r * col_peers + c, (r ^ flip) * col_peers + (c - CORES * down) % col_peers))
        return lax.ppermute(value, ("row", "col"), pairs)

    swap = [(c, c ^ 1) for c in range(col_peers)]
    other = lax.ppermute(amplitudes, "col", swap)
    other_mask = lax.ppermute(pair_mask.T, "col", swap)
    length = max(block_count, STEPS)
    plan = jnp.concatenate(
        [jnp.pad(part, ((0, 0), (0, length - part.shape[1]))) for part in (pair_mask.T, other_mask, owner.T)]
    )
    in_hbm = partial(pltpu.with_memory_space_constraint, memory_space=pltpu.HBM)

    pieces = pl.pallas_call(
        pack_kernel,
        in_specs=[VMEM, SMEM, VMEM],
        out_specs=[VMEM] * peers,
        out_shape=[jax.ShapeDtypeStruct((share + META_ROWS, tile_width), integrals.dtype)] * peers,
        compiler_params=PARAMS,
        name="pack",
    )(in_hbm(tile_list), tile_count, in_hbm(integrals))
    pieces = [piece if shift == 0 else along(piece, shift) for shift, piece in enumerate(pieces)]

    height = CORES * share + META_ROWS
    widths = []
    for offset in offsets:
        widths += [half_width] * HALVES if offset else [tile_width]
    chosen = list(
        pl.pallas_call(
            partial(choose_kernel, col_peers, offsets, peers),
            in_specs=[SMEM] + [VMEM] * peers,
            out_specs=[VMEM] * len(widths),
            out_shape=[jax.ShapeDtypeStruct((height, width), integrals.dtype) for width in widths],
            compiler_params=PARAMS,
            name="choose",
        )(plan, *pieces)
    )

    def fill(held):
        return pl.pallas_call(
            partial(fill_kernel, slots, tile_width),
            in_specs=[VMEM] * peers,
            out_specs=VMEM,
            out_shape=jax.ShapeDtypeStruct((CORES * full_width, held[0].shape[1]), integrals.dtype),
            compiler_params=PARAMS,
            name="fill",
        )(*held)

    def screen(*earlier):
        return pl.pallas_call(
            partial(screen_kernel, tile_width, block_rows),
            in_specs=[SMEM, HBM, VMEM],
            out_specs=VMEM,
            out_shape=jax.ShapeDtypeStruct((row_count, CORES * full_width), amplitudes.dtype),
            compiler_params=PARAMS,
            cost_estimate=pl.CostEstimate(
                flops=CORES * row_count * full_width,
                bytes_accessed=4 * CORES * row_count * full_width,
                transcendentals=0,
            ),
            scratch_shapes=[pltpu.SemaphoreType.DMA((SCREEN_PARTS if block_count % SCREEN_PARTS == 0 else 1,))],
            name="screen",
        )(after(plan, *earlier), in_hbm(amplitudes), other)

    own = chosen.pop(0)
    own = own + across(own, 1, 0)
    near_weights, far_weights, screened = {}, {}, None
    for offset in remote:
        near, far = chosen.pop(0), chosen.pop(0)
        data = across(near, 0, offset) + across(far, 1, offset)
        held = [data] + [along(data, shift) for shift in range(1, peers)]
        if screened is None:
            screened = screen(held[1], own)
        near_weights[offset] = fill([after(held[0], screened)] + held[1:])
        far_weights[offset] = across(near_weights[offset], 1, 0)

    def cost(span, width):
        return pl.CostEstimate(
            flops=2 * span * block_rows * CORES * full_width * width,
            bytes_accessed=span * block_rows * (CORES * full_width + width) * 2,
            transcendentals=0,
        )

    def code_shape(span):
        return (span * block_rows + -(-2 * span // TILE_ROWS) * TILE_ROWS, half_width)

    def scratch_rows(span):
        return code_shape(span)[0] - span * block_rows

    rounds = [(half, first, span) for half, parts in enumerate((near_chunks, far_chunks)) for first, span in parts]
    arrived, sent = {}, []
    order = []
    for number, (half, first, span) in enumerate(rounds):
        ahead = 2 if number in (3, 4) else 1
        earlier = sent[-1:] + [part for key in order[:-ahead] for part in arrived[key]]
        if number == len(near_chunks) - 1:
            earlier += list(far_weights.values())
        if number == len(rounds) - 2:
            earlier.append(own_weights)
        arrived[half, first] = []
        order.append((half, first))
        for offset in remote:
            weights = (near_weights, far_weights)[half][offset]
            code = pl.pallas_call(
                partial(send_kernel, first, span, block_rows),
                in_specs=[VMEM, VMEM],
                out_specs=VMEM,
                out_shape=jax.ShapeDtypeStruct(code_shape(span), jnp.int16),
                scratch_shapes=[pltpu.VMEM((scratch_rows(span), half_width), jnp.float32)],
                compiler_params=PARAMS,
                cost_estimate=cost(span, half_width),
                name="send_part",
            )(screened, after(weights, *earlier))
            arrived[half, first].append(across(code, 0, -offset))
            sent.append(code)
        if number == 0:
            own = after(own, *arrived[half, first])
            own_weights = fill([own] + [along(own, shift) for shift in range(1, peers)])

    out = None
    for first, span in chunks:
        near_first = max(start for start, _ in near_chunks if start <= first)
        far_first = max(start for start, _ in far_chunks if start <= first)
        received = [part for pair in zip(arrived[0, near_first], arrived[1, far_first]) for part in pair]
        skips = [first - near_first, first - far_first] * len(remote)
        operands = [screened, own_weights, *received]
        specs = [VMEM] * len(operands)
        aliases = {}
        if out is not None:
            aliases = {len(operands): 0}
            operands.append(out)
            specs.append(HBM)
        out = pl.pallas_call(
            partial(join_kernel, first, span, block_rows, skips),
            in_specs=specs,
            out_specs=HBM,
            out_shape=jax.ShapeDtypeStruct((row_count, tile_width), jnp.bfloat16),
            scratch_shapes=[
                pltpu.VMEM((sum(part.shape[0] % block_rows for part in received), half_width), jnp.float32),
                pltpu.VMEM((span, block_rows, tile_width), jnp.bfloat16),
                pltpu.SemaphoreType.DMA((span,)),
            ],
            input_output_aliases=aliases,
            compiler_params=PARAMS,
            cost_estimate=cost(span, tile_width),
            name="join_part",
        )(*operands)
    return out


def solution(mesh):
    return jax.shard_map(
        shards,
        mesh=mesh,
        in_specs=(
            P("row", "col"),
            P("row", "col"),
            P("row", "col", None, None, None),
            P("row", "col", None),
            P("row", "col"),
            P(None, "col"),
        ),
        out_specs=P("row", "col"),
        check_vma=False,
    )
```

```python
from functools import partial

import jax
import jax.numpy as jnp
from jax import lax
from jax.experimental import pallas as pl
from jax.experimental.pallas import tpu as pltpu
from jax.sharding import PartitionSpec as P

STEPS = 4
CORES = 2
HALVES = 2
NEAR_CUTS = (0.0, 0.25, 0.583, 1.0)
FAR_CUTS = (0.0, 0.25, 0.583, 0.917, 1.0)
CODE_TOP = 32767.0
FRACTION = 8192.0
META_ROWS = 8
TILE_ROWS = 16
SCREEN_PARTS = 4
PARAMS = pltpu.CompilerParams(vmem_limit_bytes=16 * 1024 * 1024)
SMEM = pl.BlockSpec(memory_space=pltpu.SMEM)
VMEM = pl.BlockSpec(memory_space=pltpu.VMEM)
HBM = pl.BlockSpec(memory_space=pltpu.HBM)


def pair_offsets(col_count):
    pairs = col_count // CORES
    offsets = set()
    for core in range(CORES):
        for step in range(STEPS):
            offsets.add(-((core - step) // CORES) % pairs)
    return sorted(offsets)


def partner(place, number, peers):
    return place ^ number if peers & (peers - 1) == 0 else lax.rem(place + peers - number, peers)


def row_chunks(block_count, cuts):
    marks = sorted({round(block_count * cut) for cut in cuts})
    return [(first, last - first) for first, last in zip(marks, marks[1:])]


def pack_kernel(list_ref, count_ref, panel_ref, *piece_refs):
    peers = len(piece_refs)
    slots, tile_width = panel_ref.shape[2:4]
    share = slots * tile_width // peers
    place = lax.axis_index("row") // HALVES
    lane = lax.broadcasted_iota(jnp.int32, (META_ROWS, tile_width), 1)
    lane = lax.rem(lane, tile_width // HALVES)
    info = jnp.where(lane == slots, count_ref[0, 0], 0)
    for slot in range(slots):
        info = jnp.where(lane == slot, jnp.broadcast_to(list_ref[0, :, slot : slot + 1], lane.shape), info)
    info = info.astype(jnp.float32).astype(panel_ref.dtype)
    for shift, piece_ref in enumerate(piece_refs):
        first = partner(place, shift if peers & (peers - 1) == 0 else peers - shift, peers) * share
        start = pl.multiple_of(lax.rem(first, tile_width), TILE_ROWS)
        piece_ref[pl.ds(0, share), :] = panel_ref[0, 0, first // tile_width, pl.ds(start, share), :]
        piece_ref[pl.ds(share, META_ROWS), :] = info


def choose_kernel(col_peers, offsets, peers, plan_ref, *refs):
    piece_refs, out_refs = refs[:peers], list(refs[peers:])
    share, tile_width = piece_refs[0].shape[0] - META_ROWS, piece_refs[0].shape[1]
    half_width = tile_width // HALVES
    row = lax.axis_index("row")
    half = lax.rem(row, HALVES)
    core = lax.rem(lax.axis_index("col"), CORES)
    sign = 1 - 2 * core
    for offset in offsets:
        if offset:
            spots = [pl.multiple_of(part * half_width, half_width) for part in (half, 1 - half)]
            targets = [(out_refs.pop(0), pl.ds(spot, half_width)) for spot in spots]
        else:
            targets = [(out_refs.pop(0), pl.ds(0, tile_width))]
        for out_ref, _ in targets:
            out_ref[...] = jnp.zeros_like(out_ref)
        for group, shift in enumerate((0, sign)):
            step = lax.rem(CORES * offset - shift + col_peers, col_peers)
            holder = plan_ref[plan_ref.shape[0] - 1, jnp.minimum(step, STEPS - 1)]
            here = (step < STEPS) & (lax.rem(holder, HALVES) == half)
            for number, piece_ref in enumerate(piece_refs):

                @pl.when(here & (partner(row // HALVES, number, peers) == holder // HALVES))
                def _():
                    for out_ref, columns in targets:
                        line = lax.broadcasted_iota(jnp.int32, (META_ROWS, out_ref.shape[1]), 0)
                        out_ref[pl.ds(group * share, share), :] = piece_ref[pl.ds(0, share), columns]
                        rows = pl.ds(CORES * share, META_ROWS)
                        info = piece_ref[pl.ds(share, META_ROWS), columns]
                        out_ref[rows, :] = jnp.where(line == group, info, out_ref[rows, :])


def fill_kernel(slots, tile_width, *refs):
    piece_refs, dense_ref = refs[:-1], refs[-1]
    peers = len(piece_refs)
    share = (piece_refs[0].shape[0] - META_ROWS) // CORES
    width = dense_ref.shape[0] // CORES
    place = lax.axis_index("row") // HALVES
    table = piece_refs[0][pl.ds(CORES * share, META_ROWS), :].astype(jnp.float32)
    line = lax.broadcasted_iota(jnp.int32, table.shape, 0)
    lane = lax.broadcasted_iota(jnp.int32, table.shape, 1)

    def entry(group, spot):
        return jnp.max(jnp.where((line == group) & (lane == spot), table, 0.0)).astype(jnp.int32)

    dense_ref[...] = jnp.zeros_like(dense_ref)
    for group in range(CORES):
        count = entry(group, slots)
        starts = [group * width + entry(group, slot) * tile_width for slot in range(slots)]
        for shift, piece_ref in enumerate(piece_refs):
            first = partner(place, shift, peers) * share
            slot = first // tile_width
            start = starts[0]
            for other in range(1, slots):
                start = jnp.where(slot == other, starts[other], start)

            @pl.when(slot < count)
            def _():
                spot = pl.multiple_of(start + lax.rem(first, tile_width), TILE_ROWS)
                dense_ref[pl.ds(spot, share), :] = piece_ref[pl.ds(group * share, share), :]


def screen_kernel(tile_width, block_rows, mask_ref, own_ref, other_ref, out_ref, sems):
    full_width = own_ref.shape[1]
    tiles = full_width // tile_width
    parts = sems.shape[0]
    blocks = own_ref.shape[0] // block_rows // parts
    copies = []
    for part in range(parts):
        lines = pl.ds(part * blocks * block_rows, blocks * block_rows)
        copies.append(
            pltpu.make_async_copy(own_ref.at[lines, :], out_ref.at[lines, pl.ds(0, full_width)], sems.at[part])
        )
        copies[-1].start()

    def screen(source_ref, group, block):
        lines = pl.ds(pl.multiple_of(block * block_rows, block_rows), block_rows)
        for tile in range(tiles):
            live = mask_ref[group * tiles + tile, block].astype(jnp.float32).astype(out_ref.dtype)
            part = source_ref[lines, pl.ds(tile * tile_width, tile_width)]
            out_ref[lines, pl.ds((group * tiles + tile) * tile_width, tile_width)] = part * live

    @pl.loop(0, parts * blocks)
    def _(block):
        screen(other_ref, 1, block)

    for part in range(parts):
        copies[part].wait()

        @pl.loop(part * blocks, (part + 1) * blocks)
        def _(block):
            screen(out_ref, 0, block)


def send_kernel(first, span, height, rows_ref, dense_ref, code_ref, scale_ref):
    scale_ref[...] = jnp.zeros_like(scale_ref)
    sums = jnp.dot(rows_ref[pl.ds(first * height, span * height), :], dense_ref[...], preferred_element_type=jnp.float32)
    for step in range(span):
        total = sums[step * height : (step + 1) * height]
        top = jnp.max(jnp.abs(total), axis=0, keepdims=True)
        unit = jnp.where(top > 0, top, 1.0) * (1.0 / CODE_TOP)
        power = jnp.floor(jnp.log2(unit))
        fraction = jnp.ceil(unit * jnp.exp2(-power) * FRACTION)
        unit = fraction * jnp.exp2(power) * (1.0 / FRACTION)
        code = jnp.clip(jnp.round(total * (1.0 / unit)), -CODE_TOP, CODE_TOP)
        code_ref[pl.ds(step * height, height), :] = code.astype(jnp.int32).astype(jnp.int16)
        scale_ref[pl.ds(2 * step, 1), :] = power
        scale_ref[pl.ds(2 * step + 1, 1), :] = fraction
    tail = scale_ref.shape[0]
    code_ref[pl.ds(code_ref.shape[0] - tail, tail), :] = scale_ref[...].astype(jnp.int32).astype(jnp.int16)


def join_kernel(first, span, height, skips, rows_ref, dense_ref, *refs):
    code_refs, (out_ref, scale_ref, done_ref, sems) = refs[: len(skips)], refs[-4:]
    tails = [code_ref.shape[0] % height for code_ref in code_refs]
    starts = [sum(tails[:number]) for number in range(len(tails))]
    first_half = lax.rem(lax.axis_index("row"), HALVES) == 0
    for code_ref, start, tail in zip(code_refs, starts, tails):
        scales = code_ref[pl.ds(code_ref.shape[0] - tail, tail), :].astype(jnp.int32).astype(jnp.float32)
        scale_ref[pl.ds(start, tail), :] = scales

    def decoded(number, step):
        block = skips[number] + step
        power = scale_ref[pl.ds(starts[number] + 2 * block, 1), :]
        fraction = scale_ref[pl.ds(starts[number] + 2 * block + 1, 1), :]
        code = code_refs[number][pl.ds(block * height, height), :]
        return code.astype(jnp.int32).astype(jnp.float32) * (fraction * jnp.exp2(power) * (1.0 / FRACTION))

    sums = jnp.dot(rows_ref[pl.ds(first * height, span * height), :], dense_ref[...], preferred_element_type=jnp.float32)
    copies = []
    for step in range(span):
        total = sums[step * height : (step + 1) * height]
        for number in range(0, len(code_refs), HALVES):
            near, far = decoded(number, step), decoded(number + 1, step)
            left = jnp.where(first_half, near, far)
            right = jnp.where(first_half, far, near)
            total = total + jnp.concatenate([left, right], axis=1)
        done_ref[step] = total.astype(done_ref.dtype)
        lines = pl.ds((first + step) * height, height)
        copies.append(pltpu.make_async_copy(done_ref.at[step], out_ref.at[lines, :], sems.at[step]))
        copies[-1].start()
    for copy in copies:
        copy.wait()


def after(value, *earlier):
    return lax.optimization_barrier((value, *earlier))[0]


def shards(amplitudes, pair_mask, integrals, tile_list, tile_count, owner):
    row_count, full_width = amplitudes.shape
    slots, tile_width = integrals.shape[2], integrals.shape[-1]
    half_width = tile_width // HALVES
    block_count = pair_mask.shape[0]
    block_rows = row_count // block_count
    row_peers, col_peers = lax.axis_size("row"), lax.axis_size("col")
    peers = row_peers // HALVES
    share = slots * tile_width // peers
    offsets = pair_offsets(col_peers)
    remote = [offset for offset in offsets if offset]
    near_chunks, far_chunks = row_chunks(block_count, NEAR_CUTS), row_chunks(block_count, FAR_CUTS)
    chunks = row_chunks(block_count, NEAR_CUTS + FAR_CUTS)

    def along(value, shift):
        pairs = []
        for r in range(row_peers):
            source = r // HALVES ^ shift if peers & (peers - 1) == 0 else (r // HALVES - shift) % peers
            pairs.append((source * HALVES + r % HALVES, r))
        return lax.ppermute(value, "row", pairs)

    def across(value, flip, down):
        pairs = []
        for r in range(row_peers):
            for c in range(col_peers):
                pairs.append((r * col_peers + c, (r ^ flip) * col_peers + (c - CORES * down) % col_peers))
        return lax.ppermute(value, ("row", "col"), pairs)

    swap = [(c, c ^ 1) for c in range(col_peers)]
    other = lax.ppermute(amplitudes, "col", swap)
    other_mask = lax.ppermute(pair_mask.T, "col", swap)
    length = max(block_count, STEPS)
    plan = jnp.concatenate(
        [jnp.pad(part, ((0, 0), (0, length - part.shape[1]))) for part in (pair_mask.T, other_mask, owner.T)]
    )
    in_hbm = partial(pltpu.with_memory_space_constraint, memory_space=pltpu.HBM)

    pieces = pl.pallas_call(
        pack_kernel,
        in_specs=[VMEM, SMEM, VMEM],
        out_specs=[VMEM] * peers,
        out_shape=[jax.ShapeDtypeStruct((share + META_ROWS, tile_width), integrals.dtype)] * peers,
        compiler_params=PARAMS,
        name="pack",
    )(in_hbm(tile_list), tile_count, in_hbm(integrals))
    pieces = [piece if shift == 0 else along(piece, shift) for shift, piece in enumerate(pieces)]

    height = CORES * share + META_ROWS
    widths = []
    for offset in offsets:
        widths += [half_width] * HALVES if offset else [tile_width]
    chosen = list(
        pl.pallas_call(
            partial(choose_kernel, col_peers, offsets, peers),
            in_specs=[SMEM] + [VMEM] * peers,
            out_specs=[VMEM] * len(widths),
            out_shape=[jax.ShapeDtypeStruct((height, width), integrals.dtype) for width in widths],
            compiler_params=PARAMS,
            name="choose",
        )(plan, *pieces)
    )

    def fill(held):
        return pl.pallas_call(
            partial(fill_kernel, slots, tile_width),
            in_specs=[VMEM] * peers,
            out_specs=VMEM,
            out_shape=jax.ShapeDtypeStruct((CORES * full_width, held[0].shape[1]), integrals.dtype),
            compiler_params=PARAMS,
            name="fill",
        )(*held)

    def screen(*earlier):
        return pl.pallas_call(
            partial(screen_kernel, tile_width, block_rows),
            in_specs=[SMEM, HBM, VMEM],
            out_specs=VMEM,
            out_shape=jax.ShapeDtypeStruct((row_count, CORES * full_width), amplitudes.dtype),
            compiler_params=PARAMS,
            cost_estimate=pl.CostEstimate(
                flops=CORES * row_count * full_width,
                bytes_accessed=4 * CORES * row_count * full_width,
                transcendentals=0,
            ),
            scratch_shapes=[pltpu.SemaphoreType.DMA((SCREEN_PARTS if block_count % SCREEN_PARTS == 0 else 1,))],
            name="screen",
        )(after(plan, *earlier), in_hbm(amplitudes), other)

    own = chosen.pop(0)
    own = own + across(own, 1, 0)
    near_weights, far_weights, screened = {}, {}, None
    for offset in remote:
        near, far = chosen.pop(0), chosen.pop(0)
        data = across(near, 0, offset) + across(far, 1, offset)
        held = [data] + [along(data, shift) for shift in range(1, peers)]
        if screened is None:
            screened = screen(held[1], own)
        near_weights[offset] = fill([after(held[0], screened)] + held[1:])

    def cost(span, width):
        return pl.CostEstimate(
            flops=2 * span * block_rows * CORES * full_width * width,
            bytes_accessed=span * block_rows * (CORES * full_width + width) * 2,
            transcendentals=0,
        )

    def code_shape(span):
        return (span * block_rows + -(-2 * span // TILE_ROWS) * TILE_ROWS, half_width)

    def scratch_rows(span):
        return code_shape(span)[0] - span * block_rows

    rounds = [(half, first, span) for half, parts in enumerate((near_chunks, far_chunks)) for first, span in parts]
    arrived, sent = {}, []
    order = []
    for number, (half, first, span) in enumerate(rounds):
        ahead = 2 if number in (4, 5) else 1
        earlier = sent[-1:] + [part for key in order[:-ahead] for part in arrived[key]]
        if number == len(rounds) - 2:
            earlier.append(own_weights)
        arrived[half, first] = []
        order.append((half, first))
        for offset in remote:
            weights = (near_weights, far_weights)[half][offset]
            code = pl.pallas_call(
                partial(send_kernel, first, span, block_rows),
                in_specs=[VMEM, VMEM],
                out_specs=VMEM,
                out_shape=jax.ShapeDtypeStruct(code_shape(span), jnp.int16),
                scratch_shapes=[pltpu.VMEM((scratch_rows(span), half_width), jnp.float32)],
                compiler_params=PARAMS,
                cost_estimate=cost(span, half_width),
                name="send_part",
            )(screened, after(weights, *earlier))
            arrived[half, first].append(across(code, 0, -offset))
            sent.append(code)
        if number == 1:
            for offset, code in zip(remote, sent[-len(remote) :]):
                far_weights[offset] = across(after(near_weights[offset], code), 1, 0)
        if number == 0:
            own = after(own, *arrived[half, first])
            own_weights = fill([own] + [along(own, shift) for shift in range(1, peers)])

    out = None
    for first, span in chunks:
        near_first = max(start for start, _ in near_chunks if start <= first)
        far_first = max(start for start, _ in far_chunks if start <= first)
        received = [part for pair in zip(arrived[0, near_first], arrived[1, far_first]) for part in pair]
        skips = [first - near_first, first - far_first] * len(remote)
        operands = [screened, own_weights, *received]
        specs = [VMEM] * len(operands)
        aliases = {}
        if out is not None:
            aliases = {len(operands): 0}
            operands.append(out)
            specs.append(HBM)
        out = pl.pallas_call(
            partial(join_kernel, first, span, block_rows, skips),
            in_specs=specs,
            out_specs=HBM,
            out_shape=jax.ShapeDtypeStruct((row_count, tile_width), jnp.bfloat16),
            scratch_shapes=[
                pltpu.VMEM((sum(part.shape[0] % block_rows for part in received), half_width), jnp.float32),
                pltpu.VMEM((span, block_rows, tile_width), jnp.bfloat16),
                pltpu.SemaphoreType.DMA((span,)),
            ],
            input_output_aliases=aliases,
            compiler_params=PARAMS,
            cost_estimate=cost(span, tile_width),
            name="join_part",
        )(*operands)
    return out


def solution(mesh):
    return jax.shard_map(
        shards,
        mesh=mesh,
        in_specs=(
            P("row", "col"),
            P("row", "col"),
            P("row", "col", None, None, None),
            P("row", "col", None),
            P("row", "col"),
            P(None, "col"),
        ),
        out_specs=P("row", "col"),
        check_vma=False,
    )
```

```python
from functools import partial

import jax
import jax.numpy as jnp
from jax import lax
from jax.experimental import pallas as pl
from jax.experimental.pallas import tpu as pltpu
from jax.sharding import PartitionSpec as P

STEPS = 4
CORES = 2
HALVES = 2
NEAR_CUTS = (0.0, 0.167, 0.583, 1.0)
FAR_CUTS = (0.0, 0.167, 0.583, 0.917, 1.0)
CODE_TOP = 32767.0
FRACTION = 8192.0
SMALLEST_UNIT = 2.0**-100
META_ROWS = 8
TILE_ROWS = 16
SCREEN_PARTS = 4
PARAMS = pltpu.CompilerParams(vmem_limit_bytes=16 * 1024 * 1024)
SMEM = pl.BlockSpec(memory_space=pltpu.SMEM)
VMEM = pl.BlockSpec(memory_space=pltpu.VMEM)
HBM = pl.BlockSpec(memory_space=pltpu.HBM)


def pair_offsets(col_count):
    pairs = col_count // CORES
    offsets = set()
    for core in range(CORES):
        for step in range(STEPS):
            offsets.add(-((core - step) // CORES) % pairs)
    return sorted(offsets)


def partner(place, number, peers):
    return place ^ number if peers & (peers - 1) == 0 else lax.rem(place + peers - number, peers)


def row_chunks(block_count, cuts):
    marks = sorted({round(block_count * cut) for cut in cuts})
    return [(first, last - first) for first, last in zip(marks, marks[1:])]


def pack_kernel(list_ref, count_ref, panel_ref, *piece_refs):
    peers = len(piece_refs)
    slots, tile_width = panel_ref.shape[2:4]
    share = slots * tile_width // peers
    place = lax.axis_index("row") // HALVES
    lane = lax.broadcasted_iota(jnp.int32, (META_ROWS, tile_width), 1)
    lane = lax.rem(lane, tile_width // HALVES)
    info = jnp.where(lane == slots, count_ref[0, 0], 0)
    for slot in range(slots):
        info = jnp.where(lane == slot, jnp.broadcast_to(list_ref[0, :, slot : slot + 1], lane.shape), info)
    info = info.astype(jnp.float32).astype(panel_ref.dtype)
    for shift, piece_ref in enumerate(piece_refs):
        first = partner(place, shift if peers & (peers - 1) == 0 else peers - shift, peers) * share
        start = pl.multiple_of(lax.rem(first, tile_width), TILE_ROWS)
        piece_ref[pl.ds(0, share), :] = panel_ref[0, 0, first // tile_width, pl.ds(start, share), :]
        piece_ref[pl.ds(share, META_ROWS), :] = info


def choose_kernel(col_peers, offsets, peers, plan_ref, *refs):
    piece_refs, out_refs = refs[:peers], list(refs[peers:])
    share, tile_width = piece_refs[0].shape[0] - META_ROWS, piece_refs[0].shape[1]
    half_width = tile_width // HALVES
    row = lax.axis_index("row")
    half = lax.rem(row, HALVES)
    core = lax.rem(lax.axis_index("col"), CORES)
    sign = 1 - 2 * core
    for offset in offsets:
        if offset:
            spots = [pl.multiple_of(part * half_width, half_width) for part in (half, 1 - half)]
            targets = [(out_refs.pop(0), pl.ds(spot, half_width)) for spot in spots]
        else:
            targets = [(out_refs.pop(0), pl.ds(0, tile_width))]
        for out_ref, _ in targets:
            out_ref[...] = jnp.zeros_like(out_ref)
        for group, shift in enumerate((0, sign)):
            step = lax.rem(CORES * offset - shift + col_peers, col_peers)
            holder = plan_ref[plan_ref.shape[0] - 1, jnp.minimum(step, STEPS - 1)]
            here = (step < STEPS) & (lax.rem(holder, HALVES) == half)
            for number, piece_ref in enumerate(piece_refs):

                @pl.when(here & (partner(row // HALVES, number, peers) == holder // HALVES))
                def _():
                    for out_ref, columns in targets:
                        line = lax.broadcasted_iota(jnp.int32, (META_ROWS, out_ref.shape[1]), 0)
                        out_ref[pl.ds(group * share, share), :] = piece_ref[pl.ds(0, share), columns]
                        rows = pl.ds(CORES * share, META_ROWS)
                        info = piece_ref[pl.ds(share, META_ROWS), columns]
                        out_ref[rows, :] = jnp.where(line == group, info, out_ref[rows, :])


def fill_kernel(slots, tile_width, *refs):
    piece_refs, dense_ref = refs[:-1], refs[-1]
    peers = len(piece_refs)
    share = (piece_refs[0].shape[0] - META_ROWS) // CORES
    width = dense_ref.shape[0] // CORES
    place = lax.axis_index("row") // HALVES
    table = piece_refs[0][pl.ds(CORES * share, META_ROWS), :].astype(jnp.float32)
    line = lax.broadcasted_iota(jnp.int32, table.shape, 0)
    lane = lax.broadcasted_iota(jnp.int32, table.shape, 1)

    def entry(group, spot):
        return jnp.max(jnp.where((line == group) & (lane == spot), table, 0.0)).astype(jnp.int32)

    dense_ref[...] = jnp.zeros_like(dense_ref)
    for group in range(CORES):
        count = entry(group, slots)
        starts = [group * width + entry(group, slot) * tile_width for slot in range(slots)]
        for shift, piece_ref in enumerate(piece_refs):
            first = partner(place, shift, peers) * share
            slot = first // tile_width
            start = starts[0]
            for other in range(1, slots):
                start = jnp.where(slot == other, starts[other], start)

            @pl.when(slot < count)
            def _():
                spot = pl.multiple_of(start + lax.rem(first, tile_width), TILE_ROWS)
                dense_ref[pl.ds(spot, share), :] = piece_ref[pl.ds(group * share, share), :]


def screen_kernel(tile_width, block_rows, mask_ref, own_ref, other_ref, out_ref, sems):
    full_width = own_ref.shape[1]
    tiles = full_width // tile_width
    parts = sems.shape[0]
    blocks = own_ref.shape[0] // block_rows // parts
    copies = []
    for part in range(parts):
        lines = pl.ds(part * blocks * block_rows, blocks * block_rows)
        copies.append(
            pltpu.make_async_copy(own_ref.at[lines, :], out_ref.at[lines, pl.ds(0, full_width)], sems.at[part])
        )
        copies[-1].start()

    def screen(source_ref, group, block):
        lines = pl.ds(pl.multiple_of(block * block_rows, block_rows), block_rows)
        for tile in range(tiles):
            live = mask_ref[group * tiles + tile, block].astype(jnp.float32).astype(out_ref.dtype)
            part = source_ref[lines, pl.ds(tile * tile_width, tile_width)]
            out_ref[lines, pl.ds((group * tiles + tile) * tile_width, tile_width)] = part * live

    @pl.loop(0, parts * blocks)
    def _(block):
        screen(other_ref, 1, block)

    for part in range(parts):
        copies[part].wait()

        @pl.loop(part * blocks, (part + 1) * blocks)
        def _(block):
            screen(out_ref, 0, block)


def send_kernel(first, span, height, rows_ref, dense_ref, code_ref, scale_ref):
    scale_ref[...] = jnp.zeros_like(scale_ref)
    sums = jnp.dot(rows_ref[pl.ds(first * height, span * height), :], dense_ref[...], preferred_element_type=jnp.float32)
    for step in range(span):
        total = sums[step * height : (step + 1) * height]
        top = jnp.max(jnp.abs(total), axis=0, keepdims=True)
        unit = jnp.maximum(jnp.where(top > 0, top, 1.0) * (1.0 / CODE_TOP), SMALLEST_UNIT)
        power = jnp.floor(jnp.log2(unit))
        fraction = jnp.ceil(unit * jnp.exp2(-power) * FRACTION)
        unit = fraction * jnp.exp2(power) * (1.0 / FRACTION)
        code = jnp.clip(jnp.round(total * (1.0 / unit)), -CODE_TOP, CODE_TOP)
        code_ref[pl.ds(step * height, height), :] = code.astype(jnp.int32).astype(jnp.int16)
        scale_ref[pl.ds(2 * step, 1), :] = power
        scale_ref[pl.ds(2 * step + 1, 1), :] = fraction
    tail = scale_ref.shape[0]
    code_ref[pl.ds(code_ref.shape[0] - tail, tail), :] = scale_ref[...].astype(jnp.int32).astype(jnp.int16)


def join_kernel(first, span, height, skips, rows_ref, dense_ref, *refs):
    code_refs, (out_ref, scale_ref, done_ref, sems) = refs[: len(skips)], refs[-4:]
    tails = [code_ref.shape[0] % height for code_ref in code_refs]
    starts = [sum(tails[:number]) for number in range(len(tails))]
    first_half = lax.rem(lax.axis_index("row"), HALVES) == 0
    for code_ref, start, tail in zip(code_refs, starts, tails):
        scales = code_ref[pl.ds(code_ref.shape[0] - tail, tail), :].astype(jnp.int32).astype(jnp.float32)
        scale_ref[pl.ds(start, tail), :] = scales

    def decoded(number, step):
        block = skips[number] + step
        power = scale_ref[pl.ds(starts[number] + 2 * block, 1), :]
        fraction = scale_ref[pl.ds(starts[number] + 2 * block + 1, 1), :]
        code = code_refs[number][pl.ds(block * height, height), :]
        return code.astype(jnp.int32).astype(jnp.float32) * (fraction * jnp.exp2(power) * (1.0 / FRACTION))

    sums = jnp.dot(rows_ref[pl.ds(first * height, span * height), :], dense_ref[...], preferred_element_type=jnp.float32)
    copies = []
    for step in range(span):
        total = sums[step * height : (step + 1) * height]
        for number in range(0, len(code_refs), HALVES):
            near, far = decoded(number, step), decoded(number + 1, step)
            left = jnp.where(first_half, near, far)
            right = jnp.where(first_half, far, near)
            total = total + jnp.concatenate([left, right], axis=1)
        done_ref[step] = total.astype(done_ref.dtype)
        lines = pl.ds((first + step) * height, height)
        copies.append(pltpu.make_async_copy(done_ref.at[step], out_ref.at[lines, :], sems.at[step]))
        copies[-1].start()
    for copy in copies:
        copy.wait()


def after(value, *earlier):
    return lax.optimization_barrier((value, *earlier))[0]


def shards(amplitudes, pair_mask, integrals, tile_list, tile_count, owner):
    row_count, full_width = amplitudes.shape
    slots, tile_width = integrals.shape[2], integrals.shape[-1]
    half_width = tile_width // HALVES
    block_count = pair_mask.shape[0]
    block_rows = row_count // block_count
    row_peers, col_peers = lax.axis_size("row"), lax.axis_size("col")
    peers = row_peers // HALVES
    share = slots * tile_width // peers
    offsets = pair_offsets(col_peers)
    remote = [offset for offset in offsets if offset]
    near_chunks, far_chunks = row_chunks(block_count, NEAR_CUTS), row_chunks(block_count, FAR_CUTS)
    chunks = row_chunks(block_count, NEAR_CUTS + FAR_CUTS)

    def along(value, shift):
        pairs = []
        for r in range(row_peers):
            source = r // HALVES ^ shift if peers & (peers - 1) == 0 else (r // HALVES - shift) % peers
            pairs.append((source * HALVES + r % HALVES, r))
        return lax.ppermute(value, "row", pairs)

    def across(value, flip, down):
        pairs = []
        for r in range(row_peers):
            for c in range(col_peers):
                pairs.append((r * col_peers + c, (r ^ flip) * col_peers + (c - CORES * down) % col_peers))
        return lax.ppermute(value, ("row", "col"), pairs)

    swap = [(c, c ^ 1) for c in range(col_peers)]
    other = lax.ppermute(amplitudes, "col", swap)
    other_mask = lax.ppermute(pair_mask.T, "col", swap)
    length = max(block_count, STEPS)
    plan = jnp.concatenate(
        [jnp.pad(part, ((0, 0), (0, length - part.shape[1]))) for part in (pair_mask.T, other_mask, owner.T)]
    )
    in_hbm = partial(pltpu.with_memory_space_constraint, memory_space=pltpu.HBM)

    pieces = pl.pallas_call(
        pack_kernel,
        in_specs=[VMEM, SMEM, VMEM],
        out_specs=[VMEM] * peers,
        out_shape=[jax.ShapeDtypeStruct((share + META_ROWS, tile_width), integrals.dtype)] * peers,
        compiler_params=PARAMS,
        name="pack",
    )(in_hbm(tile_list), tile_count, in_hbm(integrals))
    pieces = [piece if shift == 0 else along(piece, shift) for shift, piece in enumerate(pieces)]

    height = CORES * share + META_ROWS
    widths = []
    for offset in offsets:
        widths += [half_width] * HALVES if offset else [tile_width]
    chosen = list(
        pl.pallas_call(
            partial(choose_kernel, col_peers, offsets, peers),
            in_specs=[SMEM] + [VMEM] * peers,
            out_specs=[VMEM] * len(widths),
            out_shape=[jax.ShapeDtypeStruct((height, width), integrals.dtype) for width in widths],
            compiler_params=PARAMS,
            name="choose",
        )(plan, *pieces)
    )

    def fill(held):
        return pl.pallas_call(
            partial(fill_kernel, slots, tile_width),
            in_specs=[VMEM] * peers,
            out_specs=VMEM,
            out_shape=jax.ShapeDtypeStruct((CORES * full_width, held[0].shape[1]), integrals.dtype),
            compiler_params=PARAMS,
            name="fill",
        )(*held)

    def screen(*earlier):
        return pl.pallas_call(
            partial(screen_kernel, tile_width, block_rows),
            in_specs=[SMEM, HBM, VMEM],
            out_specs=VMEM,
            out_shape=jax.ShapeDtypeStruct((row_count, CORES * full_width), amplitudes.dtype),
            compiler_params=PARAMS,
            cost_estimate=pl.CostEstimate(
                flops=CORES * row_count * full_width,
                bytes_accessed=4 * CORES * row_count * full_width,
                transcendentals=0,
            ),
            scratch_shapes=[pltpu.SemaphoreType.DMA((SCREEN_PARTS if block_count % SCREEN_PARTS == 0 else 1,))],
            name="screen",
        )(after(plan, *earlier), in_hbm(amplitudes), other)

    own = chosen.pop(0)
    own = own + across(own, 1, 0)
    near_weights, far_weights, screened = {}, {}, None
    for offset in remote:
        near, far = chosen.pop(0), chosen.pop(0)
        data = across(near, 0, offset) + across(far, 1, offset)
        held = [data] + [along(data, shift) for shift in range(1, peers)]
        if screened is None:
            screened = screen(held[1], own)
        near_weights[offset] = fill([after(held[0], screened)] + held[1:])
        far_weights[offset] = across(near_weights[offset], 1, 0)

    def cost(span, width):
        return pl.CostEstimate(
            flops=2 * span * block_rows * CORES * full_width * width,
            bytes_accessed=span * block_rows * (CORES * full_width + width) * 2,
            transcendentals=0,
        )

    def code_shape(span):
        return (span * block_rows + -(-2 * span // TILE_ROWS) * TILE_ROWS, half_width)

    def scratch_rows(span):
        return code_shape(span)[0] - span * block_rows

    rounds = [(half, first, span) for half, parts in enumerate((near_chunks, far_chunks)) for first, span in parts]
    arrived, sent = {}, []
    order = []
    for number, (half, first, span) in enumerate(rounds):
        ahead = 2 if number in (3, 4) else 1
        earlier = sent[-1:] + [part for key in order[:-ahead] for part in arrived[key]]
        if number == len(near_chunks) - 1:
            earlier += list(far_weights.values())
        if number == len(rounds) - 2:
            earlier.append(own_weights)
        arrived[half, first] = []
        order.append((half, first))
        for offset in remote:
            weights = (near_weights, far_weights)[half][offset]
            code = pl.pallas_call(
                partial(send_kernel, first, span, block_rows),
                in_specs=[VMEM, VMEM],
                out_specs=VMEM,
                out_shape=jax.ShapeDtypeStruct(code_shape(span), jnp.int16),
                scratch_shapes=[pltpu.VMEM((scratch_rows(span), half_width), jnp.float32)],
                compiler_params=PARAMS,
                cost_estimate=cost(span, half_width),
                name="send_part",
            )(screened, after(weights, *earlier))
            arrived[half, first].append(across(code, 0, -offset))
            sent.append(code)
        if number == 0:
            own = after(own, *arrived[half, first])
            own_weights = fill([own] + [along(own, shift) for shift in range(1, peers)])

    out = None
    for first, span in chunks:
        near_first = max(start for start, _ in near_chunks if start <= first)
        far_first = max(start for start, _ in far_chunks if start <= first)
        received = [part for pair in zip(arrived[0, near_first], arrived[1, far_first]) for part in pair]
        skips = [first - near_first, first - far_first] * len(remote)
        operands = [screened, own_weights, *received]
        specs = [VMEM] * len(operands)
        aliases = {}
        if out is not None:
            aliases = {len(operands): 0}
            operands.append(out)
            specs.append(HBM)
        out = pl.pallas_call(
            partial(join_kernel, first, span, block_rows, skips),
            in_specs=specs,
            out_specs=HBM,
            out_shape=jax.ShapeDtypeStruct((row_count, tile_width), jnp.bfloat16),
            scratch_shapes=[
                pltpu.VMEM((sum(part.shape[0] % block_rows for part in received), half_width), jnp.float32),
                pltpu.VMEM((span, block_rows, tile_width), jnp.bfloat16),
                pltpu.SemaphoreType.DMA((span,)),
            ],
            input_output_aliases=aliases,
            compiler_params=PARAMS,
            cost_estimate=cost(span, tile_width),
            name="join_part",
        )(*operands)
    return out


def solution(mesh):
    return jax.shard_map(
        shards,
        mesh=mesh,
        in_specs=(
            P("row", "col"),
            P("row", "col"),
            P("row", "col", None, None, None),
            P("row", "col", None),
            P("row", "col"),
            P(None, "col"),
        ),
        out_specs=P("row", "col"),
        check_vma=False,
    )
```

```python
from functools import partial

import jax
import jax.numpy as jnp
from jax import lax
from jax.experimental import pallas as pl
from jax.experimental.pallas import tpu as pltpu
from jax.sharding import PartitionSpec as P

STEPS = 4
CORES = 2
HALVES = 2
NEAR_CUTS = (0.0, 0.167, 0.583, 1.0)
FAR_CUTS = (0.0, 0.167, 0.583, 0.917, 1.0)
CODE_TOP = 32767.0
FRACTION = 8192.0
SMALLEST_UNIT = 2.0**-100
META_ROWS = 8
TILE_ROWS = 16
SCREEN_PARTS = 4
PARAMS = pltpu.CompilerParams(vmem_limit_bytes=16 * 1024 * 1024)
SMEM = pl.BlockSpec(memory_space=pltpu.SMEM)
VMEM = pl.BlockSpec(memory_space=pltpu.VMEM)
HBM = pl.BlockSpec(memory_space=pltpu.HBM)


def pair_offsets(col_count):
    pairs = col_count // CORES
    offsets = set()
    for core in range(CORES):
        for step in range(STEPS):
            offsets.add(-((core - step) // CORES) % pairs)
    return sorted(offsets)


def partner(place, number, peers):
    return place ^ number if peers & (peers - 1) == 0 else lax.rem(place + peers - number, peers)


def row_chunks(block_count, cuts):
    marks = sorted({round(block_count * cut) for cut in cuts})
    return [(first, last - first) for first, last in zip(marks, marks[1:])]


def pack_kernel(list_ref, count_ref, panel_ref, *piece_refs):
    peers = len(piece_refs)
    slots, tile_width = panel_ref.shape[2:4]
    share = slots * tile_width // peers
    place = lax.axis_index("row") // HALVES
    lane = lax.broadcasted_iota(jnp.int32, (META_ROWS, tile_width), 1)
    lane = lax.rem(lane, tile_width // HALVES)
    info = jnp.where(lane == slots, count_ref[0, 0], 0)
    for slot in range(slots):
        info = jnp.where(lane == slot, jnp.broadcast_to(list_ref[0, :, slot : slot + 1], lane.shape), info)
    info = info.astype(jnp.float32).astype(panel_ref.dtype)
    for shift, piece_ref in enumerate(piece_refs):
        first = partner(place, shift if peers & (peers - 1) == 0 else peers - shift, peers) * share
        start = pl.multiple_of(lax.rem(first, tile_width), TILE_ROWS)
        piece_ref[pl.ds(0, share), :] = panel_ref[0, 0, first // tile_width, pl.ds(start, share), :]
        piece_ref[pl.ds(share, META_ROWS), :] = info


def choose_kernel(col_peers, offsets, peers, plan_ref, *refs):
    piece_refs, out_refs = refs[:peers], list(refs[peers:])
    share, tile_width = piece_refs[0].shape[0] - META_ROWS, piece_refs[0].shape[1]
    half_width = tile_width // HALVES
    row = lax.axis_index("row")
    half = lax.rem(row, HALVES)
    core = lax.rem(lax.axis_index("col"), CORES)
    sign = 1 - 2 * core
    for offset in offsets:
        if offset:
            spots = [pl.multiple_of(part * half_width, half_width) for part in (half, 1 - half)]
            targets = [(out_refs.pop(0), pl.ds(spot, half_width)) for spot in spots]
        else:
            targets = [(out_refs.pop(0), pl.ds(0, tile_width))]
        for out_ref, _ in targets:
            out_ref[...] = jnp.zeros_like(out_ref)
        for group, shift in enumerate((0, sign)):
            step = lax.rem(CORES * offset - shift + col_peers, col_peers)
            holder = plan_ref[plan_ref.shape[0] - 1, jnp.minimum(step, STEPS - 1)]
            here = (step < STEPS) & (lax.rem(holder, HALVES) == half)
            for number, piece_ref in enumerate(piece_refs):

                @pl.when(here & (partner(row // HALVES, number, peers) == holder // HALVES))
                def _():
                    for out_ref, columns in targets:
                        line = lax.broadcasted_iota(jnp.int32, (META_ROWS, out_ref.shape[1]), 0)
                        out_ref[pl.ds(group * share, share), :] = piece_ref[pl.ds(0, share), columns]
                        rows = pl.ds(CORES * share, META_ROWS)
                        info = piece_ref[pl.ds(share, META_ROWS), columns]
                        out_ref[rows, :] = jnp.where(line == group, info, out_ref[rows, :])


def fill_kernel(slots, tile_width, *refs):
    piece_refs, dense_ref = refs[:-1], refs[-1]
    peers = len(piece_refs)
    share = (piece_refs[0].shape[0] - META_ROWS) // CORES
    width = dense_ref.shape[0] // CORES
    place = lax.axis_index("row") // HALVES
    table = piece_refs[0][pl.ds(CORES * share, META_ROWS), :].astype(jnp.float32)
    line = lax.broadcasted_iota(jnp.int32, table.shape, 0)
    lane = lax.broadcasted_iota(jnp.int32, table.shape, 1)

    def entry(group, spot):
        return jnp.max(jnp.where((line == group) & (lane == spot), table, 0.0)).astype(jnp.int32)

    dense_ref[...] = jnp.zeros_like(dense_ref)
    for group in range(CORES):
        count = entry(group, slots)
        starts = [group * width + entry(group, slot) * tile_width for slot in range(slots)]
        for shift, piece_ref in enumerate(piece_refs):
            first = partner(place, shift, peers) * share
            slot = first // tile_width
            start = starts[0]
            for other in range(1, slots):
                start = jnp.where(slot == other, starts[other], start)

            @pl.when(slot < count)
            def _():
                spot = pl.multiple_of(start + lax.rem(first, tile_width), TILE_ROWS)
                dense_ref[pl.ds(spot, share), :] = piece_ref[pl.ds(group * share, share), :]


def screen_kernel(tile_width, block_rows, mask_ref, own_ref, other_ref, out_ref, sems):
    full_width = own_ref.shape[1]
    tiles = full_width // tile_width
    parts = sems.shape[0]
    blocks = own_ref.shape[0] // block_rows // parts
    copies = []
    for part in range(parts):
        lines = pl.ds(part * blocks * block_rows, blocks * block_rows)
        copies.append(
            pltpu.make_async_copy(own_ref.at[lines, :], out_ref.at[lines, pl.ds(0, full_width)], sems.at[part])
        )
        copies[-1].start()

    def screen(source_ref, group, block):
        lines = pl.ds(pl.multiple_of(block * block_rows, block_rows), block_rows)
        for tile in range(tiles):
            live = mask_ref[group * tiles + tile, block].astype(jnp.float32).astype(out_ref.dtype)
            part = source_ref[lines, pl.ds(tile * tile_width, tile_width)]
            out_ref[lines, pl.ds((group * tiles + tile) * tile_width, tile_width)] = part * live

    @pl.loop(0, parts * blocks)
    def _(block):
        screen(other_ref, 1, block)

    for part in range(parts):
        copies[part].wait()

        @pl.loop(part * blocks, (part + 1) * blocks)
        def _(block):
            screen(out_ref, 0, block)


def send_kernel(first, span, height, rows_ref, dense_ref, code_ref, scale_ref):
    scale_ref[...] = jnp.zeros_like(scale_ref)
    sums = jnp.dot(rows_ref[pl.ds(first * height, span * height), :], dense_ref[...], preferred_element_type=jnp.float32)
    for step in range(span):
        total = sums[step * height : (step + 1) * height]
        top = jnp.max(jnp.abs(total), axis=0, keepdims=True)
        unit = jnp.maximum(jnp.where(top > 0, top, 1.0) * (1.0 / CODE_TOP), SMALLEST_UNIT)
        power = jnp.floor(jnp.log2(unit))
        fraction = jnp.ceil(unit * jnp.exp2(-power) * FRACTION)
        unit = fraction * jnp.exp2(power) * (1.0 / FRACTION)
        code = jnp.clip(jnp.round(total * (1.0 / unit)), -CODE_TOP, CODE_TOP)
        code_ref[pl.ds(step * height, height), :] = code.astype(jnp.int32).astype(jnp.int16)
        scale_ref[pl.ds(2 * step, 1), :] = power
        scale_ref[pl.ds(2 * step + 1, 1), :] = fraction
    tail = scale_ref.shape[0]
    code_ref[pl.ds(code_ref.shape[0] - tail, tail), :] = scale_ref[...].astype(jnp.int32).astype(jnp.int16)


def join_kernel(first, span, height, skips, rows_ref, dense_ref, *refs):
    code_refs, (out_ref, scale_ref, done_ref, sems) = refs[: len(skips)], refs[-4:]
    tails = [code_ref.shape[0] % height for code_ref in code_refs]
    starts = [sum(tails[:number]) for number in range(len(tails))]
    first_half = lax.rem(lax.axis_index("row"), HALVES) == 0
    for code_ref, start, tail in zip(code_refs, starts, tails):
        scales = code_ref[pl.ds(code_ref.shape[0] - tail, tail), :].astype(jnp.int32).astype(jnp.float32)
        scale_ref[pl.ds(start, tail), :] = scales

    def decoded(number, step):
        block = skips[number] + step
        power = scale_ref[pl.ds(starts[number] + 2 * block, 1), :]
        fraction = scale_ref[pl.ds(starts[number] + 2 * block + 1, 1), :]
        code = code_refs[number][pl.ds(block * height, height), :]
        return code.astype(jnp.int32).astype(jnp.float32) * (fraction * jnp.exp2(power) * (1.0 / FRACTION))

    sums = jnp.dot(rows_ref[pl.ds(first * height, span * height), :], dense_ref[...], preferred_element_type=jnp.float32)
    copies = []
    for step in range(span):
        total = sums[step * height : (step + 1) * height]
        for number in range(0, len(code_refs), HALVES):
            near, far = decoded(number, step), decoded(number + 1, step)
            left = jnp.where(first_half, near, far)
            right = jnp.where(first_half, far, near)
            total = total + jnp.concatenate([left, right], axis=1)
        done_ref[step] = total.astype(done_ref.dtype)
        lines = pl.ds((first + step) * height, height)
        copies.append(pltpu.make_async_copy(done_ref.at[step], out_ref.at[lines, :], sems.at[step]))
        copies[-1].start()
    for copy in copies:
        copy.wait()


def after(value, *earlier):
    return lax.optimization_barrier((value, *earlier))[0]


def shards(amplitudes, pair_mask, integrals, tile_list, tile_count, owner):
    row_count, full_width = amplitudes.shape
    slots, tile_width = integrals.shape[2], integrals.shape[-1]
    half_width = tile_width // HALVES
    block_count = pair_mask.shape[0]
    block_rows = row_count // block_count
    row_peers, col_peers = lax.axis_size("row"), lax.axis_size("col")
    peers = row_peers // HALVES
    share = slots * tile_width // peers
    offsets = pair_offsets(col_peers)
    remote = [offset for offset in offsets if offset]
    near_chunks, far_chunks = row_chunks(block_count, NEAR_CUTS), row_chunks(block_count, FAR_CUTS)
    chunks = row_chunks(block_count, NEAR_CUTS + FAR_CUTS)

    def along(value, shift):
        pairs = []
        for r in range(row_peers):
            source = r // HALVES ^ shift if peers & (peers - 1) == 0 else (r // HALVES - shift) % peers
            pairs.append((source * HALVES + r % HALVES, r))
        return lax.ppermute(value, "row", pairs)

    def across(value, flip, down):
        pairs = []
        for r in range(row_peers):
            for c in range(col_peers):
                pairs.append((r * col_peers + c, (r ^ flip) * col_peers + (c - CORES * down) % col_peers))
        return lax.ppermute(value, ("row", "col"), pairs)

    swap = [(c, c ^ 1) for c in range(col_peers)]
    other = lax.ppermute(amplitudes, "col", swap)
    other_mask = lax.ppermute(pair_mask.T, "col", swap)
    length = max(block_count, STEPS)
    plan = jnp.concatenate(
        [jnp.pad(part, ((0, 0), (0, length - part.shape[1]))) for part in (pair_mask.T, other_mask, owner.T)]
    )
    in_hbm = partial(pltpu.with_memory_space_constraint, memory_space=pltpu.HBM)

    pieces = pl.pallas_call(
        pack_kernel,
        in_specs=[VMEM, SMEM, VMEM],
        out_specs=[VMEM] * peers,
        out_shape=[jax.ShapeDtypeStruct((share + META_ROWS, tile_width), integrals.dtype)] * peers,
        compiler_params=PARAMS,
        name="pack",
    )(in_hbm(tile_list), tile_count, in_hbm(integrals))
    pieces = [piece if shift == 0 else along(piece, shift) for shift, piece in enumerate(pieces)]

    height = CORES * share + META_ROWS
    widths = []
    for offset in offsets:
        widths += [half_width] * HALVES if offset else [tile_width]
    chosen = list(
        pl.pallas_call(
            partial(choose_kernel, col_peers, offsets, peers),
            in_specs=[SMEM] + [VMEM] * peers,
            out_specs=[VMEM] * len(widths),
            out_shape=[jax.ShapeDtypeStruct((height, width), integrals.dtype) for width in widths],
            compiler_params=PARAMS,
            name="choose",
        )(plan, *pieces)
    )

    def fill(held):
        return pl.pallas_call(
            partial(fill_kernel, slots, tile_width),
            in_specs=[VMEM] * peers,
            out_specs=VMEM,
            out_shape=jax.ShapeDtypeStruct((CORES * full_width, held[0].shape[1]), integrals.dtype),
            compiler_params=PARAMS,
            name="fill",
        )(*held)

    def screen(*earlier):
        return pl.pallas_call(
            partial(screen_kernel, tile_width, block_rows),
            in_specs=[SMEM, HBM, VMEM],
            out_specs=VMEM,
            out_shape=jax.ShapeDtypeStruct((row_count, CORES * full_width), amplitudes.dtype),
            compiler_params=PARAMS,
            cost_estimate=pl.CostEstimate(
                flops=CORES * row_count * full_width,
                bytes_accessed=4 * CORES * row_count * full_width,
                transcendentals=0,
            ),
            scratch_shapes=[pltpu.SemaphoreType.DMA((SCREEN_PARTS if block_count % SCREEN_PARTS == 0 else 1,))],
            name="screen",
        )(after(plan, *earlier), in_hbm(amplitudes), other)

    own = chosen.pop(0)
    own = own + across(own, 1, 0)
    near_weights, far_weights, screened = {}, {}, None
    for offset in remote:
        near, far = chosen.pop(0), chosen.pop(0)
        data = across(near, 0, offset) + across(far, 1, offset)
        held = [data] + [along(data, shift) for shift in range(1, peers)]
        if screened is None:
            screened = screen(held[1], own)
        near_weights[offset] = fill([after(held[0], screened)] + held[1:])
        far_weights[offset] = across(near_weights[offset], 1, 0)

    def cost(span, width):
        return pl.CostEstimate(
            flops=2 * span * block_rows * CORES * full_width * width,
            bytes_accessed=span * block_rows * (CORES * full_width + width) * 2,
            transcendentals=0,
        )

    def code_shape(span):
        return (span * block_rows + -(-2 * span // TILE_ROWS) * TILE_ROWS, half_width)

    def scratch_rows(span):
        return code_shape(span)[0] - span * block_rows

    rounds = [(half, first, span) for half, parts in enumerate((near_chunks, far_chunks)) for first, span in parts]
    arrived, sent = {}, []
    order = []
    for number, (half, first, span) in enumerate(rounds):
        ahead = 2 if number in (3, 4, 6) else 1
        earlier = sent[-1:] + [part for key in order[:-ahead] for part in arrived[key]]
        if number == len(near_chunks) - 1:
            earlier += list(far_weights.values())
        if number == len(rounds) - 2:
            earlier.append(own_weights)
        arrived[half, first] = []
        order.append((half, first))
        for offset in remote:
            weights = (near_weights, far_weights)[half][offset]
            code = pl.pallas_call(
                partial(send_kernel, first, span, block_rows),
                in_specs=[VMEM, VMEM],
                out_specs=VMEM,
                out_shape=jax.ShapeDtypeStruct(code_shape(span), jnp.int16),
                scratch_shapes=[pltpu.VMEM((scratch_rows(span), half_width), jnp.float32)],
                compiler_params=PARAMS,
                cost_estimate=cost(span, half_width),
                name="send_part",
            )(screened, after(weights, *earlier))
            arrived[half, first].append(across(code, 0, -offset))
            sent.append(code)
        if number == 0:
            own = after(own, *arrived[half, first])
            own_weights = fill([own] + [along(own, shift) for shift in range(1, peers)])

    out = None
    for first, span in chunks:
        near_first = max(start for start, _ in near_chunks if start <= first)
        far_first = max(start for start, _ in far_chunks if start <= first)
        received = [part for pair in zip(arrived[0, near_first], arrived[1, far_first]) for part in pair]
        skips = [first - near_first, first - far_first] * len(remote)
        operands = [screened, own_weights, *received]
        specs = [VMEM] * len(operands)
        aliases = {}
        if out is not None:
            aliases = {len(operands): 0}
            operands.append(out)
            specs.append(HBM)
        out = pl.pallas_call(
            partial(join_kernel, first, span, block_rows, skips),
            in_specs=specs,
            out_specs=HBM,
            out_shape=jax.ShapeDtypeStruct((row_count, tile_width), jnp.bfloat16),
            scratch_shapes=[
                pltpu.VMEM((sum(part.shape[0] % block_rows for part in received), half_width), jnp.float32),
                pltpu.VMEM((span, block_rows, tile_width), jnp.bfloat16),
                pltpu.SemaphoreType.DMA((span,)),
            ],
            input_output_aliases=aliases,
            compiler_params=PARAMS,
            cost_estimate=cost(span, tile_width),
            name="join_part",
        )(*operands)
    return out


def solution(mesh):
    return jax.shard_map(
        shards,
        mesh=mesh,
        in_specs=(
            P("row", "col"),
            P("row", "col"),
            P("row", "col", None, None, None),
            P("row", "col", None),
            P("row", "col"),
            P(None, "col"),
        ),
        out_specs=P("row", "col"),
        check_vma=False,
    )
```
